256 devices in a mesh: samp: 4 (over y), blk: 64 (over z, x, core).
Axes of the slice: x: 4, y: 4, z: 8, core: 2. Of those that a mesh axis runs over, the one named last changes fastest.
Arguments:
- perturb: bfloat16 [8192, 65536], P('samp', 'blk'), may hold values from -400 to 400
- partner: int32 [256, 8], P('blk'), may hold values from 0 to 255, as said below
- bins: int32 [256, 8], P('blk'), may hold values from 0 to 31
Outputs:
- localized_corr: float32 [256, 2048, 256], P('samp', 'blk')
The draws below stay inside these ranges and needn't reach their ends.
Inputs may be any that keep to these rules, and one draw needn't show every extreme that they name: The partners of one row block are distinct; they include every block of the row block's own device (itself too); every partner lies on a device at most 2 indices away along the cyclic order of blk; the partners of all row blocks of one device take exactly 2 distinct blocks from each of the 4 devices nearest to it.
All inputs are finite; a program needn't handle non-finite values.
Results may differ from the reference program's by a relative error of at most 0.0003.
Values may be sent and summed in bfloat16 or wider, within the bound.
No kernel may reach another device: no remote copies, remote signals or barrier semaphores. Data moves between devices by JAX's collectives and lax.ppermute only.
A program may use at most 192 MiB of HBM per device.

```python
import math
import jax
import jax.numpy as jnp
from jax import lax

BS = 256
B_DEV = 4
K_PART = 8
REACH = 2
CAP = 2
NBIN = 32
S = 8192
NB = 256
NCELL = 65536


def draw_perturb(key, part):
    key = jax.random.fold_in(key, 11)
    noise_key, scale_key, weight_key, common_key = jax.random.split(key, 4)
    group_width = 2 * B_DEV * BS
    noise = jnp.clip(jax.random.normal(noise_key, (S, NCELL), jnp.float32), -4.0, 4.0)
    scales = jnp.exp(jax.random.uniform(scale_key, (NCELL,), jnp.float32, 0.0, math.log(10.0)))
    weights = jax.random.uniform(weight_key, (NCELL,), jnp.float32, 0.3, 1.5)
    common = jnp.clip(jax.random.normal(common_key, (S, NCELL // group_width), jnp.float32), -4.0, 4.0)
    shared = jnp.repeat(common, group_width, axis=1)
    return (scales * (noise + weights * shared)).astype(jnp.bfloat16)


def draw_partner(key, part):
    key = jax.random.fold_in(key, 23)
    devices = NB // B_DEV
    neighbours = [shift_by for shift_by in range(-REACH, REACH + 1) if shift_by != 0]
    slot_count = 2 * REACH * CAP
    extra = K_PART - B_DEV
    stride = slot_count // B_DEV

    def one_device(dev_key, device):
        keys = jax.random.split(dev_key, len(neighbours) + 1 + B_DEV)
        remote = []
        for index, shift_by in enumerate(neighbours):
            chosen = jax.random.permutation(keys[index], B_DEV)[:CAP].astype(jnp.int32)
            remote.append((device + shift_by + devices) % devices * B_DEV + chosen)
        remote = jax.random.permutation(keys[len(neighbours)], jnp.concatenate(remote)).astype(jnp.int32)
        lists = []
        for row_index in range(B_DEV):
            positions = (row_index * stride + jnp.arange(extra, dtype=jnp.int32)) % slot_count
            picked = jnp.take(remote, positions)
            full_list = jnp.concatenate([device * B_DEV + jnp.arange(B_DEV, dtype=jnp.int32), picked])
            lists.append(jax.random.permutation(keys[len(neighbours) + 1 + row_index], full_list).astype(jnp.int32))
        return jnp.stack(lists)
    table = jax.vmap(one_device)(jax.random.split(key, devices), jnp.arange(devices, dtype=jnp.int32))
    return table.reshape(NB, K_PART).astype(jnp.int32)


def plant(values, stream_key, low, largest):
    longest = values.shape.index(max(values.shape))
    spots = []
    for shift in (0, 1):
        where = [jax.random.randint(jax.random.fold_in(stream_key, axis), (), 0, length) for axis, length in enumerate(values.shape)]
        where[longest] = (where[longest] + shift) % values.shape[longest]
        spots.append(tuple(where))
    return values.at[spots[0]].set(low).at[spots[1]].set(largest)


def setup_inputs(seed: int = 0) -> dict:
    key_list = jax.random.split(jax.random.key(seed), 4)
    perturb = draw_perturb(jax.random.fold_in(key_list[3], 71), 0)
    partner = draw_partner(jax.random.fold_in(key_list[3], 71), 0)
    bins = plant(jax.random.randint(key_list[2], (NB, K_PART), 0, NBIN), jax.random.fold_in(key_list[2], 1), 0, NBIN - 1).astype(jnp.int32)
    return dict(perturb=perturb, partner=partner, bins=bins)


EPSILON = 1e-06

def taper_table():
    scaled = 2.0 * (jnp.arange(NBIN, dtype=jnp.float32) + 0.5) / NBIN
    inner = (((-0.25 * scaled + 0.5) * scaled + 0.625) * scaled - 5.0 / 3.0) * scaled * scaled + 1.0
    outer = ((((scaled / 12.0 - 0.5) * scaled + 0.625) * scaled + 5.0 / 3.0) * scaled - 5.0) * scaled + 4.0 - 2.0 / (3.0 * scaled)
    return jnp.where(scaled <= 1.0, inner, outer)

def reference(perturb, partner, bins):
    block_ids = jnp.arange(NB, dtype=jnp.int32)

    def block_norm(block):
        slab = lax.dynamic_slice_in_dim(perturb, block * BS, BS, 1).astype(jnp.float32)
        return lax.optimization_barrier(jnp.sum(slab * slab, axis=0))
    sq_norms = lax.map(block_norm, block_ids)
    tapers = taper_table()[bins]
    col_scale = tapers[:, :, None] * lax.rsqrt(sq_norms[partner] + EPSILON)
    blocks = perturb.reshape(S, NB, BS)

    def one_row(block):
        row_slab = lax.dynamic_slice_in_dim(perturb, block * BS, BS, 1).astype(jnp.float32)
        col_slabs = blocks[:, partner[block], :].astype(jnp.float32)
        gram_tile = jnp.einsum('sa,skc->akc', row_slab, col_slabs, precision=lax.Precision.HIGHEST)
        row_scale = lax.rsqrt(sq_norms[block] + EPSILON)
        return gram_tile * row_scale[:, None, None] * col_scale[block][None]
    result = lax.map(one_row, block_ids)
    return jnp.transpose(result, (1, 0, 2, 3)).reshape(BS, NB * K_PART, BS)
```

```python
import functools

import jax
import jax.numpy as jnp
from jax import lax
from jax.experimental import pallas as pl
from jax.experimental.pallas import tpu as pltpu
from jax.sharding import PartitionSpec as P

BS = 256
B_DEV = 4
K_PART = 8
REACH = 2
NBIN = 32
PAIR_DEV = 32
SHIFTS = (-2, -1, 1, 2)
HALF = 128
STAGES = 2

EPSILON = 1e-06
MIB = 1 << 20


def passed_along(value, axis, steps):
    count = lax.axis_size(axis)
    pairs = [(source, (source + steps) % count) for source in range(count)]
    return lax.ppermute(value, axis, pairs)


def taper_table():
    scaled = 2.0 * (jnp.arange(NBIN, dtype=jnp.float32) + 0.5) / NBIN
    inner = (((-0.25 * scaled + 0.5) * scaled + 0.625) * scaled - 5.0 / 3.0) * scaled * scaled + 1.0
    outer = (
        ((((scaled / 12.0 - 0.5) * scaled + 0.625) * scaled + 5.0 / 3.0) * scaled - 5.0) * scaled
        + 4.0
        - 2.0 / (3.0 * scaled)
    )
    return jnp.where(scaled <= 1.0, inner, outer)


def select_kernel(want_ref, source_ref, *refs):
    outs, sems = refs[:-1], refs[-1]
    copies = []
    for stage in range(STAGES):
        for q in range(4):
            for side in range(2):
                start = pl.multiple_of(want_ref[q * 2 + side] * BS + stage * HALF, HALF)
                copies.append(
                    pltpu.make_async_copy(
                        source_ref.at[:, pl.ds(start, HALF)],
                        outs[stage * 4 + q].at[:, pl.ds(side * HALF, HALF)],
                        sems.at[len(copies)],
                    )
                )
    for copy in copies:
        copy.start()
    for copy in copies:
        copy.wait()


def select(want, perturb):
    samples = perturb.shape[0]
    count = STAGES * 4
    return pl.pallas_call(
        select_kernel,
        grid_spec=pltpu.PrefetchScalarGridSpec(
            num_scalar_prefetch=1,
            grid=(),
            in_specs=[pl.BlockSpec(memory_space=pl.ANY)],
            out_specs=[pl.BlockSpec(memory_space=pl.ANY)] * count,
            scratch_shapes=[pltpu.SemaphoreType.DMA((count * 2,))],
        ),
        out_shape=[jax.ShapeDtypeStruct((samples, 2 * HALF), perturb.dtype)] * count,
        cost_estimate=pl.CostEstimate(flops=0, bytes_accessed=16 * MIB, transcendentals=0),
    )(want, perturb)


def own_kernel(x_ref, at_ref, part_ref, norm_ref):
    samp = part_ref.shape[0]
    rows = BS // samp
    for r in range(B_DEV):
        at = jnp.transpose(x_ref[:, r * BS : (r + 1) * BS])
        at_ref[r * BS : (r + 1) * BS, :] = at

    @pl.loop(0, B_DEV)
    def _(r):
        at = at_ref[pl.ds(pl.multiple_of(r * BS, BS), BS), :]
        for c in range(B_DEV):
            tile = jnp.dot(at, x_ref[:, c * BS : (c + 1) * BS], preferred_element_type=jnp.float32)
            for y in range(samp):
                part_ref[y, r * B_DEV + c] = tile[y * rows : (y + 1) * rows]

            @pl.when(r == c)
            def _():
                here = lax.broadcasted_iota(jnp.int32, (BS, BS), 0) == lax.broadcasted_iota(jnp.int32, (BS, BS), 1)
                norm_ref[c : c + 1, :] = jnp.sum(jnp.where(here, tile, 0.0), axis=0, keepdims=True)


def own_tiles(perturb, samp):
    samples, cells = perturb.shape
    return pl.pallas_call(
        own_kernel,
        out_shape=[
            jax.ShapeDtypeStruct((cells, samples), perturb.dtype),
            jax.ShapeDtypeStruct((samp, 16, BS // samp, BS), jnp.float32),
            jax.ShapeDtypeStruct((B_DEV, BS), jnp.float32),
        ],
        compiler_params=pltpu.CompilerParams(vmem_limit_bytes=40 * MIB),
        cost_estimate=pl.CostEstimate(flops=2 * cells * cells * samples, bytes_accessed=12 * MIB, transcendentals=0),
    )(perturb)


def remote_kernel(slot_ref, at_ref, *refs):
    blocks, part_ref, all_ref = refs[:4], refs[4], refs[5]
    samp = part_ref.shape[0]
    rows = BS // samp
    for r in range(B_DEV):
        at = at_ref[r * BS : (r + 1) * BS, :]
        for q in range(4):
            tile = jnp.dot(at, blocks[q][...], preferred_element_type=jnp.float32)
            all_ref[2 * q] = tile[:, :HALF]
            all_ref[2 * q + 1] = tile[:, HALF:]
        for j in range(4):
            chosen = all_ref[slot_ref[r * 4 + j]]
            for y in range(samp):
                part_ref[y, r * 4 + j] = chosen[y * rows : (y + 1) * rows]


def remote_tiles(slots, at, blocks, samp):
    cells, samples = at.shape
    full = lambda shape: pl.BlockSpec(shape, lambda i, s: (0,) * len(shape))
    shape = (samp, 16, BS // samp, HALF)
    return pl.pallas_call(
        remote_kernel,
        grid_spec=pltpu.PrefetchScalarGridSpec(
            num_scalar_prefetch=1,
            grid=(1,),
            in_specs=[full(at.shape)] + [full(blocks[0].shape)] * 4,
            out_specs=full(shape),
            scratch_shapes=[pltpu.VMEM((8, BS, HALF), jnp.float32)],
        ),
        out_shape=jax.ShapeDtypeStruct(shape, jnp.float32),
        compiler_params=pltpu.CompilerParams(vmem_limit_bytes=40 * MIB),
        cost_estimate=pl.CostEstimate(flops=2 * cells * cells * samples, bytes_accessed=10 * MIB, transcendentals=0),
    )(slots, at, *blocks)


def final_kernel(source_ref, column_ref, taper_ref, own_ref, rem0_ref, rem1_ref, row_ref, norm_ref, out_ref):
    for r in range(B_DEV):
        row_scale = row_ref[:, r : r + 1]
        for k in range(K_PART):
            p = r * K_PART + k
            source = source_ref[p]
            col_scale = taper_ref[p] * lax.rsqrt(norm_ref[pl.ds(column_ref[p], 1), :] + EPSILON)
            for h, rem_ref in enumerate((rem0_ref, rem1_ref)):
                cols = slice(h * HALF, (h + 1) * HALF)

                @pl.when(source < 16)
                def _():
                    out_ref[:, p, cols] = own_ref[source, :, cols] * row_scale * col_scale[:, cols]

                @pl.when(source >= 16)
                def _():
                    out_ref[:, p, cols] = rem_ref[source - 16] * row_scale * col_scale[:, cols]


def final(source, column, tapers, own, rems, row_scale, norms):
    rows = own.shape[1]
    full = lambda shape: pl.BlockSpec(shape, lambda i, *s: (0,) * len(shape))
    return pl.pallas_call(
        final_kernel,
        grid_spec=pltpu.PrefetchScalarGridSpec(
            num_scalar_prefetch=3,
            grid=(1,),
            in_specs=[full(own.shape), full(rems[0].shape), full(rems[1].shape), full(row_scale.shape), full(norms.shape)],
            out_specs=full((rows, PAIR_DEV, BS)),
        ),
        out_shape=jax.ShapeDtypeStruct((rows, PAIR_DEV, BS), jnp.float32),
        cost_estimate=pl.CostEstimate(flops=MIB, bytes_accessed=4 * MIB, transcendentals=0),
    )(source, column, tapers, own, *rems, row_scale, norms)


def body(perturb, partner, bins):
    blk_count = lax.axis_size("blk")
    samp = lax.axis_size("samp")
    here = lax.axis_index("blk")
    owner = partner // B_DEV
    inside = partner % B_DEV
    offset = (owner - here + blk_count + REACH) % blk_count - REACH
    shifts = jnp.array(SHIFTS, jnp.int32)
    block_ids = jnp.arange(B_DEV, dtype=jnp.int32)
    hit = (offset.reshape(1, 1, -1) == shifts[:, None, None]) & (inside.reshape(1, 1, -1) == block_ids[None, :, None])
    need = jnp.any(hit, axis=2)
    low = jnp.min(jnp.where(need, block_ids[None], B_DEV - 1), axis=1)
    high = jnp.max(jnp.where(need, block_ids[None], 0), axis=1)
    want = jnp.stack([low, high], axis=1)
    asked = [passed_along(want[q], "blk", shift) for q, shift in enumerate(SHIFTS)]
    asked = jnp.concatenate(asked)
    chosen = select(asked, perturb)
    got = [
        [passed_along(chosen[stage * 4 + q], "blk", -shift) for q, shift in enumerate(SHIFTS)]
        for stage in range(STAGES)
    ]

    own = offset == 0
    q_of = jnp.where(offset < 0, offset + 2, offset + 1)
    is_high = jnp.sum(jnp.where(q_of[:, :, None] == jnp.arange(4), high[None, None], 0), axis=2) == inside
    slot = 2 * q_of + is_high.astype(jnp.int32)
    rank = jnp.cumsum(jnp.where(own, 0, 1), axis=1) - 1
    rows4 = jnp.arange(B_DEV, dtype=jnp.int32)[:, None] * 4
    source = jnp.where(own, rows4 + inside, 16 + rows4 + rank)
    column = jnp.where(own, inside, 4 + slot)
    slots = jnp.sum(
        jnp.where((~own)[:, :, None] & (rank[:, :, None] == jnp.arange(4)), slot[:, :, None], 0), axis=1
    )
    bin_match = bins[:, :, None] == jnp.arange(NBIN, dtype=jnp.int32)[None, None, :]
    tapers = jnp.sum(jnp.where(bin_match, taper_table()[None, None, :], 0.0), axis=2)

    rows = BS // samp
    at, own_part, norm_part = own_tiles(perturb, samp)
    own_sum = lax.psum_scatter(
        own_part.reshape(samp * 16 * rows, BS), "samp", scatter_dimension=0, tiled=True
    ).reshape(16, rows, BS)
    norms = norm_part + passed_along(norm_part, "samp", 2)
    norms = norms + passed_along(norms, "samp", 1)
    far = []
    for q, shift in enumerate(SHIFTS):
        theirs = passed_along(norms, "blk", -shift)
        for pick in (low[q], high[q]):
            far.append(lax.dynamic_slice_in_dim(theirs, pick, 1, 0))
    norm_table = jnp.concatenate([norms] + far, axis=0)
    row_part = lax.dynamic_slice_in_dim(norms, lax.axis_index("samp") * rows, rows, 1)
    row_scale = jnp.transpose(lax.rsqrt(row_part + EPSILON))

    rems = []
    for stage in range(STAGES):
        part = remote_tiles(slots.reshape(-1), at, got[stage], samp)
        rems.append(
            lax.psum_scatter(
                part.reshape(samp * 16 * rows, HALF), "samp", scatter_dimension=0, tiled=True
            ).reshape(16, rows, HALF)
        )
    return final(
        source.reshape(-1), column.reshape(-1), tapers.reshape(-1), own_sum, rems, row_scale, norm_table
    )


def solution(mesh):
    return jax.shard_map(
        body,
        mesh=mesh,
        in_specs=(P("samp", "blk"), P("blk", None), P("blk", None)),
        out_specs=P("samp", "blk", None),
        check_vma=False,
    )
```

```python
import functools

import jax
import jax.numpy as jnp
from jax import lax
from jax.experimental import pallas as pl
from jax.experimental.pallas import tpu as pltpu
from jax.sharding import PartitionSpec as P

BS = 256
B_DEV = 4
K_PART = 8
REACH = 2
NBIN = 32
PAIR_DEV = 32
HALF = 128
STAGES = 2
EXTRA = 8

EPSILON = 1e-06
MIB = 1 << 20


def passed_along(value, axis, steps):
    count = lax.axis_size(axis)
    pairs = [(source, (source + steps) % count) for source in range(count)]
    return lax.ppermute(value, axis, pairs)


def exchanged(value, kind, back=False):
    count = lax.axis_size("blk")
    source_of = (
        lambda i: i - 2,
        lambda i: i ^ 1,
        lambda i: i - 1 if i % 2 == 0 else i + 1,
        lambda i: i + 2,
    )[kind]
    pairs = [(source_of(i) % count, i) for i in range(count)]
    if back:
        pairs = [(b, a) for a, b in pairs]
    return lax.ppermute(value, "blk", sorted(pairs))


def ringed(value):
    samp, count = lax.axis_size("samp"), lax.axis_size("blk")
    pairs = [
        (y * count + i, (y + 1 - 2 * (i % 2)) % samp * count + i) for y in range(samp) for i in range(count)
    ]
    return lax.ppermute(value, ("samp", "blk"), pairs)


def taper_table():
    scaled = 2.0 * (jnp.arange(NBIN, dtype=jnp.float32) + 0.5) / NBIN
    inner = (((-0.25 * scaled + 0.5) * scaled + 0.625) * scaled - 5.0 / 3.0) * scaled * scaled + 1.0
    outer = (
        ((((scaled / 12.0 - 0.5) * scaled + 0.625) * scaled + 5.0 / 3.0) * scaled - 5.0) * scaled
        + 4.0
        - 2.0 / (3.0 * scaled)
    )
    return jnp.where(scaled <= 1.0, inner, outer)


def select_kernel(plan, want_ref, source_ref, *refs):
    outs, held_ref, in_sems, out_sems = refs[:-3], refs[-3], refs[-2], refs[-1]
    reads, writes = [], []
    for i, (q, side, half, out, column) in enumerate(plan):
        start = pl.multiple_of(want_ref[q * 2 + side] * BS + half * HALF, HALF)
        reads.append(pltpu.make_async_copy(source_ref.at[:, pl.ds(start, HALF)], held_ref.at[i], in_sems.at[i]))
        writes.append(
            pltpu.make_async_copy(held_ref.at[i], outs[out].at[:, pl.ds(column * HALF, HALF)], out_sems.at[i])
        )
    for read in reads:
        read.start()
    for read, write in zip(reads, writes):
        read.wait()
        write.start()
    for write in writes:
        write.wait()


def select(want, perturb):
    samples = perturb.shape[0]
    widths = [2 * HALF] * 6 + [4 * HALF]
    plan = [(q, side, 0, out, side) for out, q in enumerate((0, 2, 3)) for side in range(2)]
    plan += [(1, side, half, 6, 2 * half + side) for half in range(2) for side in range(2)]
    plan += [(q, side, 1, 3 + out, side) for out, q in enumerate((0, 2, 3)) for side in range(2)]
    return pl.pallas_call(
        functools.partial(select_kernel, plan),
        grid_spec=pltpu.PrefetchScalarGridSpec(
            num_scalar_prefetch=1,
            grid=(),
            in_specs=[pl.BlockSpec(memory_space=pl.ANY)],
            out_specs=[pl.BlockSpec(memory_space=pltpu.HBM)] * len(widths),
            scratch_shapes=[
                pltpu.VMEM((len(plan), samples, HALF), perturb.dtype),
                pltpu.SemaphoreType.DMA((len(plan),)),
                pltpu.SemaphoreType.DMA((len(plan),)),
            ],
        ),
        out_shape=[jax.ShapeDtypeStruct((samples, width), perturb.dtype) for width in widths],
        compiler_params=pltpu.CompilerParams(vmem_limit_bytes=16 * MIB),
        cost_estimate=pl.CostEstimate(flops=0, bytes_accessed=MIB * len(plan), transcendentals=0),
    )(want, perturb)


def own_kernel(x_ref, at_ref, part_ref):
    samp = part_ref.shape[0]
    rows = BS // samp
    for r in range(B_DEV):
        at_ref[r * BS : (r + 1) * BS, :] = jnp.transpose(x_ref[:, r * BS : (r + 1) * BS])

    @pl.loop(0, B_DEV)
    def _(r):
        at = at_ref[pl.ds(pl.multiple_of(r * BS, BS), BS), :]
        for c in range(B_DEV):
            tile = jnp.dot(at, x_ref[:, c * BS : (c + 1) * BS], preferred_element_type=jnp.float32)
            for y in range(samp):
                where = pl.ds(pl.multiple_of((r * B_DEV + c) * rows, rows), rows)
                part_ref[y, where, :] = tile[y * rows : (y + 1) * rows]

            @pl.when(r == c)
            def _():
                here = lax.broadcasted_iota(jnp.int32, (BS, BS), 0) == lax.broadcasted_iota(jnp.int32, (BS, BS), 1)
                norm = jnp.sum(jnp.where(here, tile, 0.0), axis=0, keepdims=True)
                for y in range(samp):
                    part_ref[y, 16 * rows + c : 16 * rows + c + 1, :] = norm

    for y in range(samp):
        part_ref[y, 16 * rows + B_DEV :, :] = jnp.zeros((EXTRA - B_DEV, BS), jnp.float32)


def own_tiles(perturb, samp):
    samples, cells = perturb.shape
    return pl.pallas_call(
        own_kernel,
        out_shape=[
            jax.ShapeDtypeStruct((cells, samples), perturb.dtype),
            jax.ShapeDtypeStruct((samp, 16 * BS // samp + EXTRA, BS), jnp.float32),
        ],
        compiler_params=pltpu.CompilerParams(vmem_limit_bytes=40 * MIB),
        cost_estimate=pl.CostEstimate(flops=2 * cells * cells * samples, bytes_accessed=10 * MIB, transcendentals=0),
    )(perturb)


def remote_kernel(slot_ref, dest_ref, at_ref, *refs):
    blocks, parts, all_ref = refs[:4], refs[4:-1], refs[-1]
    samp = len(parts)
    samples = blocks[0].shape[0]
    rows = BS // samp
    r = pl.program_id(0)
    at = at_ref[...]
    for q in range(4):
        tile = jnp.dot(at, blocks[q][...], preferred_element_type=jnp.float32)
        all_ref[2 * q] = tile[:, :HALF]
        all_ref[2 * q + 1] = tile[:, HALF:]
    for j in range(4):
        u = r * 4 + j
        place = pl.ds(pl.multiple_of(u * rows, rows), rows)
        for d in range(samp):
            first = pl.multiple_of(dest_ref[d] * rows, rows)
            parts[d][place, :] = all_ref[slot_ref[u], pl.ds(first, rows), :]

    step = 128
    for q in range(4):

        @pl.when(r == q)
        def _():
            def add(i, total):
                x = blocks[q][pl.ds(pl.multiple_of(i * step, step), step), :].astype(jnp.float32)
                return total + jnp.sum((x * x).reshape(step // 8, 8, 2 * HALF), axis=0)

            total = lax.fori_loop(0, samples // step, add, jnp.zeros((8, 2 * HALF), jnp.float32))
            norm = jnp.sum(total, axis=0, keepdims=True)
            for side in range(2):
                at_row = 16 * rows + 2 * q + side
                for d in range(samp):
                    parts[d][at_row : at_row + 1, :] = norm[:, side * HALF : (side + 1) * HALF]


def remote_tiles(stage, slots, dest, at, blocks, samp):
    cells, samples = at.shape
    full = lambda shape: pl.BlockSpec(shape, lambda i, *s: (0,) * len(shape))
    shape = (16 * BS // samp + EXTRA, HALF)
    block = lambda q: pl.BlockSpec((samples, 2 * HALF), lambda i, *s: (0, stage if q == 1 else 0))
    return pl.pallas_call(
        remote_kernel,
        grid_spec=pltpu.PrefetchScalarGridSpec(
            num_scalar_prefetch=2,
            grid=(B_DEV,),
            in_specs=[pl.BlockSpec((BS, samples), lambda i, *s: (i, 0))] + [block(q) for q in range(4)],
            out_specs=[full(shape)] * samp,
            scratch_shapes=[pltpu.VMEM((8, BS, HALF), jnp.float32)],
        ),
        out_shape=[jax.ShapeDtypeStruct(shape, jnp.float32)] * samp,
        compiler_params=pltpu.CompilerParams(vmem_limit_bytes=30 * MIB),
        cost_estimate=pl.CostEstimate(flops=2 * cells * cells * samples, bytes_accessed=10 * MIB, transcendentals=0),
    )(slots, dest, at, *blocks)


def final_kernel(half, rem_count, place_ref, slot_ref, dest_ref, taper_ref, own_ref, *refs):
    rem_refs, out_ref = refs[:rem_count], refs[-1]
    rows = out_ref.shape[0] // PAIR_DEV
    first = dest_ref[0] * rows
    cols = slice(half * HALF, (half + 1) * HALF)
    lane = lax.broadcasted_iota(jnp.int32, (rows, BS), 1)
    row = lax.broadcasted_iota(jnp.int32, (rows, BS), 0)
    mine = lane == row + first
    for r in range(B_DEV):
        row_norm = own_ref[16 * rows + r : 16 * rows + r + 1, :]
        row_norm = jnp.sum(jnp.where(mine, row_norm, 0.0), axis=1, keepdims=True)
        row_scale = jnp.broadcast_to(lax.rsqrt(row_norm + EPSILON), (rows, HALF))
        for j in range(4):
            u = r * 4 + j
            norm = own_ref[16 * rows + j : 16 * rows + j + 1, cols]
            col_scale = taper_ref[u] * lax.rsqrt(norm + EPSILON)
            tile = own_ref[u * rows : (u + 1) * rows, cols]
            out_ref[pl.ds(place_ref[u], rows, stride=PAIR_DEV), :] = tile * row_scale * col_scale
        for j in range(4):
            u = r * 4 + j
            at_norm = pl.ds(16 * rows + slot_ref[u], 1)
            norm = sum(ref[at_norm, :] for ref in rem_refs)
            col_scale = taper_ref[16 + u] * lax.rsqrt(norm + EPSILON)
            tile = sum(ref[u * rows : (u + 1) * rows, :] for ref in rem_refs)
            out_ref[pl.ds(place_ref[16 + u], rows, stride=PAIR_DEV), :] = tile * row_scale * col_scale


def final(half, place, slots, dest, tapers, own, rems, out, rows):
    full = lambda shape: pl.BlockSpec(shape, lambda i, *s: (0,) * len(shape))
    before = [] if out is None else [out]
    return pl.pallas_call(
        functools.partial(final_kernel, half, len(rems)),
        grid_spec=pltpu.PrefetchScalarGridSpec(
            num_scalar_prefetch=4,
            grid=(1,),
            in_specs=[full(own.shape)]
            + [full(rem.shape) for rem in rems]
            + [pl.BlockSpec(memory_space=pl.ANY)] * len(before),
            out_specs=pl.BlockSpec((rows * PAIR_DEV, HALF), lambda i, *s: (0, half)),
        ),
        out_shape=jax.ShapeDtypeStruct((rows * PAIR_DEV, BS), jnp.float32),
        input_output_aliases={5 + len(rems): 0} if before else {},
        cost_estimate=pl.CostEstimate(flops=MIB, bytes_accessed=4 * MIB, transcendentals=0),
    )(place, slots, dest, tapers, own, *rems, *before)


def body(perturb, partner, bins):
    blk_count = lax.axis_size("blk")
    samp = lax.axis_size("samp")
    here = lax.axis_index("blk")
    owner = partner // B_DEV
    inside = partner % B_DEV
    offset = (owner - here + blk_count + REACH) % blk_count - REACH
    mate = 1 - 2 * (here % 2)
    kind = jnp.where(offset == -2, 0, jnp.where(offset == 2, 3, jnp.where(offset == mate, 1, 2)))
    own = offset == 0
    kind = jnp.where(own, -1, kind)
    four = jnp.arange(4, dtype=jnp.int32)
    hit = (kind.reshape(1, 1, -1) == four[:, None, None]) & (inside.reshape(1, 1, -1) == four[None, :, None])
    need = jnp.any(hit, axis=2)
    low = jnp.min(jnp.where(need, four[None], B_DEV - 1), axis=1)
    high = jnp.max(jnp.where(need, four[None], 0), axis=1)
    want = jnp.stack([low, high], axis=1)
    asked = jnp.concatenate([exchanged(want[q], q, back=True) for q in range(4)])
    chosen = select(asked, perturb)
    mates = exchanged(chosen[6], 1)
    got = []
    for stage in range(STAGES):
        two_below, across, two_above = (exchanged(chosen[3 * stage + i], q) for i, q in enumerate((0, 2, 3)))
        got.append([two_below, mates, across, two_above])

    k_ids = jnp.arange(K_PART, dtype=jnp.int32)[None, :, None]
    is_high = jnp.sum(jnp.where(kind[:, :, None] == four, high[None, None], 0), axis=2) == inside
    slot = 2 * kind + is_high.astype(jnp.int32)
    remote = (~own).astype(jnp.int32)
    earlier = (jnp.arange(K_PART)[:, None] < jnp.arange(K_PART)[None, :]).astype(jnp.int32)
    rank = jnp.sum(remote[:, :, None] * earlier[None], axis=1)
    is_own = own[:, :, None] & (inside[:, :, None] == four)
    is_rem = (~own)[:, :, None] & (rank[:, :, None] == four)
    pick = lambda mask, value: jnp.sum(jnp.where(mask, value, 0), axis=1)
    bin_match = bins[:, :, None] == jnp.arange(NBIN, dtype=jnp.int32)[None, None, :]
    taper = jnp.sum(jnp.where(bin_match, taper_table()[None, None, :], 0.0), axis=2)[:, :, None]
    both = jnp.stack([is_own, is_rem])
    first_place = jnp.arange(B_DEV, dtype=jnp.int32)[None, :, None] * K_PART
    place = (jnp.sum(jnp.where(both, k_ids[None], 0), axis=2) + first_place).reshape(-1)
    tapers = jnp.sum(jnp.where(both, taper[None], 0.0), axis=2).reshape(-1)
    slots = pick(is_rem, slot[:, :, None]).reshape(-1)

    rows = BS // samp
    size = 16 * rows + EXTRA
    me = lax.axis_index("samp")
    ahead = 1 - 2 * (here % 2)
    ring_dest = (me + ahead * jnp.array([-1, -2, 1, 0], jnp.int32) + 2 * samp) % samp
    dest = (me + jnp.arange(samp, dtype=jnp.int32)) % samp
    at, own_part = own_tiles(perturb, samp)

    parts = list(remote_tiles(0, slots, ring_dest, at, got[0], samp))
    own_part, parts[0] = lax.optimization_barrier((own_part, parts[0]))
    own_sum = lax.psum_scatter(own_part.reshape(samp * size, BS), "samp", scatter_dimension=0, tiled=True)
    running = parts[0]
    for d in range(1, samp):
        running = ringed(running) + parts[d]

    parts = remote_tiles(1, slots, dest, at, got[1], samp)
    last = [parts[0]] + [passed_along(parts[d], "samp", d) for d in range(1, samp)]

    out = final(0, place, slots, dest, tapers, own_sum, [running], None, rows)
    out = final(1, place, slots, dest, tapers, own_sum, last, out, rows)
    return out.reshape(rows, PAIR_DEV, BS)


def solution(mesh):
    return jax.shard_map(
        body,
        mesh=mesh,
        in_specs=(P("samp", "blk"), P("blk", None), P("blk", None)),
        out_specs=P("samp", "blk", None),
        check_vma=False,
    )
```

```python
import functools

import jax
import jax.numpy as jnp
from jax import lax
from jax.experimental import pallas as pl
from jax.experimental.pallas import tpu as pltpu
from jax.sharding import PartitionSpec as P

BS = 256
B_DEV = 4
K_PART = 8
REACH = 2
NBIN = 32
PAIR_DEV = 32
HALF = 128
STAGES = 2
EXTRA = 8

EPSILON = 1e-06
MIB = 1 << 20
BIG = 58 * MIB


def passed_along(value, axis, steps):
    count = lax.axis_size(axis)
    pairs = [(source, (source + steps) % count) for source in range(count)]
    return lax.ppermute(value, axis, pairs)


def exchanged(value, kind, back=False):
    count = lax.axis_size("blk")
    source_of = (
        lambda i: i - 2,
        lambda i: i ^ 1,
        lambda i: i - 1 if i % 2 == 0 else i + 1,
        lambda i: i + 2,
    )[kind]
    pairs = [(source_of(i) % count, i) for i in range(count)]
    if back:
        pairs = [(b, a) for a, b in pairs]
    return lax.ppermute(value, "blk", sorted(pairs))


def ringed(value):
    samp, count = lax.axis_size("samp"), lax.axis_size("blk")
    pairs = [
        (y * count + i, (y + 1 - 2 * (i % 2)) % samp * count + i) for y in range(samp) for i in range(count)
    ]
    return lax.ppermute(value, ("samp", "blk"), pairs)


def taper_table():
    scaled = 2.0 * (jnp.arange(NBIN, dtype=jnp.float32) + 0.5) / NBIN
    inner = (((-0.25 * scaled + 0.5) * scaled + 0.625) * scaled - 5.0 / 3.0) * scaled * scaled + 1.0
    outer = (
        ((((scaled / 12.0 - 0.5) * scaled + 0.625) * scaled + 5.0 / 3.0) * scaled - 5.0) * scaled
        + 4.0
        - 2.0 / (3.0 * scaled)
    )
    return jnp.where(scaled <= 1.0, inner, outer)


def select_kernel(plan, want_ref, source_ref, *refs):
    outs, held_ref, in_sems, out_sems = refs[:-3], refs[-3], refs[-2], refs[-1]
    reads, writes = [], []
    for i, (q, side, half, out, column) in enumerate(plan):
        start = pl.multiple_of(want_ref[q * 2 + side] * BS + half * HALF, HALF)
        reads.append(pltpu.make_async_copy(source_ref.at[:, pl.ds(start, HALF)], held_ref.at[i], in_sems.at[i]))
        writes.append(
            pltpu.make_async_copy(held_ref.at[i], outs[out].at[:, pl.ds(column * HALF, HALF)], out_sems.at[i])
        )
    for read in reads:
        read.start()
    for read, write in zip(reads, writes):
        read.wait()
        write.start()
    for write in writes:
        write.wait()


def select(want, perturb):
    samples = perturb.shape[0]
    widths = [2 * HALF] * 6 + [4 * HALF]
    plan = [(q, side, 0, out, side) for out, q in enumerate((0, 2, 3)) for side in range(2)]
    plan += [(1, side, half, 6, 2 * half + side) for half in range(2) for side in range(2)]
    plan += [(q, side, 1, 3 + out, side) for out, q in enumerate((0, 2, 3)) for side in range(2)]
    return pl.pallas_call(
        functools.partial(select_kernel, plan),
        grid_spec=pltpu.PrefetchScalarGridSpec(
            num_scalar_prefetch=1,
            grid=(),
            in_specs=[pl.BlockSpec(memory_space=pl.ANY)],
            out_specs=[pl.BlockSpec(memory_space=pltpu.HBM)] * len(widths),
            scratch_shapes=[
                pltpu.VMEM((len(plan), samples, HALF), perturb.dtype),
                pltpu.SemaphoreType.DMA((len(plan),)),
                pltpu.SemaphoreType.DMA((len(plan),)),
            ],
        ),
        out_shape=[jax.ShapeDtypeStruct((samples, width), perturb.dtype) for width in widths],
        compiler_params=pltpu.CompilerParams(vmem_limit_bytes=BIG),
        cost_estimate=pl.CostEstimate(flops=0, bytes_accessed=MIB * len(plan), transcendentals=0),
    )(want, perturb)


def own_kernel(x_ref, row_ref, at_ref, part_ref):
    samp = part_ref.shape[0]
    rows = BS // samp
    r = pl.program_id(0)
    at_ref[...] = jnp.transpose(row_ref[...])
    at = at_ref[...]
    for c in range(B_DEV):
        tile = jnp.dot(at, x_ref[:, c * BS : (c + 1) * BS], preferred_element_type=jnp.float32)
        for y in range(samp):
            part_ref[y, c * rows : (c + 1) * rows, :] = tile[y * rows : (y + 1) * rows]

        @pl.when(r == c)
        def _():
            here = lax.broadcasted_iota(jnp.int32, (BS, BS), 0) == lax.broadcasted_iota(jnp.int32, (BS, BS), 1)
            norm = jnp.sum(jnp.where(here, tile, 0.0), axis=0, keepdims=True)
            for y in range(samp):
                part_ref[y, BS : BS + EXTRA, :] = jnp.broadcast_to(norm, (EXTRA, BS))


def own_tiles(perturb, samp):
    samples, cells = perturb.shape
    block = BS + EXTRA
    return pl.pallas_call(
        own_kernel,
        grid=(B_DEV,),
        in_specs=[
            pl.BlockSpec((samples, cells), lambda r: (0, 0)),
            pl.BlockSpec((samples, BS), lambda r: (0, r)),
        ],
        out_specs=[
            pl.BlockSpec((BS, samples), lambda r: (r, 0)),
            pl.BlockSpec((samp, block, BS), lambda r: (0, r, 0)),
        ],
        out_shape=[
            jax.ShapeDtypeStruct((cells, samples), perturb.dtype),
            jax.ShapeDtypeStruct((samp, B_DEV * block, BS), jnp.float32),
        ],
        compiler_params=pltpu.CompilerParams(vmem_limit_bytes=BIG),
        cost_estimate=pl.CostEstimate(flops=2 * cells * cells * samples, bytes_accessed=12 * MIB, transcendentals=0),
    )(perturb, perturb)


def remote_kernel(stage, slot_ref, dest_ref, at_ref, *refs):
    blocks, parts, cols_ref, sems = refs[:4], refs[4:-2], refs[-2], refs[-1]
    samp = len(parts)
    samples = cols_ref.shape[1]
    rows = BS // samp
    r = pl.program_id(0)

    @pl.when(r == 0)
    def _():
        copies = []
        for q in range(4):
            for side in range(2):
                column = (2 * stage if q == 1 else 0) + side
                copies.append(
                    pltpu.make_async_copy(
                        blocks[q].at[:, pl.ds(column * HALF, HALF)],
                        cols_ref.at[2 * q + side],
                        sems.at[2 * q + side],
                    )
                )
        for copy in copies:
            copy.start()
        for copy in copies:
            copy.wait()

    at = at_ref[...]
    for pair in range(2):
        u = r * 4 + 2 * pair
        cols = jnp.concatenate([cols_ref[slot_ref[u]], cols_ref[slot_ref[u + 1]]], axis=1)
        tile = jnp.dot(at, cols, preferred_element_type=jnp.float32)
        for side in range(2):
            j = 2 * pair + side
            for d in range(samp):
                for y in range(samp):

                    @pl.when(dest_ref[d] == y)
                    def _():
                        parts[d][j * rows : (j + 1) * rows, :] = tile[
                            y * rows : (y + 1) * rows, side * HALF : (side + 1) * HALF
                        ]

    step = 128
    for side in range(2):
        def add(i, total):
            x = cols_ref[2 * r + side, pl.ds(pl.multiple_of(i * step, step), step), :].astype(jnp.float32)
            return total + jnp.sum((x * x).reshape(step // 8, 8, HALF), axis=0)

        total = lax.fori_loop(0, samples // step, add, jnp.zeros((8, HALF), jnp.float32))
        norm = jnp.sum(total, axis=0, keepdims=True)
        for d in range(samp):
            parts[d][BS + side * 4 : BS + side * 4 + 4, :] = jnp.broadcast_to(norm, (4, HALF))


def remote_tiles(stage, slots, dest, at, blocks, samp):
    cells, samples = at.shape
    block = BS + EXTRA
    out_specs = [pl.BlockSpec((block, HALF), lambda r, *s: (r, 0))] * samp
    out_shape = [jax.ShapeDtypeStruct((B_DEV * block, HALF), jnp.float32)] * samp
    return pl.pallas_call(
        functools.partial(remote_kernel, stage),
        grid_spec=pltpu.PrefetchScalarGridSpec(
            num_scalar_prefetch=2,
            grid=(B_DEV,),
            in_specs=[pl.BlockSpec((BS, samples), lambda r, *s: (r, 0))] + [pl.BlockSpec(memory_space=pl.ANY)] * 4,
            out_specs=out_specs,
            scratch_shapes=[pltpu.VMEM((8, samples, HALF), at.dtype), pltpu.SemaphoreType.DMA((8,))],
        ),
        out_shape=out_shape,
        compiler_params=pltpu.CompilerParams(vmem_limit_bytes=BIG),
        cost_estimate=pl.CostEstimate(flops=2 * cells * cells * samples, bytes_accessed=10 * MIB, transcendentals=0),
    )(slots, dest, at, *blocks)


def final_kernel(half, rem_count, place_ref, slot_ref, dest_ref, taper_ref, own_ref, *refs):
    rem_refs, out_ref = refs[:rem_count], refs[-1]
    rows = out_ref.shape[0] // PAIR_DEV
    first = dest_ref[0] * rows
    cols = slice(half * HALF, (half + 1) * HALF)
    lane = lax.broadcasted_iota(jnp.int32, (rows, BS), 1)
    row = lax.broadcasted_iota(jnp.int32, (rows, BS), 0)
    mine = lane == row + first
    block = BS + EXTRA
    for r in range(B_DEV):
        base = r * block
        row_norm = own_ref[base + BS : base + BS + 1, :]
        row_norm = jnp.sum(jnp.where(mine, row_norm, 0.0), axis=1, keepdims=True)
        row_scale = jnp.broadcast_to(lax.rsqrt(row_norm + EPSILON), (rows, HALF))
        for j in range(4):
            u = r * 4 + j
            norm = own_ref[j * block + BS : j * block + BS + 1, cols]
            col_scale = taper_ref[u] * lax.rsqrt(norm + EPSILON)
            tile = own_ref[base + j * rows : base + (j + 1) * rows, cols]
            out_ref[pl.ds(place_ref[u], rows, stride=PAIR_DEV), :] = tile * row_scale * col_scale
        for j in range(4):
            u = r * 4 + j
            slot = slot_ref[u]
            at_norm = pl.ds(slot // 2 * block + BS + slot % 2 * 4, 1)
            norm = sum(ref[at_norm, :] for ref in rem_refs)
            col_scale = taper_ref[16 + u] * lax.rsqrt(norm + EPSILON)
            tile = sum(ref[base + j * rows : base + (j + 1) * rows, :] for ref in rem_refs)
            out_ref[pl.ds(place_ref[16 + u], rows, stride=PAIR_DEV), :] = tile * row_scale * col_scale


def final(half, place, slots, dest, tapers, own, rems, out, rows):
    full = lambda shape: pl.BlockSpec(shape, lambda i, *s: (0,) * len(shape))
    before = [] if out is None else [out]
    return pl.pallas_call(
        functools.partial(final_kernel, half, len(rems)),
        grid_spec=pltpu.PrefetchScalarGridSpec(
            num_scalar_prefetch=4,
            grid=(1,),
            in_specs=[full(own.shape)]
            + [full(rem.shape) for rem in rems]
            + [pl.BlockSpec(memory_space=pl.ANY)] * len(before),
            out_specs=pl.BlockSpec((rows * PAIR_DEV, HALF), lambda i, *s: (0, half)),
        ),
        out_shape=jax.ShapeDtypeStruct((rows * PAIR_DEV, BS), jnp.float32),
        input_output_aliases={5 + len(rems): 0} if before else {},
        cost_estimate=pl.CostEstimate(flops=MIB, bytes_accessed=4 * MIB, transcendentals=0),
    )(place, slots, dest, tapers, own, *rems, *before)


def body(perturb, partner, bins):
    blk_count = lax.axis_size("blk")
    samp = lax.axis_size("samp")
    here = lax.axis_index("blk")
    owner = partner // B_DEV
    inside = partner % B_DEV
    offset = (owner - here + blk_count + REACH) % blk_count - REACH
    mate = 1 - 2 * (here % 2)
    kind = jnp.where(offset == -2, 0, jnp.where(offset == 2, 3, jnp.where(offset == mate, 1, 2)))
    own = offset == 0
    kind = jnp.where(own, -1, kind)
    four = jnp.arange(4, dtype=jnp.int32)
    hit = (kind.reshape(1, 1, -1) == four[:, None, None]) & (inside.reshape(1, 1, -1) == four[None, :, None])
    need = jnp.any(hit, axis=2)
    low = jnp.min(jnp.where(need, four[None], B_DEV - 1), axis=1)
    high = jnp.max(jnp.where(need, four[None], 0), axis=1)
    want = jnp.stack([low, high], axis=1)
    at, own_part = own_tiles(perturb, samp)
    asked = jnp.concatenate([exchanged(want[q], q, back=True) for q in range(4)])
    asked, at, own_part = lax.optimization_barrier((asked, at, own_part))
    chosen = select(asked, perturb)
    mates = exchanged(chosen[6], 1)
    got = []
    for stage in range(STAGES):
        two_below, across, two_above = (exchanged(chosen[3 * stage + i], q) for i, q in enumerate((0, 2, 3)))
        got.append([two_below, mates, across, two_above])

    k_ids = jnp.arange(K_PART, dtype=jnp.int32)[None, :, None]
    is_high = jnp.sum(jnp.where(kind[:, :, None] == four, high[None, None], 0), axis=2) == inside
    slot = 2 * kind + is_high.astype(jnp.int32)
    remote = (~own).astype(jnp.int32)
    earlier = (jnp.arange(K_PART)[:, None] < jnp.arange(K_PART)[None, :]).astype(jnp.int32)
    rank = jnp.sum(remote[:, :, None] * earlier[None], axis=1)
    is_own = own[:, :, None] & (inside[:, :, None] == four)
    is_rem = (~own)[:, :, None] & (rank[:, :, None] == four)
    pick = lambda mask, value: jnp.sum(jnp.where(mask, value, 0), axis=1)
    bin_match = bins[:, :, None] == jnp.arange(NBIN, dtype=jnp.int32)[None, None, :]
    taper = jnp.sum(jnp.where(bin_match, taper_table()[None, None, :], 0.0), axis=2)[:, :, None]
    both = jnp.stack([is_own, is_rem])
    first_place = jnp.arange(B_DEV, dtype=jnp.int32)[None, :, None] * K_PART
    place = (jnp.sum(jnp.where(both, k_ids[None], 0), axis=2) + first_place).reshape(-1)
    tapers = jnp.sum(jnp.where(both, taper[None], 0.0), axis=2).reshape(-1)
    slots = pick(is_rem, slot[:, :, None]).reshape(-1)

    rows = BS // samp
    size = B_DEV * (BS + EXTRA)
    me = lax.axis_index("samp")
    ahead = 1 - 2 * (here % 2)
    ring_dest = (me + ahead * jnp.array([-1, -2, 1, 0], jnp.int32) + 2 * samp) % samp
    dest = (me + jnp.arange(samp, dtype=jnp.int32)) % samp
    own_sum = lax.psum_scatter(own_part.reshape(samp * size, BS), "samp", scatter_dimension=0, tiled=True)
    parts = remote_tiles(0, slots, ring_dest, at, got[0], samp)
    running = parts[0]
    for d in range(1, samp):
        running = ringed(running) + parts[d]
    parts = remote_tiles(1, slots, dest, at, got[1], samp)
    last = [parts[0]] + [passed_along(parts[d], "samp", d) for d in range(1, samp)]

    out = final(0, place, slots, dest, tapers, own_sum, [running], None, rows)
    out = final(1, place, slots, dest, tapers, own_sum, last, out, rows)
    return out.reshape(rows, PAIR_DEV, BS)


def solution(mesh):
    return jax.shard_map(
        body,
        mesh=mesh,
        in_specs=(P("samp", "blk"), P("blk", None), P("blk", None)),
        out_specs=P("samp", "blk", None),
        check_vma=False,
    )
```

```python
import functools

import jax
import jax.numpy as jnp
from jax import lax
from jax.experimental import pallas as pl
from jax.experimental.pallas import tpu as pltpu
from jax.sharding import PartitionSpec as P

BS = 256
B_DEV = 4
K_PART = 8
REACH = 2
NBIN = 32
PAIR_DEV = 32
HALF = 128
STAGES = 2
EXTRA = 8

EPSILON = 1e-06
MIB = 1 << 20
BIG = 58 * MIB


def passed_along(value, axis, steps):
    count = lax.axis_size(axis)
    pairs = [(source, (source + steps) % count) for source in range(count)]
    return lax.ppermute(value, axis, pairs)


def exchanged(value, kind, back=False):
    count = lax.axis_size("blk")
    source_of = (
        lambda i: i - 2,
        lambda i: i ^ 1,
        lambda i: i - 1 if i % 2 == 0 else i + 1,
        lambda i: i + 2,
    )[kind]
    pairs = [(source_of(i) % count, i) for i in range(count)]
    if back:
        pairs = [(b, a) for a, b in pairs]
    return lax.ppermute(value, "blk", sorted(pairs))


def ringed(value):
    samp, count = lax.axis_size("samp"), lax.axis_size("blk")
    pairs = [
        (y * count + i, (y + 1 - 2 * (i % 2)) % samp * count + i) for y in range(samp) for i in range(count)
    ]
    return lax.ppermute(value, ("samp", "blk"), pairs)


def taper_table():
    scaled = 2.0 * (jnp.arange(NBIN, dtype=jnp.float32) + 0.5) / NBIN
    inner = (((-0.25 * scaled + 0.5) * scaled + 0.625) * scaled - 5.0 / 3.0) * scaled * scaled + 1.0
    outer = (
        ((((scaled / 12.0 - 0.5) * scaled + 0.625) * scaled + 5.0 / 3.0) * scaled - 5.0) * scaled
        + 4.0
        - 2.0 / (3.0 * scaled)
    )
    return jnp.where(scaled <= 1.0, inner, outer)


def select_kernel(plan, want_ref, source_ref, *refs):
    outs, held_ref, in_sems, out_sems = refs[:-3], refs[-3], refs[-2], refs[-1]
    reads, writes = [], []
    for i, (q, side, half, out, column) in enumerate(plan):
        start = pl.multiple_of(want_ref[q * 2 + side] * BS + half * HALF, HALF)
        reads.append(pltpu.make_async_copy(source_ref.at[:, pl.ds(start, HALF)], held_ref.at[i], in_sems.at[i]))
        writes.append(
            pltpu.make_async_copy(held_ref.at[i], outs[out].at[:, pl.ds(column * HALF, HALF)], out_sems.at[i])
        )
    for read in reads:
        read.start()
    for read, write in zip(reads, writes):
        read.wait()
        write.start()
    for write in writes:
        write.wait()


def select(want, perturb):
    samples = perturb.shape[0]
    widths = [2 * HALF] * 6 + [4 * HALF]
    plan = [(q, side, 0, out, side) for out, q in enumerate((0, 2, 3)) for side in range(2)]
    plan += [(1, side, half, 6, 2 * half + side) for half in range(2) for side in range(2)]
    plan += [(q, side, 1, 3 + out, side) for out, q in enumerate((0, 2, 3)) for side in range(2)]
    return pl.pallas_call(
        functools.partial(select_kernel, plan),
        grid_spec=pltpu.PrefetchScalarGridSpec(
            num_scalar_prefetch=1,
            grid=(),
            in_specs=[pl.BlockSpec(memory_space=pl.ANY)],
            out_specs=[pl.BlockSpec(memory_space=pltpu.HBM)] * len(widths),
            scratch_shapes=[
                pltpu.VMEM((len(plan), samples, HALF), perturb.dtype),
                pltpu.SemaphoreType.DMA((len(plan),)),
                pltpu.SemaphoreType.DMA((len(plan),)),
            ],
        ),
        out_shape=[jax.ShapeDtypeStruct((samples, width), perturb.dtype) for width in widths],
        compiler_params=pltpu.CompilerParams(vmem_limit_bytes=BIG),
        cost_estimate=pl.CostEstimate(flops=0, bytes_accessed=MIB * len(plan), transcendentals=0),
    )(want, perturb)


def own_kernel(x_ref, row_ref, at_ref, part_ref):
    samp = part_ref.shape[0]
    rows = BS // samp
    r = pl.program_id(0)
    at_ref[...] = jnp.transpose(row_ref[...])
    at = at_ref[...]
    for c in range(B_DEV):
        tile = jnp.dot(at, x_ref[:, c * BS : (c + 1) * BS], preferred_element_type=jnp.float32)
        for y in range(samp):
            part_ref[y, c * rows : (c + 1) * rows, :] = tile[y * rows : (y + 1) * rows]

        @pl.when(r == c)
        def _():
            here = lax.broadcasted_iota(jnp.int32, (BS, BS), 0) == lax.broadcasted_iota(jnp.int32, (BS, BS), 1)
            norm = jnp.sum(jnp.where(here, tile, 0.0), axis=0, keepdims=True)
            for y in range(samp):
                part_ref[y, BS : BS + EXTRA, :] = jnp.broadcast_to(norm, (EXTRA, BS))


def own_tiles(perturb, samp):
    samples, cells = perturb.shape
    block = BS + EXTRA
    return pl.pallas_call(
        own_kernel,
        grid=(B_DEV,),
        in_specs=[
            pl.BlockSpec((samples, cells), lambda r: (0, 0)),
            pl.BlockSpec((samples, BS), lambda r: (0, r)),
        ],
        out_specs=[
            pl.BlockSpec((BS, samples), lambda r: (r, 0)),
            pl.BlockSpec((samp, block, BS), lambda r: (0, r, 0)),
        ],
        out_shape=[
            jax.ShapeDtypeStruct((cells, samples), perturb.dtype),
            jax.ShapeDtypeStruct((samp, B_DEV * block, BS), jnp.float32),
        ],
        compiler_params=pltpu.CompilerParams(vmem_limit_bytes=BIG),
        cost_estimate=pl.CostEstimate(flops=2 * cells * cells * samples, bytes_accessed=12 * MIB, transcendentals=0),
    )(perturb, perturb)


def remote_kernel(stage, slot_ref, dest_ref, at_ref, *refs):
    blocks, parts, (cols_ref, tile_ref, sems) = refs[:4], refs[4:-3], refs[-3:]
    samp = len(parts)
    samples = cols_ref.shape[1]
    rows = BS // samp
    r = pl.program_id(0)

    @pl.when(r == 0)
    def _():
        copies = []
        for q in range(4):
            for side in range(2):
                column = (2 * stage if q == 1 else 0) + side
                copies.append(
                    pltpu.make_async_copy(
                        blocks[q].at[:, pl.ds(column * HALF, HALF)],
                        cols_ref.at[2 * q + side],
                        sems.at[2 * q + side],
                    )
                )
        for copy in copies:
            copy.start()
        for copy in copies:
            copy.wait()

    at = at_ref[...]
    for pair in range(2):
        u = r * 4 + 2 * pair
        cols = jnp.concatenate([cols_ref[slot_ref[u]], cols_ref[slot_ref[u + 1]]], axis=1)
        tile = jnp.dot(at, cols, preferred_element_type=jnp.float32)
        tile_ref[...] = tile
        for side in range(2):
            j = 2 * pair + side
            for d in range(samp):
                first = pl.multiple_of(dest_ref[d] * rows, rows)
                parts[d][j * rows : (j + 1) * rows, :] = tile_ref[pl.ds(first, rows), side * HALF : (side + 1) * HALF]

    step = 128
    for side in range(2):
        def add(i, total):
            x = cols_ref[2 * r + side, pl.ds(pl.multiple_of(i * step, step), step), :].astype(jnp.float32)
            return total + jnp.sum((x * x).reshape(step // 8, 8, HALF), axis=0)

        total = lax.fori_loop(0, samples // step, add, jnp.zeros((8, HALF), jnp.float32))
        norm = jnp.sum(total, axis=0, keepdims=True)
        for d in range(samp):
            parts[d][BS + side * 4 : BS + side * 4 + 4, :] = jnp.broadcast_to(norm, (4, HALF))


def remote_tiles(stage, slots, dest, at, blocks, samp):
    cells, samples = at.shape
    block = BS + EXTRA
    out_specs = [pl.BlockSpec((block, HALF), lambda r, *s: (r, 0))] * samp
    out_shape = [jax.ShapeDtypeStruct((B_DEV * block, HALF), jnp.float32)] * samp
    return pl.pallas_call(
        functools.partial(remote_kernel, stage),
        grid_spec=pltpu.PrefetchScalarGridSpec(
            num_scalar_prefetch=2,
            grid=(B_DEV,),
            in_specs=[pl.BlockSpec((BS, samples), lambda r, *s: (r, 0))] + [pl.BlockSpec(memory_space=pl.ANY)] * 4,
            out_specs=out_specs,
            scratch_shapes=[
                pltpu.VMEM((8, samples, HALF), at.dtype),
                pltpu.VMEM((BS, BS), jnp.float32),
                pltpu.SemaphoreType.DMA((8,)),
            ],
        ),
        out_shape=out_shape,
        compiler_params=pltpu.CompilerParams(vmem_limit_bytes=BIG),
        cost_estimate=pl.CostEstimate(flops=2 * cells * cells * samples, bytes_accessed=10 * MIB, transcendentals=0),
    )(slots, dest, at, *blocks)


def final_kernel(half, rem_count, place_ref, slot_ref, dest_ref, taper_ref, own_ref, *refs):
    rem_refs, out_ref = refs[:rem_count], refs[-1]
    rows = out_ref.shape[0] // PAIR_DEV
    first = dest_ref[0] * rows
    cols = slice(half * HALF, (half + 1) * HALF)
    lane = lax.broadcasted_iota(jnp.int32, (rows, BS), 1)
    row = lax.broadcasted_iota(jnp.int32, (rows, BS), 0)
    mine = lane == row + first
    block = BS + EXTRA
    for r in range(B_DEV):
        base = r * block
        row_norm = own_ref[base + BS : base + BS + 1, :]
        row_norm = jnp.sum(jnp.where(mine, row_norm, 0.0), axis=1, keepdims=True)
        row_scale = jnp.broadcast_to(lax.rsqrt(row_norm + EPSILON), (rows, HALF))
        for j in range(4):
            u = r * 4 + j
            norm = own_ref[j * block + BS : j * block + BS + 1, cols]
            col_scale = taper_ref[u] * lax.rsqrt(norm + EPSILON)
            tile = own_ref[base + j * rows : base + (j + 1) * rows, cols]
            out_ref[pl.ds(place_ref[u], rows, stride=PAIR_DEV), :] = tile * row_scale * col_scale
        for j in range(4):
            u = r * 4 + j
            slot = slot_ref[u]
            at_norm = pl.ds(slot // 2 * block + BS + slot % 2 * 4, 1)
            norm = sum(ref[at_norm, :] for ref in rem_refs)
            col_scale = taper_ref[16 + u] * lax.rsqrt(norm + EPSILON)
            tile = sum(ref[base + j * rows : base + (j + 1) * rows, :] for ref in rem_refs)
            out_ref[pl.ds(place_ref[16 + u], rows, stride=PAIR_DEV), :] = tile * row_scale * col_scale


def final(half, place, slots, dest, tapers, own, rems, out, rows):
    full = lambda shape: pl.BlockSpec(shape, lambda i, *s: (0,) * len(shape))
    before = [] if out is None else [out]
    return pl.pallas_call(
        functools.partial(final_kernel, half, len(rems)),
        grid_spec=pltpu.PrefetchScalarGridSpec(
            num_scalar_prefetch=4,
            grid=(1,),
            in_specs=[full(own.shape)]
            + [full(rem.shape) for rem in rems]
            + [pl.BlockSpec(memory_space=pl.ANY)] * len(before),
            out_specs=pl.BlockSpec((rows * PAIR_DEV, HALF), lambda i, *s: (0, half)),
        ),
        out_shape=jax.ShapeDtypeStruct((rows * PAIR_DEV, BS), jnp.float32),
        input_output_aliases={5 + len(rems): 0} if before else {},
        cost_estimate=pl.CostEstimate(flops=MIB, bytes_accessed=4 * MIB, transcendentals=0),
    )(place, slots, dest, tapers, own, *rems, *before)


def body(perturb, partner, bins):
    blk_count = lax.axis_size("blk")
    samp = lax.axis_size("samp")
    here = lax.axis_index("blk")
    owner = partner // B_DEV
    inside = partner % B_DEV
    offset = (owner - here + blk_count + REACH) % blk_count - REACH
    mate = 1 - 2 * (here % 2)
    kind = jnp.where(offset == -2, 0, jnp.where(offset == 2, 3, jnp.where(offset == mate, 1, 2)))
    own = offset == 0
    kind = jnp.where(own, -1, kind)
    four = jnp.arange(4, dtype=jnp.int32)
    hit = (kind.reshape(1, 1, -1) == four[:, None, None]) & (inside.reshape(1, 1, -1) == four[None, :, None])
    need = jnp.any(hit, axis=2)
    low = jnp.min(jnp.where(need, four[None], B_DEV - 1), axis=1)
    high = jnp.max(jnp.where(need, four[None], 0), axis=1)
    want = jnp.stack([low, high], axis=1)
    asked = jnp.concatenate([exchanged(want[q], q, back=True) for q in range(4)])

    k_ids = jnp.arange(K_PART, dtype=jnp.int32)[None, :, None]
    is_high = jnp.sum(jnp.where(kind[:, :, None] == four, high[None, None], 0), axis=2) == inside
    slot = 2 * kind + is_high.astype(jnp.int32)
    remote = (~own).astype(jnp.int32)
    earlier = (jnp.arange(K_PART)[:, None] < jnp.arange(K_PART)[None, :]).astype(jnp.int32)
    rank = jnp.sum(remote[:, :, None] * earlier[None], axis=1)
    is_own = own[:, :, None] & (inside[:, :, None] == four)
    is_rem = (~own)[:, :, None] & (rank[:, :, None] == four)
    pick = lambda mask, value: jnp.sum(jnp.where(mask, value, 0), axis=1)
    bin_match = bins[:, :, None] == jnp.arange(NBIN, dtype=jnp.int32)[None, None, :]
    taper = jnp.sum(jnp.where(bin_match, taper_table()[None, None, :], 0.0), axis=2)[:, :, None]
    both = jnp.stack([is_own, is_rem])
    first_place = jnp.arange(B_DEV, dtype=jnp.int32)[None, :, None] * K_PART
    place = (jnp.sum(jnp.where(both, k_ids[None], 0), axis=2) + first_place).reshape(-1)
    tapers = jnp.sum(jnp.where(both, taper[None], 0.0), axis=2).reshape(-1)
    slots = pick(is_rem, slot[:, :, None]).reshape(-1)

    rows = BS // samp
    size = B_DEV * (BS + EXTRA)
    me = lax.axis_index("samp")
    ahead = 1 - 2 * (here % 2)
    ring_dest = (me + ahead * jnp.array([-1, -2, 1, 0], jnp.int32) + 2 * samp) % samp
    dest = (me + jnp.arange(samp, dtype=jnp.int32)) % samp
    chosen = select(asked, perturb)
    mates = exchanged(chosen[6], 1)
    got = []
    for stage in range(STAGES):
        two_below, across, two_above = (exchanged(chosen[3 * stage + i], q) for i, q in enumerate((0, 2, 3)))
        got.append([two_below, mates, across, two_above])
    at, own_part = own_tiles(perturb, samp)
    own_part, *arrived = lax.optimization_barrier((own_part, got[0][0], got[0][2], got[0][3]))
    got[0] = [arrived[0], mates, arrived[1], arrived[2]]
    own_sum = lax.psum_scatter(own_part.reshape(samp * size, BS), "samp", scatter_dimension=0, tiled=True)
    parts = remote_tiles(0, slots, ring_dest, at, got[0], samp)
    running = parts[0]
    for d in range(1, samp):
        running = ringed(running) + parts[d]
    parts = remote_tiles(1, slots, dest, at, got[1], samp)
    last = [parts[0]] + [passed_along(parts[d], "samp", d) for d in range(1, samp)]

    out = final(0, place, slots, dest, tapers, own_sum, [running], None, rows)
    out = final(1, place, slots, dest, tapers, own_sum, last, out, rows)
    return out.reshape(rows, PAIR_DEV, BS)


def solution(mesh):
    return jax.shard_map(
        body,
        mesh=mesh,
        in_specs=(P("samp", "blk"), P("blk", None), P("blk", None)),
        out_specs=P("samp", "blk", None),
        check_vma=False,
    )
```

```python
import functools

import jax
import jax.numpy as jnp
from jax import lax
from jax.experimental import pallas as pl
from jax.experimental.pallas import tpu as pltpu
from jax.sharding import PartitionSpec as P

BS = 256
B_DEV = 4
K_PART = 8
REACH = 2
NBIN = 32
PAIR_DEV = 32
HALF = 128
STAGES = 2
EXTRA = 8
CODE_EXTRA = 16
TOP = 32766.0
STEPS = 256.0

EPSILON = 1e-06
MIB = 1 << 20
BIG = 58 * MIB


def passed_along(value, axis, steps):
    count = lax.axis_size(axis)
    pairs = [(source, (source + steps) % count) for source in range(count)]
    return lax.ppermute(value, axis, pairs)


def exchanged(value, kind, back=False):
    count = lax.axis_size("blk")
    source_of = (
        lambda i: i - 2,
        lambda i: i ^ 1,
        lambda i: i - 1 if i % 2 == 0 else i + 1,
        lambda i: i + 2,
    )[kind]
    pairs = [(source_of(i) % count, i) for i in range(count)]
    if back:
        pairs = [(b, a) for a, b in pairs]
    return lax.ppermute(value, "blk", sorted(pairs))


def taper_table():
    scaled = 2.0 * (jnp.arange(NBIN, dtype=jnp.float32) + 0.5) / NBIN
    inner = (((-0.25 * scaled + 0.5) * scaled + 0.625) * scaled - 5.0 / 3.0) * scaled * scaled + 1.0
    outer = (
        ((((scaled / 12.0 - 0.5) * scaled + 0.625) * scaled + 5.0 / 3.0) * scaled - 5.0) * scaled
        + 4.0
        - 2.0 / (3.0 * scaled)
    )
    return jnp.where(scaled <= 1.0, inner, outer)


def scale_code(largest):
    return jnp.ceil(jnp.log2(jnp.maximum(largest, 1e-30)) * STEPS)


def encode(tile):
    code = scale_code(jnp.max(jnp.abs(tile), axis=0, keepdims=True))
    scaled = jnp.round(tile * (jnp.exp2(code * (-1.0 / STEPS)) * TOP))
    return jnp.clip(scaled, -TOP, TOP), code


def encode_norm(norm):
    code = scale_code(norm)
    scaled = norm * (jnp.exp2(code * (-1.0 / STEPS)) * TOP)
    high = jnp.round(scaled)
    return [code, high, jnp.round((scaled - high) * TOP)]


def decoded_scale(code):
    return jnp.exp2(code * (1.0 / STEPS)) * (1.0 / TOP)


def select_kernel(plan, want_ref, source_ref, *refs):
    outs, held_ref, in_sems, out_sems = refs[:-3], refs[-3], refs[-2], refs[-1]
    reads, writes = [], []
    for i, (q, side, half, out, column) in enumerate(plan):
        start = pl.multiple_of(want_ref[q * 2 + side] * BS + half * HALF, HALF)
        reads.append(pltpu.make_async_copy(source_ref.at[:, pl.ds(start, HALF)], held_ref.at[i], in_sems.at[i]))
        writes.append(
            pltpu.make_async_copy(held_ref.at[i], outs[out].at[:, pl.ds(column * HALF, HALF)], out_sems.at[i])
        )
    for read in reads:
        read.start()
    for read, write in zip(reads, writes):
        read.wait()
        write.start()
    for write in writes:
        write.wait()


def select(stage, want, perturb):
    samples = perturb.shape[0]
    widths = [2 * HALF] * 3
    plan = [(q, side, stage, out, side) for out, q in enumerate((0, 2, 3)) for side in range(2)]
    if stage == 1:
        plan += [(1, side, half, 3, 2 * half + side) for half in range(2) for side in range(2)]
        widths.append(4 * HALF)
    return pl.pallas_call(
        functools.partial(select_kernel, plan),
        grid_spec=pltpu.PrefetchScalarGridSpec(
            num_scalar_prefetch=1,
            grid=(),
            in_specs=[pl.BlockSpec(memory_space=pl.ANY)],
            out_specs=[pl.BlockSpec(memory_space=pltpu.HBM)] * len(widths),
            scratch_shapes=[
                pltpu.VMEM((len(plan), samples, HALF), perturb.dtype),
                pltpu.SemaphoreType.DMA((len(plan),)),
                pltpu.SemaphoreType.DMA((len(plan),)),
            ],
        ),
        out_shape=[jax.ShapeDtypeStruct((samples, width), perturb.dtype) for width in widths],
        compiler_params=pltpu.CompilerParams(vmem_limit_bytes=BIG),
        cost_estimate=pl.CostEstimate(flops=0, bytes_accessed=MIB * len(plan), transcendentals=0),
    )(want, perturb)


def own_kernel(x_ref, row_ref, at_ref, part_ref):
    samp = part_ref.shape[0]
    rows = BS // samp
    r = pl.program_id(0)
    at_ref[...] = jnp.transpose(row_ref[...])
    at = at_ref[...]
    for c in range(B_DEV):
        tile = jnp.dot(at, x_ref[:, c * BS : (c + 1) * BS], preferred_element_type=jnp.float32)
        for y in range(samp):
            part_ref[y, c * rows : (c + 1) * rows, :] = tile[y * rows : (y + 1) * rows]

        @pl.when(r == c)
        def _():
            here = lax.broadcasted_iota(jnp.int32, (BS, BS), 0) == lax.broadcasted_iota(jnp.int32, (BS, BS), 1)
            norm = jnp.sum(jnp.where(here, tile, 0.0), axis=0, keepdims=True)
            for y in range(samp):
                part_ref[y, BS : BS + EXTRA, :] = jnp.broadcast_to(norm, (EXTRA, BS))


def own_tiles(perturb, samp):
    samples, cells = perturb.shape
    block = BS + EXTRA
    return pl.pallas_call(
        own_kernel,
        grid=(B_DEV,),
        in_specs=[
            pl.BlockSpec((samples, cells), lambda r: (0, 0)),
            pl.BlockSpec((samples, BS), lambda r: (0, r)),
        ],
        out_specs=[
            pl.BlockSpec((BS, samples), lambda r: (r, 0)),
            pl.BlockSpec((samp, block, BS), lambda r: (0, r, 0)),
        ],
        out_shape=[
            jax.ShapeDtypeStruct((cells, samples), perturb.dtype),
            jax.ShapeDtypeStruct((samp, B_DEV * block, BS), jnp.float32),
        ],
        compiler_params=pltpu.CompilerParams(vmem_limit_bytes=BIG),
        cost_estimate=pl.CostEstimate(flops=2 * cells * cells * samples, bytes_accessed=12 * MIB, transcendentals=0),
    )(perturb, perturb)


def remote_kernel(stage, slot_ref, dest_ref, at_ref, *refs):
    blocks, parts, (cols_ref, tile_ref, sems) = refs[:4], refs[4:-3], refs[-3:]
    samp = len(parts)
    samples = cols_ref.shape[1]
    rows = BS // samp
    r = pl.program_id(0)

    @pl.when(r == 0)
    def _():
        copies = []
        for q in range(4):
            for side in range(2):
                column = (2 * stage if q == 1 else 0) + side
                copies.append(
                    pltpu.make_async_copy(
                        blocks[q].at[:, pl.ds(column * HALF, HALF)],
                        cols_ref.at[2 * q + side],
                        sems.at[2 * q + side],
                    )
                )
        for copy in copies:
            copy.start()
        for copy in copies:
            copy.wait()

    at = at_ref[...]
    codes = [[] for _ in range(samp - 1)]
    for pair in range(2):
        u = r * 4 + 2 * pair
        cols = jnp.concatenate([cols_ref[slot_ref[u]], cols_ref[slot_ref[u + 1]]], axis=1)
        tile = jnp.dot(at, cols, preferred_element_type=jnp.float32)
        tile_ref[...] = tile
        for side in range(2):
            j = 2 * pair + side
            for d in range(samp):
                first = pl.multiple_of(dest_ref[d] * rows, rows)
                piece = tile_ref[pl.ds(first, rows), side * HALF : (side + 1) * HALF]
                if d > 0:
                    piece, code = encode(piece)
                    piece = piece.astype(jnp.int32).astype(jnp.int16)
                    codes[d - 1].append(code)
                parts[d][j * rows : (j + 1) * rows, :] = piece

    step = 128
    norm_codes = []
    for side in range(2):
        def add(i, total):
            x = cols_ref[2 * r + side, pl.ds(pl.multiple_of(i * step, step), step), :].astype(jnp.float32)
            return total + jnp.sum((x * x).reshape(step // 8, 8, HALF), axis=0)

        total = lax.fori_loop(0, samples // step, add, jnp.zeros((8, HALF), jnp.float32))
        norm = jnp.sum(total, axis=0, keepdims=True)
        norm_codes += encode_norm(norm)
        parts[0][BS + side * 4 : BS + side * 4 + 4, :] = jnp.broadcast_to(norm, (4, HALF))
    row_id = lax.broadcasted_iota(jnp.int32, (CODE_EXTRA, HALF), 0)
    for d in range(1, samp):
        extra = jnp.zeros((CODE_EXTRA, HALF), jnp.float32)
        for i, row in enumerate(codes[d - 1] + norm_codes):
            extra = jnp.where(row_id == i, row, extra)
        parts[d][BS : BS + CODE_EXTRA, :] = extra.astype(jnp.int32).astype(jnp.int16)


def remote_tiles(stage, slots, dest, at, blocks, samp):
    cells, samples = at.shape
    blocks_out = [(BS + EXTRA, jnp.float32)] + [(BS + CODE_EXTRA, jnp.int16)] * (samp - 1)
    out_specs = [pl.BlockSpec((block, HALF), lambda r, *s: (r, 0)) for block, _ in blocks_out]
    out_shape = [jax.ShapeDtypeStruct((B_DEV * block, HALF), dtype) for block, dtype in blocks_out]
    return pl.pallas_call(
        functools.partial(remote_kernel, stage),
        grid_spec=pltpu.PrefetchScalarGridSpec(
            num_scalar_prefetch=2,
            grid=(B_DEV,),
            in_specs=[pl.BlockSpec((BS, samples), lambda r, *s: (r, 0))] + [pl.BlockSpec(memory_space=pl.ANY)] * 4,
            out_specs=out_specs,
            scratch_shapes=[
                pltpu.VMEM((8, samples, HALF), at.dtype),
                pltpu.VMEM((BS, BS), jnp.float32),
                pltpu.SemaphoreType.DMA((8,)),
            ],
        ),
        out_shape=out_shape,
        compiler_params=pltpu.CompilerParams(vmem_limit_bytes=BIG),
        cost_estimate=pl.CostEstimate(flops=2 * cells * cells * samples, bytes_accessed=10 * MIB, transcendentals=0),
    )(slots, dest, at, *blocks)


def final_kernel(half, place_ref, slot_ref, dest_ref, taper_ref, own_ref, kept_ref, *refs):
    coded_refs, out_ref, norm_ref = refs[:3], refs[-2], refs[-1]
    rows = out_ref.shape[0] // PAIR_DEV
    first = dest_ref[0] * rows
    cols = slice(half * HALF, (half + 1) * HALF)
    lane = lax.broadcasted_iota(jnp.int32, (rows, BS), 1)
    row = lax.broadcasted_iota(jnp.int32, (rows, BS), 0)
    mine = lane == row + first
    block = BS + EXTRA
    coded = BS + CODE_EXTRA
    extras = []
    for r in range(B_DEV):
        extras.append(
            [ref[r * coded + BS : (r + 1) * coded, :].astype(jnp.int32).astype(jnp.float32) for ref in coded_refs]
        )
        for side in range(2):
            norm = kept_ref[r * block + BS + side * 4 : r * block + BS + side * 4 + 1, :]
            for extra in extras[r]:
                code, high, low = (extra[4 + 3 * side + i : 5 + 3 * side + i, :] for i in range(3))
                norm = norm + (high + low * (1.0 / TOP)) * decoded_scale(code)
            norm_ref[2 * r + side : 2 * r + side + 1, :] = norm
    for r in range(B_DEV):
        base = r * block
        row_norm = own_ref[base + BS : base + BS + 1, :]
        row_norm = jnp.sum(jnp.where(mine, row_norm, 0.0), axis=1, keepdims=True)
        row_scale = jnp.broadcast_to(lax.rsqrt(row_norm + EPSILON), (rows, HALF))
        for j in range(4):
            u = r * 4 + j
            norm = own_ref[j * block + BS : j * block + BS + 1, cols]
            col_scale = taper_ref[u] * lax.rsqrt(norm + EPSILON)
            tile = own_ref[base + j * rows : base + (j + 1) * rows, cols]
            out_ref[pl.ds(place_ref[u], rows, stride=PAIR_DEV), :] = tile * row_scale * col_scale
        for j in range(4):
            u = r * 4 + j
            norm = norm_ref[pl.ds(slot_ref[u], 1), :]
            col_scale = taper_ref[16 + u] * lax.rsqrt(norm + EPSILON)
            tile = kept_ref[base + j * rows : base + (j + 1) * rows, :]
            for ref, extra in zip(coded_refs, extras[r]):
                piece = ref[r * coded + j * rows : r * coded + (j + 1) * rows, :].astype(jnp.int32).astype(jnp.float32)
                tile = tile + piece * decoded_scale(extra[j : j + 1, :])
            out_ref[pl.ds(place_ref[16 + u], rows, stride=PAIR_DEV), :] = tile * row_scale * col_scale


def final(half, place, slots, dest, tapers, own, rems, out, rows):
    full = lambda shape: pl.BlockSpec(shape, lambda i, *s: (0,) * len(shape))
    before = [] if out is None else [out]
    return pl.pallas_call(
        functools.partial(final_kernel, half),
        grid_spec=pltpu.PrefetchScalarGridSpec(
            num_scalar_prefetch=4,
            grid=(1,),
            in_specs=[full(own.shape)]
            + [full(rem.shape) for rem in rems]
            + [pl.BlockSpec(memory_space=pl.ANY)] * len(before),
            out_specs=pl.BlockSpec((rows * PAIR_DEV, HALF), lambda i, *s: (0, half)),
            scratch_shapes=[pltpu.VMEM((8, HALF), jnp.float32)],
        ),
        out_shape=jax.ShapeDtypeStruct((rows * PAIR_DEV, BS), jnp.float32),
        input_output_aliases={5 + len(rems): 0} if before else {},
        cost_estimate=pl.CostEstimate(flops=MIB, bytes_accessed=4 * MIB, transcendentals=0),
    )(place, slots, dest, tapers, own, *rems, *before)


def body(perturb, partner, bins):
    blk_count = lax.axis_size("blk")
    samp = lax.axis_size("samp")
    here = lax.axis_index("blk")
    owner = partner // B_DEV
    inside = partner % B_DEV
    offset = (owner - here + blk_count + REACH) % blk_count - REACH
    mate = 1 - 2 * (here % 2)
    kind = jnp.where(offset == -2, 0, jnp.where(offset == 2, 3, jnp.where(offset == mate, 1, 2)))
    own = offset == 0
    kind = jnp.where(own, -1, kind)
    four = jnp.arange(4, dtype=jnp.int32)
    hit = (kind.reshape(1, 1, -1) == four[:, None, None]) & (inside.reshape(1, 1, -1) == four[None, :, None])
    need = jnp.any(hit, axis=2)
    low = jnp.min(jnp.where(need, four[None], B_DEV - 1), axis=1)
    high = jnp.max(jnp.where(need, four[None], 0), axis=1)
    want = jnp.stack([low, high], axis=1)
    asked = jnp.concatenate([exchanged(want[q], q, back=True) for q in range(4)])

    k_ids = jnp.arange(K_PART, dtype=jnp.int32)[None, :, None]
    is_high = jnp.sum(jnp.where(kind[:, :, None] == four, high[None, None], 0), axis=2) == inside
    slot = 2 * kind + is_high.astype(jnp.int32)
    remote = (~own).astype(jnp.int32)
    earlier = (jnp.arange(K_PART)[:, None] < jnp.arange(K_PART)[None, :]).astype(jnp.int32)
    rank = jnp.sum(remote[:, :, None] * earlier[None], axis=1)
    is_own = own[:, :, None] & (inside[:, :, None] == four)
    is_rem = (~own)[:, :, None] & (rank[:, :, None] == four)
    pick = lambda mask, value: jnp.sum(jnp.where(mask, value, 0), axis=1)
    bin_match = bins[:, :, None] == jnp.arange(NBIN, dtype=jnp.int32)[None, None, :]
    taper = jnp.sum(jnp.where(bin_match, taper_table()[None, None, :], 0.0), axis=2)[:, :, None]
    both = jnp.stack([is_own, is_rem])
    first_place = jnp.arange(B_DEV, dtype=jnp.int32)[None, :, None] * K_PART
    place = (jnp.sum(jnp.where(both, k_ids[None], 0), axis=2) + first_place).reshape(-1)
    tapers = jnp.sum(jnp.where(both, taper[None], 0.0), axis=2).reshape(-1)
    slots = pick(is_rem, slot[:, :, None]).reshape(-1)

    rows = BS // samp
    size = B_DEV * (BS + EXTRA)
    me = lax.axis_index("samp")
    dest = (me + jnp.arange(samp, dtype=jnp.int32)) % samp
    chosen = [select(stage, asked, perturb) for stage in range(STAGES)]
    mates = exchanged(chosen[1][3], 1)
    got = []
    for stage in range(STAGES):
        two_below, across, two_above = (exchanged(chosen[stage][i], q) for i, q in enumerate((0, 2, 3)))
        got.append([two_below, mates, across, two_above])
    held, _ = lax.optimization_barrier((perturb, chosen[1][0]))
    at, own_part = own_tiles(held, samp)
    own_part, *arrived = lax.optimization_barrier((own_part, got[0][0], got[0][2], got[0][3]))
    got[0] = [arrived[0], mates, arrived[1], arrived[2]]
    own_sum = lax.psum_scatter(own_part.reshape(samp * size, BS), "samp", scatter_dimension=0, tiled=True)
    sums = []
    for stage in range(STAGES):
        parts = remote_tiles(stage, slots, dest, at, got[stage], samp)
        last = [parts[0]] + [passed_along(parts[d], "samp", d) for d in range(1, samp)]
        if stage == 0:
            dest, *last[1:3] = lax.optimization_barrier((dest, *last[1:3]))
        sums.append(last)

    out = final(0, place, slots, dest, tapers, own_sum, sums[0], None, rows)
    out = final(1, place, slots, dest, tapers, own_sum, sums[1], out, rows)
    return out.reshape(rows, PAIR_DEV, BS)


def solution(mesh):
    return jax.shard_map(
        body,
        mesh=mesh,
        in_specs=(P("samp", "blk"), P("blk", None), P("blk", None)),
        out_specs=P("samp", "blk", None),
        check_vma=False,
    )
```

```python
import functools

import jax
import jax.numpy as jnp
from jax import lax
from jax.experimental import pallas as pl
from jax.experimental.pallas import tpu as pltpu
from jax.sharding import PartitionSpec as P

BS = 256
B_DEV = 4
K_PART = 8
REACH = 2
NBIN = 32
PAIR_DEV = 32
HALF = 128
STAGES = 2
EXTRA = 8
CODE_EXTRA = 16
TOP = 32766.0
STEPS = 256.0

EPSILON = 1e-06
MIB = 1 << 20
BIG = 58 * MIB


def passed_along(value, axis, steps):
    count = lax.axis_size(axis)
    pairs = [(source, (source + steps) % count) for source in range(count)]
    return lax.ppermute(value, axis, pairs)


def exchanged(value, kind, back=False):
    count = lax.axis_size("blk")
    source_of = (
        lambda i: i - 2,
        lambda i: i ^ 1,
        lambda i: i - 1 if i % 2 == 0 else i + 1,
        lambda i: i + 2,
    )[kind]
    pairs = [(source_of(i) % count, i) for i in range(count)]
    if back:
        pairs = [(b, a) for a, b in pairs]
    return lax.ppermute(value, "blk", sorted(pairs))


def taper_table():
    scaled = 2.0 * (jnp.arange(NBIN, dtype=jnp.float32) + 0.5) / NBIN
    inner = (((-0.25 * scaled + 0.5) * scaled + 0.625) * scaled - 5.0 / 3.0) * scaled * scaled + 1.0
    outer = (
        ((((scaled / 12.0 - 0.5) * scaled + 0.625) * scaled + 5.0 / 3.0) * scaled - 5.0) * scaled
        + 4.0
        - 2.0 / (3.0 * scaled)
    )
    return jnp.where(scaled <= 1.0, inner, outer)


def scale_code(largest):
    return jnp.ceil(jnp.log2(jnp.maximum(largest, 1e-30)) * STEPS)


def encode(tile):
    code = scale_code(jnp.max(jnp.abs(tile), axis=0, keepdims=True))
    scaled = jnp.round(tile * (jnp.exp2(code * (-1.0 / STEPS)) * TOP))
    return jnp.clip(scaled, -TOP, TOP), code


def encode_norm(norm):
    code = scale_code(norm)
    scaled = norm * (jnp.exp2(code * (-1.0 / STEPS)) * TOP)
    high = jnp.round(scaled)
    return [code, high, jnp.round((scaled - high) * TOP)]


def decoded_scale(code):
    return jnp.exp2(code * (1.0 / STEPS)) * (1.0 / TOP)


def select_kernel(plan, want_ref, source_ref, *refs):
    outs, held_ref, in_sems, out_sems = refs[:-3], refs[-3], refs[-2], refs[-1]
    reads, writes = [], []
    for i, (q, side, half, out, column) in enumerate(plan):
        start = pl.multiple_of(want_ref[q * 2 + side] * BS + half * HALF, HALF)
        reads.append(pltpu.make_async_copy(source_ref.at[:, pl.ds(start, HALF)], held_ref.at[i], in_sems.at[i]))
        writes.append(
            pltpu.make_async_copy(held_ref.at[i], outs[out].at[:, pl.ds(column * HALF, HALF)], out_sems.at[i])
        )
    for read in reads:
        read.start()
    for read, write in zip(reads, writes):
        read.wait()
        write.start()
    for write in writes:
        write.wait()


def select(stage, want, perturb):
    samples = perturb.shape[0]
    widths = [2 * HALF] * 3
    plan = [(q, side, stage, out, side) for out, q in enumerate((0, 2, 3)) for side in range(2)]
    if stage == 1:
        plan += [(1, side, half, 3, 2 * half + side) for half in range(2) for side in range(2)]
        widths.append(4 * HALF)
    return pl.pallas_call(
        functools.partial(select_kernel, plan),
        grid_spec=pltpu.PrefetchScalarGridSpec(
            num_scalar_prefetch=1,
            grid=(),
            in_specs=[pl.BlockSpec(memory_space=pl.ANY)],
            out_specs=[pl.BlockSpec(memory_space=pltpu.HBM)] * len(widths),
            scratch_shapes=[
                pltpu.VMEM((len(plan), samples, HALF), perturb.dtype),
                pltpu.SemaphoreType.DMA((len(plan),)),
                pltpu.SemaphoreType.DMA((len(plan),)),
            ],
        ),
        out_shape=[jax.ShapeDtypeStruct((samples, width), perturb.dtype) for width in widths],
        compiler_params=pltpu.CompilerParams(vmem_limit_bytes=BIG),
        cost_estimate=pl.CostEstimate(flops=0, bytes_accessed=MIB * len(plan), transcendentals=0),
    )(want, perturb)


def with_rows(count, width, rows):
    row_id = lax.broadcasted_iota(jnp.int32, (count, width), 0)
    block = jnp.zeros((count, width), jnp.float32)
    for i, row in enumerate(rows):
        block = jnp.where(row_id == i, row, block)
    return block.astype(jnp.int32).astype(jnp.int16)


def own_kernel(dest_ref, x_ref, row_ref, at_ref, *refs):
    parts, tile_ref, norm_ref = refs[:-2], refs[-2], refs[-1]
    samp = len(parts)
    rows = BS // samp
    r = pl.program_id(0)
    at_ref[...] = jnp.transpose(row_ref[...])
    at = at_ref[...]
    codes = [[] for _ in range(samp - 1)]
    for c in range(B_DEV):
        tile_ref[...] = jnp.dot(at, x_ref[:, c * BS : (c + 1) * BS], preferred_element_type=jnp.float32)
        for d in range(samp):
            piece = tile_ref[pl.ds(pl.multiple_of(dest_ref[d] * rows, rows), rows), :]
            if d > 0:
                piece, code = encode(piece)
                piece = piece.astype(jnp.int32).astype(jnp.int16)
                codes[d - 1].append(code)
            parts[d][c * rows : (c + 1) * rows, :] = piece

        @pl.when(r == c)
        def _():
            here = lax.broadcasted_iota(jnp.int32, (BS, BS), 0) == lax.broadcasted_iota(jnp.int32, (BS, BS), 1)
            norm = jnp.sum(jnp.where(here, tile_ref[...], 0.0), axis=0, keepdims=True)
            norm_ref[...] = jnp.broadcast_to(norm, norm_ref.shape)

    parts[0][BS : BS + EXTRA, :] = norm_ref[...]
    norm_codes = encode_norm(norm_ref[0:1, :])
    for d in range(1, samp):
        parts[d][BS : BS + CODE_EXTRA, :] = with_rows(CODE_EXTRA, BS, codes[d - 1] + norm_codes)


def own_tiles(dest, perturb):
    samples, cells = perturb.shape
    samp = dest.shape[0]
    blocks_out = [(BS + EXTRA, jnp.float32)] + [(BS + CODE_EXTRA, jnp.int16)] * (samp - 1)
    return pl.pallas_call(
        own_kernel,
        grid_spec=pltpu.PrefetchScalarGridSpec(
            num_scalar_prefetch=1,
            grid=(B_DEV,),
            in_specs=[
                pl.BlockSpec((samples, cells), lambda r, *s: (0, 0)),
                pl.BlockSpec((samples, BS), lambda r, *s: (0, r)),
            ],
            out_specs=[pl.BlockSpec((BS, samples), lambda r, *s: (r, 0))]
            + [pl.BlockSpec((block, BS), lambda r, *s: (r, 0)) for block, _ in blocks_out],
            scratch_shapes=[pltpu.VMEM((BS, BS), jnp.float32), pltpu.VMEM((EXTRA, BS), jnp.float32)],
        ),
        out_shape=[jax.ShapeDtypeStruct((cells, samples), perturb.dtype)]
        + [jax.ShapeDtypeStruct((B_DEV * block, BS), dtype) for block, dtype in blocks_out],
        compiler_params=pltpu.CompilerParams(vmem_limit_bytes=BIG),
        cost_estimate=pl.CostEstimate(flops=2 * cells * cells * samples, bytes_accessed=12 * MIB, transcendentals=0),
    )(dest, perturb, perturb)


def total_kernel(kept_ref, *refs):
    coded_refs, out_ref = refs[:-1], refs[-1]
    rows = BS // (len(coded_refs) + 1)
    block = BS + EXTRA
    coded = BS + CODE_EXTRA
    for r in range(B_DEV):
        extras = [
            ref[r * coded + BS : (r + 1) * coded, :].astype(jnp.int32).astype(jnp.float32) for ref in coded_refs
        ]
        for j in range(4):
            here = slice(r * block + j * rows, r * block + (j + 1) * rows)
            tile = kept_ref[here, :]
            for ref, extra in zip(coded_refs, extras):
                piece = ref[r * coded + j * rows : r * coded + (j + 1) * rows, :].astype(jnp.int32)
                tile = tile + piece.astype(jnp.float32) * decoded_scale(extra[j : j + 1, :])
            out_ref[here, :] = tile
        norm = kept_ref[r * block + BS : r * block + BS + 1, :]
        for extra in extras:
            code, high, low = (extra[4 + i : 5 + i, :] for i in range(3))
            norm = norm + (high + low * (1.0 / TOP)) * decoded_scale(code)
        out_ref[r * block + BS : (r + 1) * block, :] = jnp.broadcast_to(norm, (EXTRA, BS))


def own_total(kept, coded):
    return pl.pallas_call(
        total_kernel,
        out_shape=jax.ShapeDtypeStruct(kept.shape, kept.dtype),
        compiler_params=pltpu.CompilerParams(vmem_limit_bytes=16 * MIB),
        cost_estimate=pl.CostEstimate(flops=4 * MIB, bytes_accessed=4 * MIB, transcendentals=0),
    )(kept, *coded)


def remote_kernel(stage, slot_ref, dest_ref, at_ref, *refs):
    blocks, parts, (cols_ref, tile_ref, sems) = refs[:4], refs[4:-3], refs[-3:]
    samp = len(parts)
    samples = cols_ref.shape[1]
    rows = BS // samp
    r = pl.program_id(0)

    @pl.when(r == 0)
    def _():
        copies = []
        for q in range(4):
            for side in range(2):
                column = (2 * stage if q == 1 else 0) + side
                copies.append(
                    pltpu.make_async_copy(
                        blocks[q].at[:, pl.ds(column * HALF, HALF)],
                        cols_ref.at[2 * q + side],
                        sems.at[2 * q + side],
                    )
                )
        for copy in copies:
            copy.start()
        for copy in copies:
            copy.wait()

    at = at_ref[...]
    codes = [[] for _ in range(samp - 1)]
    for pair in range(2):
        u = r * 4 + 2 * pair
        cols = jnp.concatenate([cols_ref[slot_ref[u]], cols_ref[slot_ref[u + 1]]], axis=1)
        tile = jnp.dot(at, cols, preferred_element_type=jnp.float32)
        tile_ref[...] = tile
        for side in range(2):
            j = 2 * pair + side
            for d in range(samp):
                first = pl.multiple_of(dest_ref[d] * rows, rows)
                piece = tile_ref[pl.ds(first, rows), side * HALF : (side + 1) * HALF]
                if d > 0:
                    piece, code = encode(piece)
                    piece = piece.astype(jnp.int32).astype(jnp.int16)
                    codes[d - 1].append(code)
                parts[d][j * rows : (j + 1) * rows, :] = piece

    step, lanes = 256, 32

    def add(i, totals):
        at_rows = pl.ds(pl.multiple_of(i * step, step), step)
        squares = [jnp.square(cols_ref[2 * r + side, at_rows, :].astype(jnp.float32)) for side in range(2)]
        return [
            total + jnp.sum(square.reshape(step // lanes, lanes, HALF), axis=0)
            for total, square in zip(totals, squares)
        ]

    totals = lax.fori_loop(0, samples // step, add, [jnp.zeros((lanes, HALF), jnp.float32)] * 2)
    norm_codes = []
    for side, total in enumerate(totals):
        norm = jnp.sum(total, axis=0, keepdims=True)
        norm_codes += encode_norm(norm)
        parts[0][BS + side * 4 : BS + side * 4 + 4, :] = jnp.broadcast_to(norm, (4, HALF))
    for d in range(1, samp):
        parts[d][BS : BS + CODE_EXTRA, :] = with_rows(CODE_EXTRA, HALF, codes[d - 1] + norm_codes)


def remote_tiles(stage, slots, dest, at, blocks, samp):
    cells, samples = at.shape
    blocks_out = [(BS + EXTRA, jnp.float32)] + [(BS + CODE_EXTRA, jnp.int16)] * (samp - 1)
    out_specs = [pl.BlockSpec((block, HALF), lambda r, *s: (r, 0)) for block, _ in blocks_out]
    out_shape = [jax.ShapeDtypeStruct((B_DEV * block, HALF), dtype) for block, dtype in blocks_out]
    return pl.pallas_call(
        functools.partial(remote_kernel, stage),
        grid_spec=pltpu.PrefetchScalarGridSpec(
            num_scalar_prefetch=2,
            grid=(B_DEV,),
            in_specs=[pl.BlockSpec((BS, samples), lambda r, *s: (r, 0))] + [pl.BlockSpec(memory_space=pl.ANY)] * 4,
            out_specs=out_specs,
            scratch_shapes=[
                pltpu.VMEM((8, samples, HALF), at.dtype),
                pltpu.VMEM((BS, BS), jnp.float32),
                pltpu.SemaphoreType.DMA((8,)),
            ],
        ),
        out_shape=out_shape,
        compiler_params=pltpu.CompilerParams(vmem_limit_bytes=BIG),
        cost_estimate=pl.CostEstimate(flops=2 * cells * cells * samples, bytes_accessed=10 * MIB, transcendentals=0),
    )(slots, dest, at, *blocks)


def final_kernel(half, place_ref, slot_ref, dest_ref, taper_ref, own_ref, kept_ref, *refs):
    coded_refs, out_ref, norm_ref = refs[:3], refs[-2], refs[-1]
    rows = out_ref.shape[0] // PAIR_DEV
    first = dest_ref[0] * rows
    cols = slice(half * HALF, (half + 1) * HALF)
    lane = lax.broadcasted_iota(jnp.int32, (rows, BS), 1)
    row = lax.broadcasted_iota(jnp.int32, (rows, BS), 0)
    mine = lane == row + first
    block = BS + EXTRA
    coded = BS + CODE_EXTRA
    extras = []
    for r in range(B_DEV):
        extras.append(
            [ref[r * coded + BS : (r + 1) * coded, :].astype(jnp.int32).astype(jnp.float32) for ref in coded_refs]
        )
        for side in range(2):
            norm = kept_ref[r * block + BS + side * 4 : r * block + BS + side * 4 + 1, :]
            for extra in extras[r]:
                code, high, low = (extra[4 + 3 * side + i : 5 + 3 * side + i, :] for i in range(3))
                norm = norm + (high + low * (1.0 / TOP)) * decoded_scale(code)
            norm_ref[2 * r + side : 2 * r + side + 1, :] = norm
    for r in range(B_DEV):
        base = r * block
        row_norm = own_ref[base + BS : base + BS + 1, :]
        row_norm = jnp.sum(jnp.where(mine, row_norm, 0.0), axis=1, keepdims=True)
        row_scale = jnp.broadcast_to(lax.rsqrt(row_norm + EPSILON), (rows, HALF))
        for j in range(4):
            u = r * 4 + j
            norm = own_ref[j * block + BS : j * block + BS + 1, cols]
            col_scale = taper_ref[u] * lax.rsqrt(norm + EPSILON)
            tile = own_ref[base + j * rows : base + (j + 1) * rows, cols]
            out_ref[pl.ds(place_ref[u], rows, stride=PAIR_DEV), :] = tile * row_scale * col_scale
        for j in range(4):
            u = r * 4 + j
            norm = norm_ref[pl.ds(slot_ref[u], 1), :]
            col_scale = taper_ref[16 + u] * lax.rsqrt(norm + EPSILON)
            tile = kept_ref[base + j * rows : base + (j + 1) * rows, :]
            for ref, extra in zip(coded_refs, extras[r]):
                piece = ref[r * coded + j * rows : r * coded + (j + 1) * rows, :].astype(jnp.int32).astype(jnp.float32)
                tile = tile + piece * decoded_scale(extra[j : j + 1, :])
            out_ref[pl.ds(place_ref[16 + u], rows, stride=PAIR_DEV), :] = tile * row_scale * col_scale


def final(half, place, slots, dest, tapers, own, rems, out, rows):
    full = lambda shape: pl.BlockSpec(shape, lambda i, *s: (0,) * len(shape))
    before = [] if out is None else [out]
    return pl.pallas_call(
        functools.partial(final_kernel, half),
        grid_spec=pltpu.PrefetchScalarGridSpec(
            num_scalar_prefetch=4,
            grid=(1,),
            in_specs=[full(own.shape)]
            + [full(rem.shape) for rem in rems]
            + [pl.BlockSpec(memory_space=pl.ANY)] * len(before),
            out_specs=pl.BlockSpec((rows * PAIR_DEV, HALF), lambda i, *s: (0, half)),
            scratch_shapes=[pltpu.VMEM((8, HALF), jnp.float32)],
        ),
        out_shape=jax.ShapeDtypeStruct((rows * PAIR_DEV, BS), jnp.float32),
        input_output_aliases={5 + len(rems): 0} if before else {},
        cost_estimate=pl.CostEstimate(flops=MIB, bytes_accessed=4 * MIB, transcendentals=0),
    )(place, slots, dest, tapers, own, *rems, *before)


def body(perturb, partner, bins):
    blk_count = lax.axis_size("blk")
    samp = lax.axis_size("samp")
    here = lax.axis_index("blk")
    owner = partner // B_DEV
    inside = partner % B_DEV
    offset = (owner - here + blk_count + REACH) % blk_count - REACH
    mate = 1 - 2 * (here % 2)
    kind = jnp.where(offset == -2, 0, jnp.where(offset == 2, 3, jnp.where(offset == mate, 1, 2)))
    own = offset == 0
    kind = jnp.where(own, -1, kind)
    four = jnp.arange(4, dtype=jnp.int32)
    hit = (kind.reshape(1, 1, -1) == four[:, None, None]) & (inside.reshape(1, 1, -1) == four[None, :, None])
    need = jnp.any(hit, axis=2)
    low = jnp.min(jnp.where(need, four[None], B_DEV - 1), axis=1)
    high = jnp.max(jnp.where(need, four[None], 0), axis=1)
    want = jnp.stack([low, high], axis=1)
    asked = jnp.concatenate([exchanged(want[q], q, back=True) for q in range(4)])

    k_ids = jnp.arange(K_PART, dtype=jnp.int32)[None, :, None]
    is_high = jnp.sum(jnp.where(kind[:, :, None] == four, high[None, None], 0), axis=2) == inside
    slot = 2 * kind + is_high.astype(jnp.int32)
    remote = (~own).astype(jnp.int32)
    earlier = (jnp.arange(K_PART)[:, None] < jnp.arange(K_PART)[None, :]).astype(jnp.int32)
    rank = jnp.sum(remote[:, :, None] * earlier[None], axis=1)
    is_own = own[:, :, None] & (inside[:, :, None] == four)
    is_rem = (~own)[:, :, None] & (rank[:, :, None] == four)
    pick = lambda mask, value: jnp.sum(jnp.where(mask, value, 0), axis=1)
    bin_match = bins[:, :, None] == jnp.arange(NBIN, dtype=jnp.int32)[None, None, :]
    taper = jnp.sum(jnp.where(bin_match, taper_table()[None, None, :], 0.0), axis=2)[:, :, None]
    both = jnp.stack([is_own, is_rem])
    first_place = jnp.arange(B_DEV, dtype=jnp.int32)[None, :, None] * K_PART
    place = (jnp.sum(jnp.where(both, k_ids[None], 0), axis=2) + first_place).reshape(-1)
    tapers = jnp.sum(jnp.where(both, taper[None], 0.0), axis=2).reshape(-1)
    slots = pick(is_rem, slot[:, :, None]).reshape(-1)

    rows = BS // samp
    me = lax.axis_index("samp")
    dest = (me + jnp.arange(samp, dtype=jnp.int32)) % samp
    chosen = [select(stage, asked, perturb) for stage in range(STAGES)]
    got = []
    for stage in range(STAGES):
        got.append([exchanged(chosen[stage][i], q) for i, q in enumerate((0, 2, 3))])
    held, _ = lax.optimization_barrier((perturb, chosen[1][0]))
    at, kept, *own_parts = own_tiles(dest, held)
    *own_parts, to_mate, below, across, above = lax.optimization_barrier((*own_parts, chosen[1][3], *got[0]))
    mates = exchanged(to_mate, 1)
    got = [[below, mates, across, above], [got[1][0], mates, got[1][1], got[1][2]]]
    own_parts = [passed_along(part, "samp", d) for d, part in enumerate(own_parts, 1)]
    sums = []
    for stage in range(STAGES):
        parts = list(remote_tiles(stage, slots, dest, at, got[stage], samp))
        if stage == 0:
            parts, own_parts = lax.optimization_barrier((parts, own_parts))
        last = [parts[0]] + [passed_along(parts[d], "samp", d) for d in range(1, samp)]
        if stage == 0:
            dest, *last[1:3] = lax.optimization_barrier((dest, *last[1:3]))
        sums.append(last)

    own_sum = own_total(kept, own_parts)
    out = final(0, place, slots, dest, tapers, own_sum, sums[0], None, rows)
    out = final(1, place, slots, dest, tapers, own_sum, sums[1], out, rows)
    return out.reshape(rows, PAIR_DEV, BS)


def solution(mesh):
    return jax.shard_map(
        body,
        mesh=mesh,
        in_specs=(P("samp", "blk"), P("blk", None), P("blk", None)),
        out_specs=P("samp", "blk", None),
        check_vma=False,
    )
```

```python
import functools

import jax
import jax.numpy as jnp
from jax import lax
from jax.experimental import pallas as pl
from jax.experimental.pallas import tpu as pltpu
from jax.sharding import PartitionSpec as P

BS = 256
B_DEV = 4
K_PART = 8
REACH = 2
NBIN = 32
PAIR_DEV = 32
HALF = 128
STAGES = 2
EXTRA = 8
CODE_EXTRA = 16
TOP = 32766.0
STEPS = 256.0

EPSILON = 1e-06
MIB = 1 << 20
BIG = 58 * MIB


def passed_along(value, axis, steps):
    count = lax.axis_size(axis)
    pairs = [(source, (source + steps) % count) for source in range(count)]
    return lax.ppermute(value, axis, pairs)


def exchanged(value, kind, back=False):
    count = lax.axis_size("blk")
    source_of = (
        lambda i: i - 2,
        lambda i: i ^ 1,
        lambda i: i - 1 if i % 2 == 0 else i + 1,
        lambda i: i + 2,
    )[kind]
    pairs = [(source_of(i) % count, i) for i in range(count)]
    if back:
        pairs = [(b, a) for a, b in pairs]
    return lax.ppermute(value, "blk", sorted(pairs))


def spread(parts):
    one, two, three = parts
    count, half = three.shape[0], two.shape[0] // 2
    down = passed_along(jnp.concatenate([three, two[half:]]), "samp", -1)
    up = passed_along(one, "samp", 1)
    first = passed_along(two[:half], "samp", 2)
    second = passed_along(down[count:], "samp", -1)
    return [up, first, second, down]


def taper_table():
    scaled = 2.0 * (jnp.arange(NBIN, dtype=jnp.float32) + 0.5) / NBIN
    inner = (((-0.25 * scaled + 0.5) * scaled + 0.625) * scaled - 5.0 / 3.0) * scaled * scaled + 1.0
    outer = (
        ((((scaled / 12.0 - 0.5) * scaled + 0.625) * scaled + 5.0 / 3.0) * scaled - 5.0) * scaled
        + 4.0
        - 2.0 / (3.0 * scaled)
    )
    return jnp.where(scaled <= 1.0, inner, outer)


def scale_code(largest):
    return jnp.ceil(jnp.log2(jnp.maximum(largest, 1e-30)) * STEPS)


def encode(tile):
    code = scale_code(jnp.max(jnp.abs(tile), axis=0, keepdims=True))
    scaled = jnp.round(tile * (jnp.exp2(code * (-1.0 / STEPS)) * TOP))
    return jnp.clip(scaled, -TOP, TOP), code


def encode_norm(norm):
    code = scale_code(norm)
    scaled = norm * (jnp.exp2(code * (-1.0 / STEPS)) * TOP)
    high = jnp.round(scaled)
    return [code, high, jnp.round((scaled - high) * TOP)]


def decoded_scale(code):
    return jnp.exp2(code * (1.0 / STEPS)) * (1.0 / TOP)


def select_kernel(plan, want_ref, source_ref, *refs):
    outs, held_ref, in_sems, out_sems = refs[:-3], refs[-3], refs[-2], refs[-1]
    reads, writes = [], []
    for i, (q, side, half, out, column) in enumerate(plan):
        start = pl.multiple_of(want_ref[q * 2 + side] * BS + half * HALF, HALF)
        reads.append(pltpu.make_async_copy(source_ref.at[:, pl.ds(start, HALF)], held_ref.at[i], in_sems.at[i]))
        writes.append(
            pltpu.make_async_copy(held_ref.at[i], outs[out].at[:, pl.ds(column * HALF, HALF)], out_sems.at[i])
        )
    for read in reads:
        read.start()
    for read, write in zip(reads, writes):
        read.wait()
        write.start()
    for write in writes:
        write.wait()


def select(stage, want, perturb):
    samples = perturb.shape[0]
    widths = [2 * HALF] * 3
    plan = [(q, side, stage, out, side) for out, q in enumerate((0, 2, 3)) for side in range(2)]
    if stage == 1:
        plan += [(1, side, half, 3, 2 * half + side) for half in range(2) for side in range(2)]
        widths.append(4 * HALF)
    return pl.pallas_call(
        functools.partial(select_kernel, plan),
        grid_spec=pltpu.PrefetchScalarGridSpec(
            num_scalar_prefetch=1,
            grid=(),
            in_specs=[pl.BlockSpec(memory_space=pl.ANY)],
            out_specs=[pl.BlockSpec(memory_space=pltpu.HBM)] * len(widths),
            scratch_shapes=[
                pltpu.VMEM((len(plan), samples, HALF), perturb.dtype),
                pltpu.SemaphoreType.DMA((len(plan),)),
                pltpu.SemaphoreType.DMA((len(plan),)),
            ],
        ),
        out_shape=[jax.ShapeDtypeStruct((samples, width), perturb.dtype) for width in widths],
        compiler_params=pltpu.CompilerParams(vmem_limit_bytes=BIG),
        cost_estimate=pl.CostEstimate(flops=0, bytes_accessed=MIB * len(plan), transcendentals=0),
    )(want, perturb)


def with_rows(count, width, rows):
    row_id = lax.broadcasted_iota(jnp.int32, (count, width), 0)
    block = jnp.zeros((count, width), jnp.float32)
    for i, row in enumerate(rows):
        block = jnp.where(row_id == i, row, block)
    return block.astype(jnp.int32).astype(jnp.int16)


def own_kernel(dest_ref, x_ref, row_ref, at_ref, *refs):
    parts, tile_ref, norm_ref = refs[:-2], refs[-2], refs[-1]
    samp = len(parts)
    rows = BS // samp
    r = pl.program_id(0)
    at_ref[...] = jnp.transpose(row_ref[...])
    at = at_ref[...]
    codes = [[] for _ in range(samp - 1)]
    for c in range(B_DEV):
        tile_ref[...] = jnp.dot(at, x_ref[:, c * BS : (c + 1) * BS], preferred_element_type=jnp.float32)
        for d in range(samp):
            piece = tile_ref[pl.ds(pl.multiple_of(dest_ref[d] * rows, rows), rows), :]
            if d > 0:
                piece, code = encode(piece)
                piece = piece.astype(jnp.int32).astype(jnp.int16)
                codes[d - 1].append(code)
            parts[d][c * rows : (c + 1) * rows, :] = piece

        @pl.when(r == c)
        def _():
            here = lax.broadcasted_iota(jnp.int32, (BS, BS), 0) == lax.broadcasted_iota(jnp.int32, (BS, BS), 1)
            norm = jnp.sum(jnp.where(here, tile_ref[...], 0.0), axis=0, keepdims=True)
            norm_ref[...] = jnp.broadcast_to(norm, norm_ref.shape)

    parts[0][BS : BS + EXTRA, :] = norm_ref[...]
    norm_codes = encode_norm(norm_ref[0:1, :])
    for d in range(1, samp):
        parts[d][BS : BS + CODE_EXTRA, :] = with_rows(CODE_EXTRA, BS, codes[d - 1] + norm_codes)


def own_tiles(dest, perturb):
    samples, cells = perturb.shape
    samp = dest.shape[0]
    blocks_out = [(BS + EXTRA, jnp.float32)] + [(BS + CODE_EXTRA, jnp.int16)] * (samp - 1)
    return pl.pallas_call(
        own_kernel,
        grid_spec=pltpu.PrefetchScalarGridSpec(
            num_scalar_prefetch=1,
            grid=(B_DEV,),
            in_specs=[
                pl.BlockSpec((samples, cells), lambda r, *s: (0, 0)),
                pl.BlockSpec((samples, BS), lambda r, *s: (0, r)),
            ],
            out_specs=[pl.BlockSpec((BS, samples), lambda r, *s: (r, 0))]
            + [pl.BlockSpec((block, BS), lambda r, *s: (r, 0)) for block, _ in blocks_out],
            scratch_shapes=[pltpu.VMEM((BS, BS), jnp.float32), pltpu.VMEM((EXTRA, BS), jnp.float32)],
        ),
        out_shape=[jax.ShapeDtypeStruct((cells, samples), perturb.dtype)]
        + [jax.ShapeDtypeStruct((B_DEV * block, BS), dtype) for block, dtype in blocks_out],
        compiler_params=pltpu.CompilerParams(vmem_limit_bytes=BIG),
        cost_estimate=pl.CostEstimate(flops=2 * cells * cells * samples, bytes_accessed=12 * MIB, transcendentals=0),
    )(dest, perturb, perturb)


def total_kernel(kept_ref, up_ref, first_ref, second_ref, down_ref, out_ref):
    rows = BS // 4
    block = BS + EXTRA
    coded = BS + CODE_EXTRA
    for r in range(B_DEV):
        middle = (first_ref, r) if r < B_DEV // 2 else (second_ref, r - B_DEV // 2)
        sources = [(up_ref, r), middle, (down_ref, r)]
        extras = [
            ref[at * coded + BS : (at + 1) * coded, :].astype(jnp.int32).astype(jnp.float32) for ref, at in sources
        ]
        for j in range(4):
            here = slice(r * block + j * rows, r * block + (j + 1) * rows)
            tile = kept_ref[here, :]
            for (ref, at), extra in zip(sources, extras):
                piece = ref[at * coded + j * rows : at * coded + (j + 1) * rows, :].astype(jnp.int32)
                tile = tile + piece.astype(jnp.float32) * decoded_scale(extra[j : j + 1, :])
            out_ref[here, :] = tile
        norm = kept_ref[r * block + BS : r * block + BS + 1, :]
        for extra in extras:
            code, high, low = (extra[4 + i : 5 + i, :] for i in range(3))
            norm = norm + (high + low * (1.0 / TOP)) * decoded_scale(code)
        out_ref[r * block + BS : (r + 1) * block, :] = jnp.broadcast_to(norm, (EXTRA, BS))


def own_total(kept, coded):
    return pl.pallas_call(
        total_kernel,
        out_shape=jax.ShapeDtypeStruct(kept.shape, kept.dtype),
        compiler_params=pltpu.CompilerParams(vmem_limit_bytes=16 * MIB),
        cost_estimate=pl.CostEstimate(flops=4 * MIB, bytes_accessed=4 * MIB, transcendentals=0),
    )(kept, *coded)


def remote_kernel(stage, slot_ref, dest_ref, at_ref, *refs):
    blocks, parts, (cols_ref, tile_ref, sems) = refs[:4], refs[4:-3], refs[-3:]
    samp = len(parts)
    samples = cols_ref.shape[1]
    rows = BS // samp
    r = pl.program_id(0)

    @pl.when(r == 0)
    def _():
        copies = []
        for q in range(4):
            for side in range(2):
                column = (2 * stage if q == 1 else 0) + side
                copies.append(
                    pltpu.make_async_copy(
                        blocks[q].at[:, pl.ds(column * HALF, HALF)],
                        cols_ref.at[2 * q + side],
                        sems.at[2 * q + side],
                    )
                )
        for copy in copies:
            copy.start()
        for copy in copies:
            copy.wait()

    at = at_ref[...]
    codes = [[] for _ in range(samp - 1)]
    for pair in range(2):
        u = r * 4 + 2 * pair
        cols = jnp.concatenate([cols_ref[slot_ref[u]], cols_ref[slot_ref[u + 1]]], axis=1)
        tile = jnp.dot(at, cols, preferred_element_type=jnp.float32)
        tile_ref[...] = tile
        for side in range(2):
            j = 2 * pair + side
            for d in range(samp):
                first = pl.multiple_of(dest_ref[d] * rows, rows)
                piece = tile_ref[pl.ds(first, rows), side * HALF : (side + 1) * HALF]
                if d > 0:
                    piece, code = encode(piece)
                    piece = piece.astype(jnp.int32).astype(jnp.int16)
                    codes[d - 1].append(code)
                parts[d][j * rows : (j + 1) * rows, :] = piece

    step, lanes = 256, 32

    def add(i, totals):
        at_rows = pl.ds(pl.multiple_of(i * step, step), step)
        squares = [jnp.square(cols_ref[2 * r + side, at_rows, :].astype(jnp.float32)) for side in range(2)]
        return [
            total + jnp.sum(square.reshape(step // lanes, lanes, HALF), axis=0)
            for total, square in zip(totals, squares)
        ]

    totals = lax.fori_loop(0, samples // step, add, [jnp.zeros((lanes, HALF), jnp.float32)] * 2)
    norm_codes = []
    for side, total in enumerate(totals):
        norm = jnp.sum(total, axis=0, keepdims=True)
        norm_codes += encode_norm(norm)
        parts[0][BS + side * 4 : BS + side * 4 + 4, :] = jnp.broadcast_to(norm, (4, HALF))
    for d in range(1, samp):
        parts[d][BS : BS + CODE_EXTRA, :] = with_rows(CODE_EXTRA, HALF, codes[d - 1] + norm_codes)


def remote_tiles(stage, slots, dest, at, blocks, samp):
    cells, samples = at.shape
    blocks_out = [(BS + EXTRA, jnp.float32)] + [(BS + CODE_EXTRA, jnp.int16)] * (samp - 1)
    out_specs = [pl.BlockSpec((block, HALF), lambda r, *s: (r, 0)) for block, _ in blocks_out]
    out_shape = [jax.ShapeDtypeStruct((B_DEV * block, HALF), dtype) for block, dtype in blocks_out]
    return pl.pallas_call(
        functools.partial(remote_kernel, stage),
        grid_spec=pltpu.PrefetchScalarGridSpec(
            num_scalar_prefetch=2,
            grid=(B_DEV,),
            in_specs=[pl.BlockSpec((BS, samples), lambda r, *s: (r, 0))] + [pl.BlockSpec(memory_space=pl.ANY)] * 4,
            out_specs=out_specs,
            scratch_shapes=[
                pltpu.VMEM((8, samples, HALF), at.dtype),
                pltpu.VMEM((BS, BS), jnp.float32),
                pltpu.SemaphoreType.DMA((8,)),
            ],
        ),
        out_shape=out_shape,
        compiler_params=pltpu.CompilerParams(vmem_limit_bytes=BIG),
        cost_estimate=pl.CostEstimate(flops=2 * cells * cells * samples, bytes_accessed=10 * MIB, transcendentals=0),
    )(slots, dest, at, *blocks)


def final_kernel(half, place_ref, slot_ref, dest_ref, taper_ref, own_ref, kept_ref, *refs):
    coded_refs, out_ref, norm_ref = refs[:3], refs[-2], refs[-1]
    rows = out_ref.shape[0] // PAIR_DEV
    first = dest_ref[0] * rows
    cols = slice(half * HALF, (half + 1) * HALF)
    lane = lax.broadcasted_iota(jnp.int32, (rows, BS), 1)
    row = lax.broadcasted_iota(jnp.int32, (rows, BS), 0)
    mine = lane == row + first
    block = BS + EXTRA
    coded = BS + CODE_EXTRA
    extras = []
    for r in range(B_DEV):
        extras.append(
            [ref[r * coded + BS : (r + 1) * coded, :].astype(jnp.int32).astype(jnp.float32) for ref in coded_refs]
        )
        for side in range(2):
            norm = kept_ref[r * block + BS + side * 4 : r * block + BS + side * 4 + 1, :]
            for extra in extras[r]:
                code, high, low = (extra[4 + 3 * side + i : 5 + 3 * side + i, :] for i in range(3))
                norm = norm + (high + low * (1.0 / TOP)) * decoded_scale(code)
            norm_ref[2 * r + side : 2 * r + side + 1, :] = norm
    for r in range(B_DEV):
        base = r * block
        row_norm = own_ref[base + BS : base + BS + 1, :]
        row_norm = jnp.sum(jnp.where(mine, row_norm, 0.0), axis=1, keepdims=True)
        row_scale = jnp.broadcast_to(lax.rsqrt(row_norm + EPSILON), (rows, HALF))
        for j in range(4):
            u = r * 4 + j
            norm = own_ref[j * block + BS : j * block + BS + 1, cols]
            col_scale = taper_ref[u] * lax.rsqrt(norm + EPSILON)
            tile = own_ref[base + j * rows : base + (j + 1) * rows, cols]
            out_ref[pl.ds(place_ref[u], rows, stride=PAIR_DEV), :] = tile * row_scale * col_scale
        for j in range(4):
            u = r * 4 + j
            norm = norm_ref[pl.ds(slot_ref[u], 1), :]
            col_scale = taper_ref[16 + u] * lax.rsqrt(norm + EPSILON)
            tile = kept_ref[base + j * rows : base + (j + 1) * rows, :]
            for ref, extra in zip(coded_refs, extras[r]):
                piece = ref[r * coded + j * rows : r * coded + (j + 1) * rows, :].astype(jnp.int32).astype(jnp.float32)
                tile = tile + piece * decoded_scale(extra[j : j + 1, :])
            out_ref[pl.ds(place_ref[16 + u], rows, stride=PAIR_DEV), :] = tile * row_scale * col_scale


def final(half, place, slots, dest, tapers, own, rems, out, rows):
    full = lambda shape: pl.BlockSpec(shape, lambda i, *s: (0,) * len(shape))
    before = [] if out is None else [out]
    return pl.pallas_call(
        functools.partial(final_kernel, half),
        grid_spec=pltpu.PrefetchScalarGridSpec(
            num_scalar_prefetch=4,
            grid=(1,),
            in_specs=[full(own.shape)]
            + [full(rem.shape) for rem in rems]
            + [pl.BlockSpec(memory_space=pl.ANY)] * len(before),
            out_specs=pl.BlockSpec((rows * PAIR_DEV, HALF), lambda i, *s: (0, half)),
            scratch_shapes=[pltpu.VMEM((8, HALF), jnp.float32)],
        ),
        out_shape=jax.ShapeDtypeStruct((rows * PAIR_DEV, BS), jnp.float32),
        input_output_aliases={5 + len(rems): 0} if before else {},
        cost_estimate=pl.CostEstimate(flops=MIB, bytes_accessed=4 * MIB, transcendentals=0),
    )(place, slots, dest, tapers, own, *rems, *before)


def body(perturb, partner, bins):
    blk_count = lax.axis_size("blk")
    samp = lax.axis_size("samp")
    here = lax.axis_index("blk")
    owner = partner // B_DEV
    inside = partner % B_DEV
    offset = (owner - here + blk_count + REACH) % blk_count - REACH
    mate = 1 - 2 * (here % 2)
    kind = jnp.where(offset == -2, 0, jnp.where(offset == 2, 3, jnp.where(offset == mate, 1, 2)))
    own = offset == 0
    kind = jnp.where(own, -1, kind)
    four = jnp.arange(4, dtype=jnp.int32)
    hit = (kind.reshape(1, 1, -1) == four[:, None, None]) & (inside.reshape(1, 1, -1) == four[None, :, None])
    need = jnp.any(hit, axis=2)
    low = jnp.min(jnp.where(need, four[None], B_DEV - 1), axis=1)
    high = jnp.max(jnp.where(need, four[None], 0), axis=1)
    want = jnp.stack([low, high], axis=1)
    asked = jnp.concatenate([exchanged(want[q], q, back=True) for q in range(4)])

    k_ids = jnp.arange(K_PART, dtype=jnp.int32)[None, :, None]
    is_high = jnp.sum(jnp.where(kind[:, :, None] == four, high[None, None], 0), axis=2) == inside
    slot = 2 * kind + is_high.astype(jnp.int32)
    remote = (~own).astype(jnp.int32)
    earlier = (jnp.arange(K_PART)[:, None] < jnp.arange(K_PART)[None, :]).astype(jnp.int32)
    rank = jnp.sum(remote[:, :, None] * earlier[None], axis=1)
    is_own = own[:, :, None] & (inside[:, :, None] == four)
    is_rem = (~own)[:, :, None] & (rank[:, :, None] == four)
    pick = lambda mask, value: jnp.sum(jnp.where(mask, value, 0), axis=1)
    bin_match = bins[:, :, None] == jnp.arange(NBIN, dtype=jnp.int32)[None, None, :]
    taper = jnp.sum(jnp.where(bin_match, taper_table()[None, None, :], 0.0), axis=2)[:, :, None]
    both = jnp.stack([is_own, is_rem])
    first_place = jnp.arange(B_DEV, dtype=jnp.int32)[None, :, None] * K_PART
    place = (jnp.sum(jnp.where(both, k_ids[None], 0), axis=2) + first_place).reshape(-1)
    tapers = jnp.sum(jnp.where(both, taper[None], 0.0), axis=2).reshape(-1)
    slots = pick(is_rem, slot[:, :, None]).reshape(-1)

    rows = BS // samp
    me = lax.axis_index("samp")
    dest = (me + jnp.arange(samp, dtype=jnp.int32)) % samp
    chosen = [select(stage, asked, perturb) for stage in range(STAGES)]
    got = []
    for stage in range(STAGES):
        got.append([exchanged(chosen[stage][i], q) for i, q in enumerate((0, 2, 3))])
    held, _ = lax.optimization_barrier((perturb, chosen[1][0]))
    at, kept, *own_parts = own_tiles(dest, held)
    *own_parts, to_mate, below, across, above = lax.optimization_barrier((*own_parts, chosen[1][3], *got[0]))
    mates = exchanged(to_mate, 1)
    got = [[below, mates, across, above], [got[1][0], mates, got[1][1], got[1][2]]]
    own_parts = spread(own_parts)
    sums = []
    for stage in range(STAGES):
        parts = list(remote_tiles(stage, slots, dest, at, got[stage], samp))
        if stage == 0:
            parts, own_parts = lax.optimization_barrier((parts, own_parts))
        last = [parts[0]] + [passed_along(parts[d], "samp", d) for d in range(1, samp)]
        if stage == 0:
            dest, last[1] = lax.optimization_barrier((dest, last[1]))
        sums.append(last)

    own_sum = own_total(kept, own_parts)
    out = final(0, place, slots, dest, tapers, own_sum, sums[0], None, rows)
    out = final(1, place, slots, dest, tapers, own_sum, sums[1], out, rows)
    return out.reshape(rows, PAIR_DEV, BS)


def solution(mesh):
    return jax.shard_map(
        body,
        mesh=mesh,
        in_specs=(P("samp", "blk"), P("blk", None), P("blk", None)),
        out_specs=P("samp", "blk", None),
        check_vma=False,
    )
```

```python
import functools

import jax
import jax.numpy as jnp
from jax import lax
from jax.experimental import pallas as pl
from jax.experimental.pallas import tpu as pltpu
from jax.sharding import PartitionSpec as P

BS = 256
B_DEV = 4
K_PART = 8
REACH = 2
NBIN = 32
PAIR_DEV = 32
HALF = 128
STAGES = 2
EXTRA = 8
CODE_EXTRA = 16
TOP = 32766.0
STEPS = 256.0

EPSILON = 1e-06
MIB = 1 << 20
BIG = 58 * MIB


def passed_along(value, axis, steps):
    count = lax.axis_size(axis)
    pairs = [(source, (source + steps) % count) for source in range(count)]
    return lax.ppermute(value, axis, pairs)


def exchanged(value, kind, back=False):
    count = lax.axis_size("blk")
    source_of = (
        lambda i: i - 2,
        lambda i: i ^ 1,
        lambda i: i - 1 if i % 2 == 0 else i + 1,
        lambda i: i + 2,
    )[kind]
    pairs = [(source_of(i) % count, i) for i in range(count)]
    if back:
        pairs = [(b, a) for a, b in pairs]
    return lax.ppermute(value, "blk", sorted(pairs))


def spread(parts):
    one, two, three = parts
    count, half = three.shape[0], two.shape[0] // 2
    down = passed_along(jnp.concatenate([three, two[half:]]), "samp", -1)
    up = passed_along(one, "samp", 1)
    first = passed_along(two[:half], "samp", 2)
    second = passed_along(down[count:], "samp", -1)
    return [up, first, second, down]


def taper_table():
    scaled = 2.0 * (jnp.arange(NBIN, dtype=jnp.float32) + 0.5) / NBIN
    inner = (((-0.25 * scaled + 0.5) * scaled + 0.625) * scaled - 5.0 / 3.0) * scaled * scaled + 1.0
    outer = (
        ((((scaled / 12.0 - 0.5) * scaled + 0.625) * scaled + 5.0 / 3.0) * scaled - 5.0) * scaled
        + 4.0
        - 2.0 / (3.0 * scaled)
    )
    return jnp.where(scaled <= 1.0, inner, outer)


def scale_code(largest):
    return jnp.ceil(jnp.log2(jnp.maximum(largest, 1e-30)) * STEPS)


def encode(tile):
    code = scale_code(jnp.max(jnp.abs(tile), axis=0, keepdims=True))
    scaled = jnp.round(tile * (jnp.exp2(code * (-1.0 / STEPS)) * TOP))
    return jnp.clip(scaled, -TOP, TOP), code


def encode_norm(norm):
    code = scale_code(norm)
    scaled = norm * (jnp.exp2(code * (-1.0 / STEPS)) * TOP)
    high = jnp.round(scaled)
    return [code, high, jnp.round((scaled - high) * TOP)]


def decoded_scale(code):
    return jnp.exp2(code * (1.0 / STEPS)) * (1.0 / TOP)


def select_kernel(plan, want_ref, source_ref, *refs):
    outs, held_ref, in_sems, out_sems = refs[:-3], refs[-3], refs[-2], refs[-1]
    reads, writes = [], []
    for i, (q, side, half, out, column) in enumerate(plan):
        start = pl.multiple_of(want_ref[q * 2 + side] * BS + half * HALF, HALF)
        reads.append(pltpu.make_async_copy(source_ref.at[:, pl.ds(start, HALF)], held_ref.at[i], in_sems.at[i]))
        writes.append(
            pltpu.make_async_copy(held_ref.at[i], outs[out].at[:, pl.ds(column * HALF, HALF)], out_sems.at[i])
        )
    for read in reads:
        read.start()
    for read, write in zip(reads, writes):
        read.wait()
        write.start()
    for write in writes:
        write.wait()


def select(stage, want, perturb):
    samples = perturb.shape[0]
    widths = [2 * HALF] * 3
    plan = [(q, side, stage, out, side) for out, q in enumerate((0, 2, 3)) for side in range(2)]
    return pl.pallas_call(
        functools.partial(select_kernel, plan),
        grid_spec=pltpu.PrefetchScalarGridSpec(
            num_scalar_prefetch=1,
            grid=(),
            in_specs=[pl.BlockSpec(memory_space=pl.ANY)],
            out_specs=[pl.BlockSpec(memory_space=pltpu.HBM)] * len(widths),
            scratch_shapes=[
                pltpu.VMEM((len(plan), samples, HALF), perturb.dtype),
                pltpu.SemaphoreType.DMA((len(plan),)),
                pltpu.SemaphoreType.DMA((len(plan),)),
            ],
        ),
        out_shape=[jax.ShapeDtypeStruct((samples, width), perturb.dtype) for width in widths],
        compiler_params=pltpu.CompilerParams(vmem_limit_bytes=BIG),
        cost_estimate=pl.CostEstimate(flops=0, bytes_accessed=MIB * len(plan), transcendentals=0),
    )(want, perturb)


def with_rows(count, width, rows):
    row_id = lax.broadcasted_iota(jnp.int32, (count, width), 0)
    block = jnp.zeros((count, width), jnp.float32)
    for i, row in enumerate(rows):
        block = jnp.where(row_id == i, row, block)
    return block.astype(jnp.int32).astype(jnp.int16)


def own_kernel(dest_ref, x_ref, row_ref, at_ref, *refs):
    parts, tile_ref, norm_ref = refs[:-2], refs[-2], refs[-1]
    samp = len(parts)
    rows = BS // samp
    r = pl.program_id(0)
    at_ref[...] = jnp.transpose(row_ref[...])
    at = at_ref[...]
    codes = [[] for _ in range(samp - 1)]
    for c in range(B_DEV):
        tile_ref[...] = jnp.dot(at, x_ref[:, c * BS : (c + 1) * BS], preferred_element_type=jnp.float32)
        for d in range(samp):
            piece = tile_ref[pl.ds(pl.multiple_of(dest_ref[d] * rows, rows), rows), :]
            if d > 0:
                piece, code = encode(piece)
                piece = piece.astype(jnp.int32).astype(jnp.int16)
                codes[d - 1].append(code)
            parts[d][c * rows : (c + 1) * rows, :] = piece

        @pl.when(r == c)
        def _():
            here = lax.broadcasted_iota(jnp.int32, (BS, BS), 0) == lax.broadcasted_iota(jnp.int32, (BS, BS), 1)
            norm = jnp.sum(jnp.where(here, tile_ref[...], 0.0), axis=0, keepdims=True)
            norm_ref[...] = jnp.broadcast_to(norm, norm_ref.shape)

    parts[0][BS : BS + EXTRA, :] = norm_ref[...]
    norm_codes = encode_norm(norm_ref[0:1, :])
    for d in range(1, samp):
        parts[d][BS : BS + CODE_EXTRA, :] = with_rows(CODE_EXTRA, BS, codes[d - 1] + norm_codes)


def own_tiles(dest, perturb):
    samples, cells = perturb.shape
    samp = dest.shape[0]
    blocks_out = [(BS + EXTRA, jnp.float32)] + [(BS + CODE_EXTRA, jnp.int16)] * (samp - 1)
    return pl.pallas_call(
        own_kernel,
        grid_spec=pltpu.PrefetchScalarGridSpec(
            num_scalar_prefetch=1,
            grid=(B_DEV,),
            in_specs=[
                pl.BlockSpec((samples, cells), lambda r, *s: (0, 0)),
                pl.BlockSpec((samples, BS), lambda r, *s: (0, r)),
            ],
            out_specs=[pl.BlockSpec((BS, samples), lambda r, *s: (r, 0))]
            + [pl.BlockSpec((block, BS), lambda r, *s: (r, 0)) for block, _ in blocks_out],
            scratch_shapes=[pltpu.VMEM((BS, BS), jnp.float32), pltpu.VMEM((EXTRA, BS), jnp.float32)],
        ),
        out_shape=[jax.ShapeDtypeStruct((cells, samples), perturb.dtype)]
        + [jax.ShapeDtypeStruct((B_DEV * block, BS), dtype) for block, dtype in blocks_out],
        compiler_params=pltpu.CompilerParams(vmem_limit_bytes=BIG),
        cost_estimate=pl.CostEstimate(flops=2 * cells * cells * samples, bytes_accessed=12 * MIB, transcendentals=0),
    )(dest, perturb, perturb)


def total_kernel(kept_ref, up_ref, first_ref, second_ref, down_ref, out_ref):
    rows = BS // 4
    block = BS + EXTRA
    coded = BS + CODE_EXTRA
    for r in range(B_DEV):
        middle = (first_ref, r) if r < B_DEV // 2 else (second_ref, r - B_DEV // 2)
        sources = [(up_ref, r), middle, (down_ref, r)]
        extras = [
            ref[at * coded + BS : (at + 1) * coded, :].astype(jnp.int32).astype(jnp.float32) for ref, at in sources
        ]
        for j in range(4):
            here = slice(r * block + j * rows, r * block + (j + 1) * rows)
            tile = kept_ref[here, :]
            for (ref, at), extra in zip(sources, extras):
                piece = ref[at * coded + j * rows : at * coded + (j + 1) * rows, :].astype(jnp.int32)
                tile = tile + piece.astype(jnp.float32) * decoded_scale(extra[j : j + 1, :])
            out_ref[here, :] = tile
        norm = kept_ref[r * block + BS : r * block + BS + 1, :]
        for extra in extras:
            code, high, low = (extra[4 + i : 5 + i, :] for i in range(3))
            norm = norm + (high + low * (1.0 / TOP)) * decoded_scale(code)
        out_ref[r * block + BS : (r + 1) * block, :] = jnp.broadcast_to(norm, (EXTRA, BS))


def own_total(kept, coded):
    return pl.pallas_call(
        total_kernel,
        out_shape=jax.ShapeDtypeStruct(kept.shape, kept.dtype),
        compiler_params=pltpu.CompilerParams(vmem_limit_bytes=16 * MIB),
        cost_estimate=pl.CostEstimate(flops=4 * MIB, bytes_accessed=4 * MIB, transcendentals=0),
    )(kept, *coded)


def remote_kernel(stage, slot_ref, dest_ref, mate_ref, at_ref, *refs):
    blocks, parts, (cols_ref, tile_ref, sems) = refs[:4], refs[4:-3], refs[-3:]
    samp = len(parts)
    samples = cols_ref.shape[1]
    rows = BS // samp
    r = pl.program_id(0)

    @pl.when(r == 0)
    def _():
        copies = []
        for q in range(4):
            for side in range(2):
                start = pl.multiple_of(mate_ref[side] * BS + stage * HALF, HALF) if q == 1 else side * HALF
                copies.append(
                    pltpu.make_async_copy(
                        blocks[q].at[:, pl.ds(start, HALF)],
                        cols_ref.at[2 * q + side],
                        sems.at[2 * q + side],
                    )
                )
        for copy in copies:
            copy.start()
        for copy in copies:
            copy.wait()

    at = at_ref[...]
    codes = [[] for _ in range(samp - 1)]
    for pair in range(2):
        u = r * 4 + 2 * pair
        cols = jnp.concatenate([cols_ref[slot_ref[u]], cols_ref[slot_ref[u + 1]]], axis=1)
        tile = jnp.dot(at, cols, preferred_element_type=jnp.float32)
        tile_ref[...] = tile
        for side in range(2):
            j = 2 * pair + side
            for d in range(samp):
                first = pl.multiple_of(dest_ref[d] * rows, rows)
                piece = tile_ref[pl.ds(first, rows), side * HALF : (side + 1) * HALF]
                if d > 0:
                    piece, code = encode(piece)
                    piece = piece.astype(jnp.int32).astype(jnp.int16)
                    codes[d - 1].append(code)
                parts[d][j * rows : (j + 1) * rows, :] = piece

    step, lanes = 256, 32

    def add(i, totals):
        at_rows = pl.ds(pl.multiple_of(i * step, step), step)
        squares = [jnp.square(cols_ref[2 * r + side, at_rows, :].astype(jnp.float32)) for side in range(2)]
        return [
            total + jnp.sum(square.reshape(step // lanes, lanes, HALF), axis=0)
            for total, square in zip(totals, squares)
        ]

    totals = lax.fori_loop(0, samples // step, add, [jnp.zeros((lanes, HALF), jnp.float32)] * 2)
    norm_codes = []
    for side, total in enumerate(totals):
        norm = jnp.sum(total, axis=0, keepdims=True)
        norm_codes += encode_norm(norm)
        parts[0][BS + side * 4 : BS + side * 4 + 4, :] = jnp.broadcast_to(norm, (4, HALF))
    for d in range(1, samp):
        parts[d][BS : BS + CODE_EXTRA, :] = with_rows(CODE_EXTRA, HALF, codes[d - 1] + norm_codes)


def remote_tiles(stage, slots, dest, mate_blocks, at, blocks, samp):
    cells, samples = at.shape
    blocks_out = [(BS + EXTRA, jnp.float32)] + [(BS + CODE_EXTRA, jnp.int16)] * (samp - 1)
    out_specs = [pl.BlockSpec((block, HALF), lambda r, *s: (r, 0)) for block, _ in blocks_out]
    out_shape = [jax.ShapeDtypeStruct((B_DEV * block, HALF), dtype) for block, dtype in blocks_out]
    return pl.pallas_call(
        functools.partial(remote_kernel, stage),
        grid_spec=pltpu.PrefetchScalarGridSpec(
            num_scalar_prefetch=3,
            grid=(B_DEV,),
            in_specs=[pl.BlockSpec((BS, samples), lambda r, *s: (r, 0))] + [pl.BlockSpec(memory_space=pl.ANY)] * 4,
            out_specs=out_specs,
            scratch_shapes=[
                pltpu.VMEM((8, samples, HALF), at.dtype),
                pltpu.VMEM((BS, BS), jnp.float32),
                pltpu.SemaphoreType.DMA((8,)),
            ],
        ),
        out_shape=out_shape,
        compiler_params=pltpu.CompilerParams(vmem_limit_bytes=BIG),
        cost_estimate=pl.CostEstimate(flops=2 * cells * cells * samples, bytes_accessed=10 * MIB, transcendentals=0),
    )(slots, dest, mate_blocks, at, *blocks)


def final_kernel(half, place_ref, slot_ref, dest_ref, taper_ref, own_ref, kept_ref, *refs):
    coded_refs, out_ref, norm_ref = refs[:3], refs[-2], refs[-1]
    rows = out_ref.shape[0] // PAIR_DEV
    first = dest_ref[0] * rows
    cols = slice(half * HALF, (half + 1) * HALF)
    lane = lax.broadcasted_iota(jnp.int32, (rows, BS), 1)
    row = lax.broadcasted_iota(jnp.int32, (rows, BS), 0)
    mine = lane == row + first
    block = BS + EXTRA
    coded = BS + CODE_EXTRA
    extras = []
    for r in range(B_DEV):
        extras.append(
            [ref[r * coded + BS : (r + 1) * coded, :].astype(jnp.int32).astype(jnp.float32) for ref in coded_refs]
        )
        for side in range(2):
            norm = kept_ref[r * block + BS + side * 4 : r * block + BS + side * 4 + 1, :]
            for extra in extras[r]:
                code, high, low = (extra[4 + 3 * side + i : 5 + 3 * side + i, :] for i in range(3))
                norm = norm + (high + low * (1.0 / TOP)) * decoded_scale(code)
            norm_ref[2 * r + side : 2 * r + side + 1, :] = norm
    for r in range(B_DEV):
        base = r * block
        row_norm = own_ref[base + BS : base + BS + 1, :]
        row_norm = jnp.sum(jnp.where(mine, row_norm, 0.0), axis=1, keepdims=True)
        row_scale = jnp.broadcast_to(lax.rsqrt(row_norm + EPSILON), (rows, HALF))
        for j in range(4):
            u = r * 4 + j
            norm = own_ref[j * block + BS : j * block + BS + 1, cols]
            col_scale = taper_ref[u] * lax.rsqrt(norm + EPSILON)
            tile = own_ref[base + j * rows : base + (j + 1) * rows, cols]
            out_ref[pl.ds(place_ref[u], rows, stride=PAIR_DEV), :] = tile * row_scale * col_scale
        for j in range(4):
            u = r * 4 + j
            norm = norm_ref[pl.ds(slot_ref[u], 1), :]
            col_scale = taper_ref[16 + u] * lax.rsqrt(norm + EPSILON)
            tile = kept_ref[base + j * rows : base + (j + 1) * rows, :]
            for ref, extra in zip(coded_refs, extras[r]):
                piece = ref[r * coded + j * rows : r * coded + (j + 1) * rows, :].astype(jnp.int32).astype(jnp.float32)
                tile = tile + piece * decoded_scale(extra[j : j + 1, :])
            out_ref[pl.ds(place_ref[16 + u], rows, stride=PAIR_DEV), :] = tile * row_scale * col_scale


def final(half, place, slots, dest, tapers, own, rems, out, rows):
    full = lambda shape: pl.BlockSpec(shape, lambda i, *s: (0,) * len(shape))
    before = [] if out is None else [out]
    return pl.pallas_call(
        functools.partial(final_kernel, half),
        grid_spec=pltpu.PrefetchScalarGridSpec(
            num_scalar_prefetch=4,
            grid=(1,),
            in_specs=[full(own.shape)]
            + [full(rem.shape) for rem in rems]
            + [pl.BlockSpec(memory_space=pl.ANY)] * len(before),
            out_specs=pl.BlockSpec((rows * PAIR_DEV, HALF), lambda i, *s: (0, half)),
            scratch_shapes=[pltpu.VMEM((8, HALF), jnp.float32)],
        ),
        out_shape=jax.ShapeDtypeStruct((rows * PAIR_DEV, BS), jnp.float32),
        input_output_aliases={5 + len(rems): 0} if before else {},
        cost_estimate=pl.CostEstimate(flops=MIB, bytes_accessed=4 * MIB, transcendentals=0),
    )(place, slots, dest, tapers, own, *rems, *before)


def body(perturb, partner, bins):
    blk_count = lax.axis_size("blk")
    samp = lax.axis_size("samp")
    here = lax.axis_index("blk")
    owner = partner // B_DEV
    inside = partner % B_DEV
    offset = (owner - here + blk_count + REACH) % blk_count - REACH
    mate = 1 - 2 * (here % 2)
    kind = jnp.where(offset == -2, 0, jnp.where(offset == 2, 3, jnp.where(offset == mate, 1, 2)))
    own = offset == 0
    kind = jnp.where(own, -1, kind)
    four = jnp.arange(4, dtype=jnp.int32)
    hit = (kind.reshape(1, 1, -1) == four[:, None, None]) & (inside.reshape(1, 1, -1) == four[None, :, None])
    need = jnp.any(hit, axis=2)
    low = jnp.min(jnp.where(need, four[None], B_DEV - 1), axis=1)
    high = jnp.max(jnp.where(need, four[None], 0), axis=1)
    want = jnp.stack([low, high], axis=1)
    mates = exchanged(perturb, 1)
    asked = jnp.concatenate([exchanged(want[q], q, back=True) for q in range(4)])

    k_ids = jnp.arange(K_PART, dtype=jnp.int32)[None, :, None]
    is_high = jnp.sum(jnp.where(kind[:, :, None] == four, high[None, None], 0), axis=2) == inside
    slot = 2 * kind + is_high.astype(jnp.int32)
    remote = (~own).astype(jnp.int32)
    earlier = (jnp.arange(K_PART)[:, None] < jnp.arange(K_PART)[None, :]).astype(jnp.int32)
    rank = jnp.sum(remote[:, :, None] * earlier[None], axis=1)
    is_own = own[:, :, None] & (inside[:, :, None] == four)
    is_rem = (~own)[:, :, None] & (rank[:, :, None] == four)
    pick = lambda mask, value: jnp.sum(jnp.where(mask, value, 0), axis=1)
    bin_match = bins[:, :, None] == jnp.arange(NBIN, dtype=jnp.int32)[None, None, :]
    taper = jnp.sum(jnp.where(bin_match, taper_table()[None, None, :], 0.0), axis=2)[:, :, None]
    both = jnp.stack([is_own, is_rem])
    first_place = jnp.arange(B_DEV, dtype=jnp.int32)[None, :, None] * K_PART
    place = (jnp.sum(jnp.where(both, k_ids[None], 0), axis=2) + first_place).reshape(-1)
    tapers = jnp.sum(jnp.where(both, taper[None], 0.0), axis=2).reshape(-1)
    slots = pick(is_rem, slot[:, :, None]).reshape(-1)

    rows = BS // samp
    me = lax.axis_index("samp")
    dest = (me + jnp.arange(samp, dtype=jnp.int32)) % samp
    chosen = [select(stage, asked, perturb) for stage in range(STAGES)]
    got = []
    for stage in range(STAGES):
        got.append([exchanged(chosen[stage][i], q) for i, q in enumerate((0, 2, 3))])
    held, _, mates = lax.optimization_barrier((perturb, chosen[1][0], mates))
    at, kept, *own_parts = own_tiles(dest, held)
    *own_parts, below, across, above = lax.optimization_barrier((*own_parts, *got[0]))
    got = [[below, mates, across, above], [got[1][0], mates, got[1][1], got[1][2]]]
    own_parts = spread(own_parts)
    sums = []
    for stage in range(STAGES):
        parts = list(remote_tiles(stage, slots, dest, want[1], at, got[stage], samp))
        if stage == 0:
            parts, own_parts = lax.optimization_barrier((parts, own_parts))
        last = [parts[0]] + [passed_along(parts[d], "samp", d) for d in range(1, samp)]
        if stage == 0:
            dest, last[1] = lax.optimization_barrier((dest, last[1]))
        sums.append(last)

    own_sum = own_total(kept, own_parts)
    out = final(0, place, slots, dest, tapers, own_sum, sums[0], None, rows)
    out = final(1, place, slots, dest, tapers, own_sum, sums[1], out, rows)
    return out.reshape(rows, PAIR_DEV, BS)


def solution(mesh):
    return jax.shard_map(
        body,
        mesh=mesh,
        in_specs=(P("samp", "blk"), P("blk", None), P("blk", None)),
        out_specs=P("samp", "blk", None),
        check_vma=False,
    )
```

```python
import functools

import jax
import jax.numpy as jnp
from jax import lax
from jax.experimental import pallas as pl
from jax.experimental.pallas import tpu as pltpu
from jax.sharding import PartitionSpec as P

BS = 256
B_DEV = 4
K_PART = 8
REACH = 2
NBIN = 32
PAIR_DEV = 32
HALF = 128
STAGES = 2
EXTRA = 8
CODE_EXTRA = 16
TOP = 32766.0
STEPS = 256.0

EPSILON = 1e-06
MIB = 1 << 20
BIG = 58 * MIB


def passed_along(value, axis, steps):
    count = lax.axis_size(axis)
    pairs = [(source, (source + steps) % count) for source in range(count)]
    return lax.ppermute(value, axis, pairs)


def exchanged(value, kind, back=False):
    count = lax.axis_size("blk")
    source_of = (
        lambda i: i - 2,
        lambda i: i ^ 1,
        lambda i: i - 1 if i % 2 == 0 else i + 1,
        lambda i: i + 2,
    )[kind]
    pairs = [(source_of(i) % count, i) for i in range(count)]
    if back:
        pairs = [(b, a) for a, b in pairs]
    return lax.ppermute(value, "blk", sorted(pairs))


def spread(parts):
    up, first, down = parts
    down = passed_along(down, "samp", -1)
    up = passed_along(up, "samp", 1)
    first = passed_along(first, "samp", 2)
    second = passed_along(down[up.shape[0] :], "samp", -1)
    return [up, first, second, down]


def taper_table():
    scaled = 2.0 * (jnp.arange(NBIN, dtype=jnp.float32) + 0.5) / NBIN
    inner = (((-0.25 * scaled + 0.5) * scaled + 0.625) * scaled - 5.0 / 3.0) * scaled * scaled + 1.0
    outer = (
        ((((scaled / 12.0 - 0.5) * scaled + 0.625) * scaled + 5.0 / 3.0) * scaled - 5.0) * scaled
        + 4.0
        - 2.0 / (3.0 * scaled)
    )
    return jnp.where(scaled <= 1.0, inner, outer)


def scale_code(largest):
    return jnp.ceil(jnp.log2(jnp.maximum(largest, 1e-30)) * STEPS)


def encode(tile):
    code = scale_code(jnp.max(jnp.abs(tile), axis=0, keepdims=True))
    scaled = jnp.round(tile * (jnp.exp2(code * (-1.0 / STEPS)) * TOP))
    return jnp.clip(scaled, -TOP, TOP), code


def encode_norm(norm):
    code = scale_code(norm)
    scaled = norm * (jnp.exp2(code * (-1.0 / STEPS)) * TOP)
    high = jnp.round(scaled)
    return [code, high, jnp.round((scaled - high) * TOP)]


def decoded_scale(code):
    return jnp.exp2(code * (1.0 / STEPS)) * (1.0 / TOP)


def select_kernel(plan, want_ref, source_ref, *refs):
    outs, held_ref, in_sems, out_sems = refs[:-3], refs[-3], refs[-2], refs[-1]
    reads, writes = [], []
    for i, (q, side, half, out, column) in enumerate(plan):
        start = pl.multiple_of(want_ref[q * 2 + side] * BS + half * HALF, HALF)
        reads.append(pltpu.make_async_copy(source_ref.at[:, pl.ds(start, HALF)], held_ref.at[i], in_sems.at[i]))
        writes.append(
            pltpu.make_async_copy(held_ref.at[i], outs[out].at[:, pl.ds(column * HALF, HALF)], out_sems.at[i])
        )
    for read in reads:
        read.start()
    for read, write in zip(reads, writes):
        read.wait()
        write.start()
    for write in writes:
        write.wait()


def select(stage, want, perturb):
    samples = perturb.shape[0]
    widths = [2 * HALF] * 3
    plan = [(out, side, stage, out, side) for out in range(3) for side in range(2)]
    return pl.pallas_call(
        functools.partial(select_kernel, plan),
        grid_spec=pltpu.PrefetchScalarGridSpec(
            num_scalar_prefetch=1,
            grid=(),
            in_specs=[pl.BlockSpec(memory_space=pl.ANY)],
            out_specs=[pl.BlockSpec(memory_space=pltpu.HBM)] * len(widths),
            scratch_shapes=[
                pltpu.VMEM((len(plan), samples, HALF), perturb.dtype),
                pltpu.SemaphoreType.DMA((len(plan),)),
                pltpu.SemaphoreType.DMA((len(plan),)),
            ],
        ),
        out_shape=[jax.ShapeDtypeStruct((samples, width), perturb.dtype) for width in widths],
        compiler_params=pltpu.CompilerParams(vmem_limit_bytes=BIG),
        cost_estimate=pl.CostEstimate(flops=0, bytes_accessed=MIB * len(plan), transcendentals=0),
    )(want, perturb)


def with_rows(count, width, rows):
    row_id = lax.broadcasted_iota(jnp.int32, (count, width), 0)
    block = jnp.zeros((count, width), jnp.float32)
    for i, row in enumerate(rows):
        block = jnp.where(row_id == i, row, block)
    return block.astype(jnp.int32).astype(jnp.int16)


def own_kernel(dest_ref, x_ref, row_ref, at_ref, kept_ref, up_ref, first_ref, down_ref, tile_ref, norm_ref):
    rows = BS // 4
    coded = BS + CODE_EXTRA
    r = pl.program_id(0)
    half = B_DEV // 2
    at_ref[...] = jnp.transpose(row_ref[...])
    at = at_ref[...]

    def store(d, start, value):
        size = value.shape[0]
        base = pl.multiple_of(r * coded, 16) + start
        if d == 1:
            up_ref[pl.ds(base, size), :] = value
        elif d == 3:
            down_ref[pl.ds(base, size), :] = value
        else:

            @pl.when(r < half)
            def _():
                first_ref[pl.ds(base, size), :] = value

            @pl.when(r >= half)
            def _():
                down_ref[pl.ds(base + half * coded, size), :] = value

    codes = [[] for _ in range(3)]
    for c in range(B_DEV):
        tile_ref[...] = jnp.dot(at, x_ref[:, c * BS : (c + 1) * BS], preferred_element_type=jnp.float32)
        for d in range(4):
            piece = tile_ref[pl.ds(pl.multiple_of(dest_ref[d] * rows, rows), rows), :]
            if d == 0:
                kept_ref[c * rows : (c + 1) * rows, :] = piece
                continue
            piece, code = encode(piece)
            codes[d - 1].append(code)
            store(d, c * rows, piece.astype(jnp.int32).astype(jnp.int16))

        @pl.when(r == c)
        def _():
            here = lax.broadcasted_iota(jnp.int32, (BS, BS), 0) == lax.broadcasted_iota(jnp.int32, (BS, BS), 1)
            norm = jnp.sum(jnp.where(here, tile_ref[...], 0.0), axis=0, keepdims=True)
            norm_ref[...] = jnp.broadcast_to(norm, norm_ref.shape)

    kept_ref[BS : BS + EXTRA, :] = norm_ref[...]
    norm_codes = encode_norm(norm_ref[0:1, :])
    for d in range(1, 4):
        store(d, BS, with_rows(CODE_EXTRA, BS, codes[d - 1] + norm_codes))


def own_tiles(dest, perturb):
    samples, cells = perturb.shape
    coded = BS + CODE_EXTRA
    counts = [B_DEV * coded, B_DEV // 2 * coded, (B_DEV + B_DEV // 2) * coded]
    return pl.pallas_call(
        own_kernel,
        grid_spec=pltpu.PrefetchScalarGridSpec(
            num_scalar_prefetch=1,
            grid=(B_DEV,),
            in_specs=[
                pl.BlockSpec((samples, cells), lambda r, *s: (0, 0)),
                pl.BlockSpec((samples, BS), lambda r, *s: (0, r)),
            ],
            out_specs=[
                pl.BlockSpec((BS, samples), lambda r, *s: (r, 0)),
                pl.BlockSpec((BS + EXTRA, BS), lambda r, *s: (r, 0)),
            ]
            + [pl.BlockSpec((count, BS), lambda r, *s: (0, 0)) for count in counts],
            scratch_shapes=[pltpu.VMEM((BS, BS), jnp.float32), pltpu.VMEM((EXTRA, BS), jnp.float32)],
        ),
        out_shape=[
            jax.ShapeDtypeStruct((cells, samples), perturb.dtype),
            jax.ShapeDtypeStruct((B_DEV * (BS + EXTRA), BS), jnp.float32),
        ]
        + [jax.ShapeDtypeStruct((count, BS), jnp.int16) for count in counts],
        compiler_params=pltpu.CompilerParams(vmem_limit_bytes=BIG),
        cost_estimate=pl.CostEstimate(flops=2 * cells * cells * samples, bytes_accessed=12 * MIB, transcendentals=0),
    )(dest, perturb, perturb)


def total_kernel(kept_ref, up_ref, first_ref, second_ref, down_ref, out_ref):
    rows = BS // 4
    block = BS + EXTRA
    coded = BS + CODE_EXTRA
    for r in range(B_DEV):
        middle = (first_ref, r) if r < B_DEV // 2 else (second_ref, r - B_DEV // 2)
        sources = [(up_ref, r), middle, (down_ref, r)]
        extras = [
            ref[at * coded + BS : (at + 1) * coded, :].astype(jnp.int32).astype(jnp.float32) for ref, at in sources
        ]
        for j in range(4):
            here = slice(r * block + j * rows, r * block + (j + 1) * rows)
            tile = kept_ref[here, :]
            for (ref, at), extra in zip(sources, extras):
                piece = ref[at * coded + j * rows : at * coded + (j + 1) * rows, :].astype(jnp.int32)
                tile = tile + piece.astype(jnp.float32) * decoded_scale(extra[j : j + 1, :])
            out_ref[here, :] = tile
        norm = kept_ref[r * block + BS : r * block + BS + 1, :]
        for extra in extras:
            code, high, low = (extra[4 + i : 5 + i, :] for i in range(3))
            norm = norm + (high + low * (1.0 / TOP)) * decoded_scale(code)
        out_ref[r * block + BS : (r + 1) * block, :] = jnp.broadcast_to(norm, (EXTRA, BS))


def own_total(kept, coded):
    return pl.pallas_call(
        total_kernel,
        out_shape=jax.ShapeDtypeStruct(kept.shape, kept.dtype),
        compiler_params=pltpu.CompilerParams(vmem_limit_bytes=16 * MIB),
        cost_estimate=pl.CostEstimate(flops=4 * MIB, bytes_accessed=4 * MIB, transcendentals=0),
    )(kept, *coded)


def remote_kernel(stage, slot_ref, dest_ref, mate_ref, at_ref, *refs):
    blocks, parts, (cols_ref, tile_ref, sems) = refs[:4], refs[4:-3], refs[-3:]
    samp = len(parts)
    samples = cols_ref.shape[1]
    rows = BS // samp
    r = pl.program_id(0)

    @pl.when(r == 0)
    def _():
        copies = []
        for q in range(4):
            for side in range(2):
                start = pl.multiple_of(mate_ref[side] * BS + stage * HALF, HALF) if q == 1 else side * HALF
                copies.append(
                    pltpu.make_async_copy(
                        blocks[q].at[:, pl.ds(start, HALF)],
                        cols_ref.at[2 * q + side],
                        sems.at[2 * q + side],
                    )
                )
        for copy in copies:
            copy.start()
        for copy in copies:
            copy.wait()

    at = at_ref[...]
    codes = [[] for _ in range(samp - 1)]
    for pair in range(2):
        u = r * 4 + 2 * pair
        cols = jnp.concatenate([cols_ref[slot_ref[u]], cols_ref[slot_ref[u + 1]]], axis=1)
        tile = jnp.dot(at, cols, preferred_element_type=jnp.float32)
        tile_ref[...] = tile
        for side in range(2):
            j = 2 * pair + side
            for d in range(samp):
                first = pl.multiple_of(dest_ref[d] * rows, rows)
                piece = tile_ref[pl.ds(first, rows), side * HALF : (side + 1) * HALF]
                if d > 0:
                    piece, code = encode(piece)
                    piece = piece.astype(jnp.int32).astype(jnp.int16)
                    codes[d - 1].append(code)
                parts[d][j * rows : (j + 1) * rows, :] = piece

    step, lanes = 256, 32

    def add(i, totals):
        at_rows = pl.ds(pl.multiple_of(i * step, step), step)
        squares = [jnp.square(cols_ref[2 * r + side, at_rows, :].astype(jnp.float32)) for side in range(2)]
        return [
            total + jnp.sum(square.reshape(step // lanes, lanes, HALF), axis=0)
            for total, square in zip(totals, squares)
        ]

    totals = lax.fori_loop(0, samples // step, add, [jnp.zeros((lanes, HALF), jnp.float32)] * 2)
    norm_codes = []
    for side, total in enumerate(totals):
        norm = jnp.sum(total, axis=0, keepdims=True)
        norm_codes += encode_norm(norm)
        parts[0][BS + side * 4 : BS + side * 4 + 4, :] = jnp.broadcast_to(norm, (4, HALF))
    for d in range(1, samp):
        parts[d][BS : BS + CODE_EXTRA, :] = with_rows(CODE_EXTRA, HALF, codes[d - 1] + norm_codes)


def remote_tiles(stage, slots, dest, mate_blocks, at, blocks, samp):
    cells, samples = at.shape
    blocks_out = [(BS + EXTRA, jnp.float32)] + [(BS + CODE_EXTRA, jnp.int16)] * (samp - 1)
    out_specs = [pl.BlockSpec((block, HALF), lambda r, *s: (r, 0)) for block, _ in blocks_out]
    out_shape = [jax.ShapeDtypeStruct((B_DEV * block, HALF), dtype) for block, dtype in blocks_out]
    return pl.pallas_call(
        functools.partial(remote_kernel, stage),
        grid_spec=pltpu.PrefetchScalarGridSpec(
            num_scalar_prefetch=3,
            grid=(B_DEV,),
            in_specs=[pl.BlockSpec((BS, samples), lambda r, *s: (r, 0))] + [pl.BlockSpec(memory_space=pl.ANY)] * 4,
            out_specs=out_specs,
            scratch_shapes=[
                pltpu.VMEM((8, samples, HALF), at.dtype),
                pltpu.VMEM((BS, BS), jnp.float32),
                pltpu.SemaphoreType.DMA((8,)),
            ],
        ),
        out_shape=out_shape,
        compiler_params=pltpu.CompilerParams(vmem_limit_bytes=BIG),
        cost_estimate=pl.CostEstimate(flops=2 * cells * cells * samples, bytes_accessed=10 * MIB, transcendentals=0),
    )(slots, dest, mate_blocks, at, *blocks)


def final_kernel(half, place_ref, slot_ref, dest_ref, taper_ref, own_ref, kept_ref, *refs):
    coded_refs, out_ref, norm_ref = refs[:3], refs[-2], refs[-1]
    rows = out_ref.shape[0] // PAIR_DEV
    first = dest_ref[0] * rows
    cols = slice(half * HALF, (half + 1) * HALF)
    lane = lax.broadcasted_iota(jnp.int32, (rows, BS), 1)
    row = lax.broadcasted_iota(jnp.int32, (rows, BS), 0)
    mine = lane == row + first
    block = BS + EXTRA
    coded = BS + CODE_EXTRA
    extras = []
    for r in range(B_DEV):
        extras.append(
            [ref[r * coded + BS : (r + 1) * coded, :].astype(jnp.int32).astype(jnp.float32) for ref in coded_refs]
        )
        for side in range(2):
            norm = kept_ref[r * block + BS + side * 4 : r * block + BS + side * 4 + 1, :]
            for extra in extras[r]:
                code, high, low = (extra[4 + 3 * side + i : 5 + 3 * side + i, :] for i in range(3))
                norm = norm + (high + low * (1.0 / TOP)) * decoded_scale(code)
            norm_ref[2 * r + side : 2 * r + side + 1, :] = norm
    for r in range(B_DEV):
        base = r * block
        row_norm = own_ref[base + BS : base + BS + 1, :]
        row_norm = jnp.sum(jnp.where(mine, row_norm, 0.0), axis=1, keepdims=True)
        row_scale = jnp.broadcast_to(lax.rsqrt(row_norm + EPSILON), (rows, HALF))
        for j in range(4):
            u = r * 4 + j
            norm = own_ref[j * block + BS : j * block + BS + 1, cols]
            col_scale = taper_ref[u] * lax.rsqrt(norm + EPSILON)
            tile = own_ref[base + j * rows : base + (j + 1) * rows, cols]
            out_ref[pl.ds(place_ref[u], rows, stride=PAIR_DEV), :] = tile * row_scale * col_scale
        for j in range(4):
            u = r * 4 + j
            norm = norm_ref[pl.ds(slot_ref[u], 1), :]
            col_scale = taper_ref[16 + u] * lax.rsqrt(norm + EPSILON)
            tile = kept_ref[base + j * rows : base + (j + 1) * rows, :]
            for ref, extra in zip(coded_refs, extras[r]):
                piece = ref[r * coded + j * rows : r * coded + (j + 1) * rows, :].astype(jnp.int32).astype(jnp.float32)
                tile = tile + piece * decoded_scale(extra[j : j + 1, :])
            out_ref[pl.ds(place_ref[16 + u], rows, stride=PAIR_DEV), :] = tile * row_scale * col_scale


def final(half, place, slots, dest, tapers, own, rems, out, rows):
    full = lambda shape: pl.BlockSpec(shape, lambda i, *s: (0,) * len(shape))
    before = [] if out is None else [out]
    return pl.pallas_call(
        functools.partial(final_kernel, half),
        grid_spec=pltpu.PrefetchScalarGridSpec(
            num_scalar_prefetch=4,
            grid=(1,),
            in_specs=[full(own.shape)]
            + [full(rem.shape) for rem in rems]
            + [pl.BlockSpec(memory_space=pl.ANY)] * len(before),
            out_specs=pl.BlockSpec((rows * PAIR_DEV, HALF), lambda i, *s: (0, half)),
            scratch_shapes=[pltpu.VMEM((8, HALF), jnp.float32)],
        ),
        out_shape=jax.ShapeDtypeStruct((rows * PAIR_DEV, BS), jnp.float32),
        input_output_aliases={5 + len(rems): 0} if before else {},
        cost_estimate=pl.CostEstimate(flops=MIB, bytes_accessed=4 * MIB, transcendentals=0),
    )(place, slots, dest, tapers, own, *rems, *before)


def body(perturb, partner, bins):
    blk_count = lax.axis_size("blk")
    samp = lax.axis_size("samp")
    here = lax.axis_index("blk")
    owner = partner // B_DEV
    inside = partner % B_DEV
    offset = (owner - here + blk_count + REACH) % blk_count - REACH
    mate = 1 - 2 * (here % 2)
    kind = jnp.where(offset == -2, 0, jnp.where(offset == 2, 3, jnp.where(offset == mate, 1, 2)))
    own = offset == 0
    kind = jnp.where(own, -1, kind)
    four = jnp.arange(4, dtype=jnp.int32)
    hit = (kind.reshape(1, 1, -1) == four[:, None, None]) & (inside.reshape(1, 1, -1) == four[None, :, None])
    need = jnp.any(hit, axis=2)
    low = jnp.min(jnp.where(need, four[None], B_DEV - 1), axis=1)
    high = jnp.max(jnp.where(need, four[None], 0), axis=1)
    want = jnp.stack([low, high], axis=1)
    mates = exchanged(perturb, 1)
    asked = jnp.concatenate([exchanged(want[q], q, back=True) for q in (0, 2, 3)])

    k_ids = jnp.arange(K_PART, dtype=jnp.int32)[None, :, None]
    is_high = jnp.sum(jnp.where(kind[:, :, None] == four, high[None, None], 0), axis=2) == inside
    slot = 2 * kind + is_high.astype(jnp.int32)
    remote = (~own).astype(jnp.int32)
    earlier = (jnp.arange(K_PART)[:, None] < jnp.arange(K_PART)[None, :]).astype(jnp.int32)
    rank = jnp.sum(remote[:, :, None] * earlier[None], axis=1)
    is_own = own[:, :, None] & (inside[:, :, None] == four)
    is_rem = (~own)[:, :, None] & (rank[:, :, None] == four)
    pick = lambda mask, value: jnp.sum(jnp.where(mask, value, 0), axis=1)
    bin_match = bins[:, :, None] == jnp.arange(NBIN, dtype=jnp.int32)[None, None, :]
    taper = jnp.sum(jnp.where(bin_match, taper_table()[None, None, :], 0.0), axis=2)[:, :, None]
    both = jnp.stack([is_own, is_rem])
    first_place = jnp.arange(B_DEV, dtype=jnp.int32)[None, :, None] * K_PART
    place = (jnp.sum(jnp.where(both, k_ids[None], 0), axis=2) + first_place).reshape(-1)
    tapers = jnp.sum(jnp.where(both, taper[None], 0.0), axis=2).reshape(-1)
    slots = pick(is_rem, slot[:, :, None]).reshape(-1)

    rows = BS // samp
    me = lax.axis_index("samp")
    dest = (me + jnp.arange(samp, dtype=jnp.int32)) % samp
    chosen = [select(stage, asked, perturb) for stage in range(STAGES)]
    got = []
    for stage in range(STAGES):
        got.append([exchanged(chosen[stage][i], q) for i, q in enumerate((0, 2, 3))])
    held, _, mates = lax.optimization_barrier((perturb, chosen[1][0], mates))
    at, kept, *own_parts = own_tiles(dest, held)
    *own_parts, below, across, above = lax.optimization_barrier((*own_parts, *got[0]))
    got = [[below, mates, across, above], [got[1][0], mates, got[1][1], got[1][2]]]
    own_parts = spread(own_parts)
    sums = []
    for stage in range(STAGES):
        parts = list(remote_tiles(stage, slots, dest, want[1], at, got[stage], samp))
        if stage == 0:
            parts, own_parts = lax.optimization_barrier((parts, own_parts))
        last = [parts[0]] + [passed_along(parts[d], "samp", d) for d in range(1, samp)]
        if stage == 0:
            dest, last[1] = lax.optimization_barrier((dest, last[1]))
        sums.append(last)

    own_sum = own_total(kept, own_parts)
    out = final(0, place, slots, dest, tapers, own_sum, sums[0], None, rows)
    out = final(1, place, slots, dest, tapers, own_sum, sums[1], out, rows)
    return out.reshape(rows, PAIR_DEV, BS)


def solution(mesh):
    return jax.shard_map(
        body,
        mesh=mesh,
        in_specs=(P("samp", "blk"), P("blk", None), P("blk", None)),
        out_specs=P("samp", "blk", None),
        check_vma=False,
    )
```

```python
import functools

import jax
import jax.numpy as jnp
from jax import lax
from jax.experimental import pallas as pl
from jax.experimental.pallas import tpu as pltpu
from jax.sharding import PartitionSpec as P

BS = 256
B_DEV = 4
K_PART = 8
REACH = 2
NBIN = 32
PAIR_DEV = 32
HALF = 128
STAGES = 2
EXTRA = 8
CODE_EXTRA = 16
TOP = 32766.0
STEPS = 256.0

EPSILON = 1e-06
MIB = 1 << 20
BIG = 58 * MIB


def passed_along(value, axis, steps):
    count = lax.axis_size(axis)
    pairs = [(source, (source + steps) % count) for source in range(count)]
    return lax.ppermute(value, axis, pairs)


def exchanged(value, kind, back=False):
    count = lax.axis_size("blk")
    source_of = (
        lambda i: i - 2,
        lambda i: i ^ 1,
        lambda i: i - 1 if i % 2 == 0 else i + 1,
        lambda i: i + 2,
    )[kind]
    pairs = [(source_of(i) % count, i) for i in range(count)]
    if back:
        pairs = [(b, a) for a, b in pairs]
    return lax.ppermute(value, "blk", sorted(pairs))


def spread(parts):
    up, first, down = parts
    down = passed_along(down, "samp", -1)
    up = passed_along(up, "samp", 1)
    first = passed_along(first, "samp", 2)
    second = passed_along(down[up.shape[0] :], "samp", -1)
    return [up, first, second, down]


def taper_table():
    scaled = 2.0 * (jnp.arange(NBIN, dtype=jnp.float32) + 0.5) / NBIN
    inner = (((-0.25 * scaled + 0.5) * scaled + 0.625) * scaled - 5.0 / 3.0) * scaled * scaled + 1.0
    outer = (
        ((((scaled / 12.0 - 0.5) * scaled + 0.625) * scaled + 5.0 / 3.0) * scaled - 5.0) * scaled
        + 4.0
        - 2.0 / (3.0 * scaled)
    )
    return jnp.where(scaled <= 1.0, inner, outer)


def scale_code(largest):
    return jnp.ceil(jnp.log2(jnp.maximum(largest, 1e-30)) * STEPS)


def encode(tile):
    code = scale_code(jnp.max(jnp.abs(tile), axis=0, keepdims=True))
    scaled = jnp.round(tile * (jnp.exp2(code * (-1.0 / STEPS)) * TOP))
    return jnp.clip(scaled, -TOP, TOP), code


def encode_norm(norm):
    code = scale_code(norm)
    scaled = norm * (jnp.exp2(code * (-1.0 / STEPS)) * TOP)
    high = jnp.round(scaled)
    return [code, high, jnp.round((scaled - high) * TOP)]


def decoded_scale(code):
    return jnp.exp2(code * (1.0 / STEPS)) * (1.0 / TOP)


def select_kernel(plan, want_ref, source_ref, *refs):
    outs, held_ref, in_sems, out_sems = refs[:-3], refs[-3], refs[-2], refs[-1]
    reads, writes = [], []
    for i, (q, side, half, out, column) in enumerate(plan):
        start = pl.multiple_of(want_ref[q * 2 + side] * BS + half * HALF, HALF)
        reads.append(pltpu.make_async_copy(source_ref.at[:, pl.ds(start, HALF)], held_ref.at[i], in_sems.at[i]))
        writes.append(
            pltpu.make_async_copy(held_ref.at[i], outs[out].at[:, pl.ds(column * HALF, HALF)], out_sems.at[i])
        )
    for read in reads:
        read.start()
    for read, write in zip(reads, writes):
        read.wait()
        write.start()
    for write in writes:
        write.wait()


def select(stage, want, perturb):
    samples = perturb.shape[0]
    widths = [2 * HALF] * 3
    plan = [(out, side, stage, out, side) for out in range(3) for side in range(2)]
    return pl.pallas_call(
        functools.partial(select_kernel, plan),
        grid_spec=pltpu.PrefetchScalarGridSpec(
            num_scalar_prefetch=1,
            grid=(),
            in_specs=[pl.BlockSpec(memory_space=pl.ANY)],
            out_specs=[pl.BlockSpec(memory_space=pltpu.HBM)] * len(widths),
            scratch_shapes=[
                pltpu.VMEM((len(plan), samples, HALF), perturb.dtype),
                pltpu.SemaphoreType.DMA((len(plan),)),
                pltpu.SemaphoreType.DMA((len(plan),)),
            ],
        ),
        out_shape=[jax.ShapeDtypeStruct((samples, width), perturb.dtype) for width in widths],
        compiler_params=pltpu.CompilerParams(vmem_limit_bytes=BIG),
        cost_estimate=pl.CostEstimate(flops=0, bytes_accessed=MIB * len(plan), transcendentals=0),
    )(want, perturb)


def with_rows(count, width, rows):
    row_id = lax.broadcasted_iota(jnp.int32, (count, width), 0)
    block = jnp.zeros((count, width), jnp.float32)
    for i, row in enumerate(rows):
        block = jnp.where(row_id == i, row, block)
    return block.astype(jnp.int32).astype(jnp.int16)


def own_kernel(dest_ref, x_ref, row_ref, at_ref, kept_ref, up_ref, first_ref, down_ref, tile_ref, norm_ref):
    rows = BS // 4
    coded = BS + CODE_EXTRA
    r = pl.program_id(0)
    half = B_DEV // 2
    at_ref[...] = jnp.transpose(row_ref[...])
    at = at_ref[...]

    def store(d, start, value):
        size = value.shape[0]
        base = pl.multiple_of(r * coded, 16) + start
        if d == 1:
            up_ref[pl.ds(base, size), :] = value
        elif d == 3:
            down_ref[pl.ds(base, size), :] = value
        else:

            @pl.when(r < half)
            def _():
                first_ref[pl.ds(base, size), :] = value

            @pl.when(r >= half)
            def _():
                down_ref[pl.ds(base + half * coded, size), :] = value

    codes = [[] for _ in range(3)]
    for c in range(B_DEV):
        tile_ref[...] = jnp.dot(at, x_ref[:, c * BS : (c + 1) * BS], preferred_element_type=jnp.float32)
        for d in range(4):
            piece = tile_ref[pl.ds(pl.multiple_of(dest_ref[d] * rows, rows), rows), :]
            if d == 0:
                kept_ref[c * rows : (c + 1) * rows, :] = piece
                continue
            piece, code = encode(piece)
            codes[d - 1].append(code)
            store(d, c * rows, piece.astype(jnp.int32).astype(jnp.int16))

        @pl.when(r == c)
        def _():
            here = lax.broadcasted_iota(jnp.int32, (BS, BS), 0) == lax.broadcasted_iota(jnp.int32, (BS, BS), 1)
            norm = jnp.sum(jnp.where(here, tile_ref[...], 0.0), axis=0, keepdims=True)
            norm_ref[...] = jnp.broadcast_to(norm, norm_ref.shape)

    kept_ref[BS : BS + EXTRA, :] = norm_ref[...]
    norm_codes = encode_norm(norm_ref[0:1, :])
    for d in range(1, 4):
        store(d, BS, with_rows(CODE_EXTRA, BS, codes[d - 1] + norm_codes))


def own_tiles(dest, perturb):
    samples, cells = perturb.shape
    coded = BS + CODE_EXTRA
    counts = [B_DEV * coded, B_DEV // 2 * coded, (B_DEV + B_DEV // 2) * coded]
    return pl.pallas_call(
        own_kernel,
        grid_spec=pltpu.PrefetchScalarGridSpec(
            num_scalar_prefetch=1,
            grid=(B_DEV,),
            in_specs=[
                pl.BlockSpec((samples, cells), lambda r, *s: (0, 0)),
                pl.BlockSpec((samples, BS), lambda r, *s: (0, r)),
            ],
            out_specs=[
                pl.BlockSpec((BS, samples), lambda r, *s: (r, 0)),
                pl.BlockSpec((BS + EXTRA, BS), lambda r, *s: (r, 0)),
            ]
            + [pl.BlockSpec((count, BS), lambda r, *s: (0, 0)) for count in counts],
            scratch_shapes=[pltpu.VMEM((BS, BS), jnp.float32), pltpu.VMEM((EXTRA, BS), jnp.float32)],
        ),
        out_shape=[
            jax.ShapeDtypeStruct((cells, samples), perturb.dtype),
            jax.ShapeDtypeStruct((B_DEV * (BS + EXTRA), BS), jnp.float32),
        ]
        + [jax.ShapeDtypeStruct((count, BS), jnp.int16) for count in counts],
        compiler_params=pltpu.CompilerParams(vmem_limit_bytes=BIG),
        cost_estimate=pl.CostEstimate(flops=2 * cells * cells * samples, bytes_accessed=12 * MIB, transcendentals=0),
    )(dest, perturb, perturb)


def total_kernel(kept_ref, up_ref, first_ref, second_ref, down_ref, out_ref):
    rows = BS // 4
    block = BS + EXTRA
    coded = BS + CODE_EXTRA
    for r in range(B_DEV):
        middle = (first_ref, r) if r < B_DEV // 2 else (second_ref, r - B_DEV // 2)
        sources = [(up_ref, r), middle, (down_ref, r)]
        extras = [
            ref[at * coded + BS : (at + 1) * coded, :].astype(jnp.int32).astype(jnp.float32) for ref, at in sources
        ]
        for j in range(4):
            here = slice(r * block + j * rows, r * block + (j + 1) * rows)
            tile = kept_ref[here, :]
            for (ref, at), extra in zip(sources, extras):
                piece = ref[at * coded + j * rows : at * coded + (j + 1) * rows, :].astype(jnp.int32)
                tile = tile + piece.astype(jnp.float32) * decoded_scale(extra[j : j + 1, :])
            out_ref[here, :] = tile
        norm = kept_ref[r * block + BS : r * block + BS + 1, :]
        for extra in extras:
            code, high, low = (extra[4 + i : 5 + i, :] for i in range(3))
            norm = norm + (high + low * (1.0 / TOP)) * decoded_scale(code)
        out_ref[r * block + BS : (r + 1) * block, :] = jnp.broadcast_to(norm, (EXTRA, BS))


def own_total(kept, coded):
    return pl.pallas_call(
        total_kernel,
        out_shape=jax.ShapeDtypeStruct(kept.shape, kept.dtype),
        compiler_params=pltpu.CompilerParams(vmem_limit_bytes=16 * MIB),
        cost_estimate=pl.CostEstimate(flops=4 * MIB, bytes_accessed=4 * MIB, transcendentals=0),
    )(kept, *coded)


def remote_kernel(stage, slot_ref, dest_ref, mate_ref, at_ref, *refs):
    blocks, parts, (cols_ref, tile_ref, norm_ref, sems) = refs[:4], refs[4:-4], refs[-4:]
    samp = len(parts)
    samples = cols_ref.shape[1]
    rows = BS // samp
    r = pl.program_id(0)

    @pl.when(r == 0)
    def _():
        copies = []
        for q in range(4):
            for side in range(2):
                start = pl.multiple_of(mate_ref[side] * BS + stage * HALF, HALF) if q == 1 else side * HALF
                copies.append(
                    pltpu.make_async_copy(
                        blocks[q].at[:, pl.ds(start, HALF)],
                        cols_ref.at[2 * q + side],
                        sems.at[2 * q + side],
                    )
                )
        for copy in copies:
            copy.start()
        step, lanes = 256, 32
        for slot, copy in enumerate(copies):
            copy.wait()

            def add(i, total):
                x = cols_ref[slot, pl.ds(pl.multiple_of(i * step, step), step), :].astype(jnp.float32)
                return total + jnp.sum(jnp.square(x).reshape(step // lanes, lanes, HALF), axis=0)

            total = lax.fori_loop(0, samples // step, add, jnp.zeros((lanes, HALF), jnp.float32))
            norm_ref[slot // 2, slot % 2 : slot % 2 + 1, :] = jnp.sum(total, axis=0, keepdims=True)

    at = at_ref[...]
    codes = [[] for _ in range(samp - 1)]
    for pair in range(2):
        u = r * 4 + 2 * pair
        cols = jnp.concatenate([cols_ref[slot_ref[u]], cols_ref[slot_ref[u + 1]]], axis=1)
        tile = jnp.dot(at, cols, preferred_element_type=jnp.float32)
        tile_ref[...] = tile
        for side in range(2):
            j = 2 * pair + side
            for d in range(samp):
                first = pl.multiple_of(dest_ref[d] * rows, rows)
                piece = tile_ref[pl.ds(first, rows), side * HALF : (side + 1) * HALF]
                if d > 0:
                    piece, code = encode(piece)
                    piece = piece.astype(jnp.int32).astype(jnp.int16)
                    codes[d - 1].append(code)
                parts[d][j * rows : (j + 1) * rows, :] = piece

    norms = norm_ref[r]
    norm_codes = []
    for side in range(2):
        norm = norms[side : side + 1, :]
        norm_codes += encode_norm(norm)
        parts[0][BS + side * 4 : BS + side * 4 + 4, :] = jnp.broadcast_to(norm, (4, HALF))
    for d in range(1, samp):
        parts[d][BS : BS + CODE_EXTRA, :] = with_rows(CODE_EXTRA, HALF, codes[d - 1] + norm_codes)


def remote_tiles(stage, slots, dest, mate_blocks, at, blocks, samp):
    cells, samples = at.shape
    blocks_out = [(BS + EXTRA, jnp.float32)] + [(BS + CODE_EXTRA, jnp.int16)] * (samp - 1)
    out_specs = [pl.BlockSpec((block, HALF), lambda r, *s: (r, 0)) for block, _ in blocks_out]
    out_shape = [jax.ShapeDtypeStruct((B_DEV * block, HALF), dtype) for block, dtype in blocks_out]
    return pl.pallas_call(
        functools.partial(remote_kernel, stage),
        grid_spec=pltpu.PrefetchScalarGridSpec(
            num_scalar_prefetch=3,
            grid=(B_DEV,),
            in_specs=[pl.BlockSpec((BS, samples), lambda r, *s: (r, 0))] + [pl.BlockSpec(memory_space=pl.ANY)] * 4,
            out_specs=out_specs,
            scratch_shapes=[
                pltpu.VMEM((8, samples, HALF), at.dtype),
                pltpu.VMEM((BS, BS), jnp.float32),
                pltpu.VMEM((B_DEV, 8, HALF), jnp.float32),
                pltpu.SemaphoreType.DMA((8,)),
            ],
        ),
        out_shape=out_shape,
        compiler_params=pltpu.CompilerParams(vmem_limit_bytes=BIG),
        cost_estimate=pl.CostEstimate(flops=2 * cells * cells * samples, bytes_accessed=10 * MIB, transcendentals=0),
    )(slots, dest, mate_blocks, at, *blocks)


def final_kernel(half, place_ref, slot_ref, dest_ref, taper_ref, own_ref, kept_ref, *refs):
    coded_refs, out_ref, norm_ref = refs[:3], refs[-2], refs[-1]
    rows = out_ref.shape[0] // PAIR_DEV
    first = dest_ref[0] * rows
    cols = slice(half * HALF, (half + 1) * HALF)
    lane = lax.broadcasted_iota(jnp.int32, (rows, BS), 1)
    row = lax.broadcasted_iota(jnp.int32, (rows, BS), 0)
    mine = lane == row + first
    block = BS + EXTRA
    coded = BS + CODE_EXTRA
    extras = []
    for r in range(B_DEV):
        extras.append(
            [ref[r * coded + BS : (r + 1) * coded, :].astype(jnp.int32).astype(jnp.float32) for ref in coded_refs]
        )
        for side in range(2):
            norm = kept_ref[r * block + BS + side * 4 : r * block + BS + side * 4 + 1, :]
            for extra in extras[r]:
                code, high, low = (extra[4 + 3 * side + i : 5 + 3 * side + i, :] for i in range(3))
                norm = norm + (high + low * (1.0 / TOP)) * decoded_scale(code)
            norm_ref[2 * r + side : 2 * r + side + 1, :] = norm
    for r in range(B_DEV):
        base = r * block
        row_norm = own_ref[base + BS : base + BS + 1, :]
        row_norm = jnp.sum(jnp.where(mine, row_norm, 0.0), axis=1, keepdims=True)
        row_scale = jnp.broadcast_to(lax.rsqrt(row_norm + EPSILON), (rows, HALF))
        for j in range(4):
            u = r * 4 + j
            norm = own_ref[j * block + BS : j * block + BS + 1, cols]
            col_scale = taper_ref[u] * lax.rsqrt(norm + EPSILON)
            tile = own_ref[base + j * rows : base + (j + 1) * rows, cols]
            out_ref[pl.ds(place_ref[u], rows, stride=PAIR_DEV), :] = tile * row_scale * col_scale
        for j in range(4):
            u = r * 4 + j
            norm = norm_ref[pl.ds(slot_ref[u], 1), :]
            col_scale = taper_ref[16 + u] * lax.rsqrt(norm + EPSILON)
            tile = kept_ref[base + j * rows : base + (j + 1) * rows, :]
            for ref, extra in zip(coded_refs, extras[r]):
                piece = ref[r * coded + j * rows : r * coded + (j + 1) * rows, :].astype(jnp.int32).astype(jnp.float32)
                tile = tile + piece * decoded_scale(extra[j : j + 1, :])
            out_ref[pl.ds(place_ref[16 + u], rows, stride=PAIR_DEV), :] = tile * row_scale * col_scale


def final(half, place, slots, dest, tapers, own, rems, out, rows):
    before = [] if out is None else [out]
    return pl.pallas_call(
        functools.partial(final_kernel, half),
        grid_spec=pltpu.PrefetchScalarGridSpec(
            num_scalar_prefetch=4,
            grid=(1,),
            in_specs=[pl.BlockSpec(memory_space=pltpu.VMEM)] * (1 + len(rems))
            + [pl.BlockSpec(memory_space=pl.ANY)] * len(before),
            out_specs=pl.BlockSpec((rows * PAIR_DEV, HALF), lambda i, *s: (0, half)),
            scratch_shapes=[pltpu.VMEM((8, HALF), jnp.float32)],
        ),
        out_shape=jax.ShapeDtypeStruct((rows * PAIR_DEV, BS), jnp.float32),
        compiler_params=pltpu.CompilerParams(vmem_limit_bytes=16 * MIB),
        input_output_aliases={5 + len(rems): 0} if before else {},
        cost_estimate=pl.CostEstimate(flops=MIB, bytes_accessed=4 * MIB, transcendentals=0),
    )(place, slots, dest, tapers, own, *rems, *before)


def body(perturb, partner, bins):
    blk_count = lax.axis_size("blk")
    samp = lax.axis_size("samp")
    here = lax.axis_index("blk")
    owner = partner // B_DEV
    inside = partner % B_DEV
    offset = (owner - here + blk_count + REACH) % blk_count - REACH
    mate = 1 - 2 * (here % 2)
    kind = jnp.where(offset == -2, 0, jnp.where(offset == 2, 3, jnp.where(offset == mate, 1, 2)))
    own = offset == 0
    kind = jnp.where(own, -1, kind)
    four = jnp.arange(4, dtype=jnp.int32)
    hit = (kind.reshape(1, 1, -1) == four[:, None, None]) & (inside.reshape(1, 1, -1) == four[None, :, None])
    need = jnp.any(hit, axis=2)
    low = jnp.min(jnp.where(need, four[None], B_DEV - 1), axis=1)
    high = jnp.max(jnp.where(need, four[None], 0), axis=1)
    want = jnp.stack([low, high], axis=1)
    mates = exchanged(perturb, 1)
    asked = jnp.concatenate([exchanged(want[q], q, back=True) for q in (0, 2, 3)])

    k_ids = jnp.arange(K_PART, dtype=jnp.int32)[None, :, None]
    is_high = jnp.sum(jnp.where(kind[:, :, None] == four, high[None, None], 0), axis=2) == inside
    slot = 2 * kind + is_high.astype(jnp.int32)
    remote = (~own).astype(jnp.int32)
    earlier = (jnp.arange(K_PART)[:, None] < jnp.arange(K_PART)[None, :]).astype(jnp.int32)
    rank = jnp.sum(remote[:, :, None] * earlier[None], axis=1)
    is_own = own[:, :, None] & (inside[:, :, None] == four)
    is_rem = (~own)[:, :, None] & (rank[:, :, None] == four)
    pick = lambda mask, value: jnp.sum(jnp.where(mask, value, 0), axis=1)
    bin_match = bins[:, :, None] == jnp.arange(NBIN, dtype=jnp.int32)[None, None, :]
    taper = jnp.sum(jnp.where(bin_match, taper_table()[None, None, :], 0.0), axis=2)[:, :, None]
    both = jnp.stack([is_own, is_rem])
    first_place = jnp.arange(B_DEV, dtype=jnp.int32)[None, :, None] * K_PART
    place = (jnp.sum(jnp.where(both, k_ids[None], 0), axis=2) + first_place).reshape(-1)
    tapers = jnp.sum(jnp.where(both, taper[None], 0.0), axis=2).reshape(-1)
    slots = pick(is_rem, slot[:, :, None]).reshape(-1)

    rows = BS // samp
    me = lax.axis_index("samp")
    dest = (me + jnp.arange(samp, dtype=jnp.int32)) % samp
    chosen = [select(stage, asked, perturb) for stage in range(STAGES)]
    got = []
    for stage in range(STAGES):
        got.append([exchanged(chosen[stage][i], q) for i, q in enumerate((0, 2, 3))])
    held, _, mates = lax.optimization_barrier((perturb, chosen[1][0], mates))
    at, kept, *own_parts = own_tiles(dest, held)
    *own_parts, below, across, above = lax.optimization_barrier((*own_parts, *got[0]))
    got = [[below, mates, across, above], [got[1][0], mates, got[1][1], got[1][2]]]
    own_parts = spread(own_parts)
    sums = []
    for stage in range(STAGES):
        parts = list(remote_tiles(stage, slots, dest, want[1], at, got[stage], samp))
        if stage == 0:
            parts, own_parts = lax.optimization_barrier((parts, own_parts))
        last = [parts[0]] + [passed_along(parts[d], "samp", d) for d in range(1, samp)]
        if stage == 0:
            dest, last[1] = lax.optimization_barrier((dest, last[1]))
        sums.append(last)

    own_sum = own_total(kept, own_parts)
    out = final(0, place, slots, dest, tapers, own_sum, sums[0], None, rows)
    out = final(1, place, slots, dest, tapers, own_sum, sums[1], out, rows)
    return out.reshape(rows, PAIR_DEV, BS)


def solution(mesh):
    return jax.shard_map(
        body,
        mesh=mesh,
        in_specs=(P("samp", "blk"), P("blk", None), P("blk", None)),
        out_specs=P("samp", "blk", None),
        check_vma=False,
    )
```

```python
import functools

import jax
import jax.numpy as jnp
from jax import lax
from jax.experimental import pallas as pl
from jax.experimental.pallas import tpu as pltpu
from jax.sharding import PartitionSpec as P

BS = 256
B_DEV = 4
K_PART = 8
REACH = 2
NBIN = 32
PAIR_DEV = 32
HALF = 128
STAGES = 2
EXTRA = 8
CODE_EXTRA = 16
TOP = 32766.0
STEPS = 256.0

EPSILON = 1e-06
MIB = 1 << 20
BIG = 58 * MIB


def passed_along(value, axis, steps):
    count = lax.axis_size(axis)
    pairs = [(source, (source + steps) % count) for source in range(count)]
    return lax.ppermute(value, axis, pairs)


def exchanged(value, kind, back=False):
    count = lax.axis_size("blk")
    source_of = (
        lambda i: i - 2,
        lambda i: i ^ 1,
        lambda i: i - 1 if i % 2 == 0 else i + 1,
        lambda i: i + 2,
    )[kind]
    pairs = [(source_of(i) % count, i) for i in range(count)]
    if back:
        pairs = [(b, a) for a, b in pairs]
    return lax.ppermute(value, "blk", sorted(pairs))


def spread(parts):
    up, first, down = parts
    down = passed_along(down, "samp", -1)
    up = passed_along(up, "samp", 1)
    first = passed_along(first, "samp", 2)
    second = passed_along(down[up.shape[0] :], "samp", -1)
    return [up, first, second, down]


def taper_table():
    scaled = 2.0 * (jnp.arange(NBIN, dtype=jnp.float32) + 0.5) / NBIN
    inner = (((-0.25 * scaled + 0.5) * scaled + 0.625) * scaled - 5.0 / 3.0) * scaled * scaled + 1.0
    outer = (
        ((((scaled / 12.0 - 0.5) * scaled + 0.625) * scaled + 5.0 / 3.0) * scaled - 5.0) * scaled
        + 4.0
        - 2.0 / (3.0 * scaled)
    )
    return jnp.where(scaled <= 1.0, inner, outer)


def scale_code(largest):
    return jnp.ceil(jnp.log2(jnp.maximum(largest, 1e-30)) * STEPS)


def encode(tile):
    code = scale_code(jnp.max(jnp.abs(tile), axis=0, keepdims=True))
    scaled = jnp.round(tile * (jnp.exp2(code * (-1.0 / STEPS)) * TOP))
    return jnp.clip(scaled, -TOP, TOP), code


def encode_norm(norm):
    code = scale_code(norm)
    scaled = norm * (jnp.exp2(code * (-1.0 / STEPS)) * TOP)
    high = jnp.round(scaled)
    return [code, high, jnp.round((scaled - high) * TOP)]


def decoded_scale(code):
    return jnp.exp2(code * (1.0 / STEPS)) * (1.0 / TOP)


def select_kernel(plan, want_ref, source_ref, *refs):
    outs, held_ref, in_sems, out_sems = refs[:-3], refs[-3], refs[-2], refs[-1]
    reads, writes = [], []
    for i, (q, side, half, out, column) in enumerate(plan):
        start = pl.multiple_of(want_ref[q * 2 + side] * BS + half * HALF, HALF)
        reads.append(pltpu.make_async_copy(source_ref.at[:, pl.ds(start, HALF)], held_ref.at[i], in_sems.at[i]))
        writes.append(
            pltpu.make_async_copy(held_ref.at[i], outs[out].at[:, pl.ds(column * HALF, HALF)], out_sems.at[i])
        )
    for read in reads:
        read.start()
    for read, write in zip(reads, writes):
        read.wait()
        write.start()
    for write in writes:
        write.wait()


def select(stage, want, perturb):
    samples = perturb.shape[0]
    widths = [2 * HALF] * 3
    plan = [(out, side, stage, out, side) for out in range(3) for side in range(2)]
    return pl.pallas_call(
        functools.partial(select_kernel, plan),
        grid_spec=pltpu.PrefetchScalarGridSpec(
            num_scalar_prefetch=1,
            grid=(),
            in_specs=[pl.BlockSpec(memory_space=pl.ANY)],
            out_specs=[pl.BlockSpec(memory_space=pltpu.HBM)] * len(widths),
            scratch_shapes=[
                pltpu.VMEM((len(plan), samples, HALF), perturb.dtype),
                pltpu.SemaphoreType.DMA((len(plan),)),
                pltpu.SemaphoreType.DMA((len(plan),)),
            ],
        ),
        out_shape=[jax.ShapeDtypeStruct((samples, width), perturb.dtype) for width in widths],
        compiler_params=pltpu.CompilerParams(vmem_limit_bytes=BIG),
        cost_estimate=pl.CostEstimate(flops=0, bytes_accessed=MIB * len(plan), transcendentals=0),
    )(want, perturb)


def with_rows(count, width, rows):
    row_id = lax.broadcasted_iota(jnp.int32, (count, width), 0)
    block = jnp.zeros((count, width), jnp.float32)
    for i, row in enumerate(rows):
        block = jnp.where(row_id == i, row, block)
    return block.astype(jnp.int32).astype(jnp.int16)


def own_kernel(dest_ref, x_ref, row_ref, at_ref, kept_ref, up_ref, first_ref, down_ref, tile_ref, norm_ref):
    rows = BS // 4
    coded = BS + CODE_EXTRA
    r = pl.program_id(0)
    half = B_DEV // 2
    at_ref[...] = jnp.transpose(row_ref[...])
    at = at_ref[...]

    def store(d, start, value):
        size = value.shape[0]
        base = pl.multiple_of(r * coded, 16) + start
        if d == 1:
            up_ref[pl.ds(base, size), :] = value
        elif d == 3:
            down_ref[pl.ds(base, size), :] = value
        else:

            @pl.when(r < half)
            def _():
                first_ref[pl.ds(base, size), :] = value

            @pl.when(r >= half)
            def _():
                down_ref[pl.ds(base + half * coded, size), :] = value

    codes = [[] for _ in range(3)]
    for c in range(B_DEV):
        tile_ref[...] = jnp.dot(at, x_ref[:, c * BS : (c + 1) * BS], preferred_element_type=jnp.float32)
        for d in range(4):
            piece = tile_ref[pl.ds(pl.multiple_of(dest_ref[d] * rows, rows), rows), :]
            if d == 0:
                kept_ref[c * rows : (c + 1) * rows, :] = piece
                continue
            piece, code = encode(piece)
            codes[d - 1].append(code)
            store(d, c * rows, piece.astype(jnp.int32).astype(jnp.int16))

        @pl.when(r == c)
        def _():
            here = lax.broadcasted_iota(jnp.int32, (BS, BS), 0) == lax.broadcasted_iota(jnp.int32, (BS, BS), 1)
            norm = jnp.sum(jnp.where(here, tile_ref[...], 0.0), axis=0, keepdims=True)
            norm_ref[...] = jnp.broadcast_to(norm, norm_ref.shape)

    kept_ref[BS : BS + EXTRA, :] = norm_ref[...]
    norm_codes = encode_norm(norm_ref[0:1, :])
    for d in range(1, 4):
        store(d, BS, with_rows(CODE_EXTRA, BS, codes[d - 1] + norm_codes))


def own_tiles(dest, perturb):
    samples, cells = perturb.shape
    coded = BS + CODE_EXTRA
    counts = [B_DEV * coded, B_DEV // 2 * coded, (B_DEV + B_DEV // 2) * coded]
    return pl.pallas_call(
        own_kernel,
        grid_spec=pltpu.PrefetchScalarGridSpec(
            num_scalar_prefetch=1,
            grid=(B_DEV,),
            in_specs=[
                pl.BlockSpec((samples, cells), lambda r, *s: (0, 0)),
                pl.BlockSpec((samples, BS), lambda r, *s: (0, r)),
            ],
            out_specs=[
                pl.BlockSpec((BS, samples), lambda r, *s: (r, 0)),
                pl.BlockSpec((BS + EXTRA, BS), lambda r, *s: (r, 0)),
            ]
            + [pl.BlockSpec((count, BS), lambda r, *s: (0, 0)) for count in counts],
            scratch_shapes=[pltpu.VMEM((BS, BS), jnp.float32), pltpu.VMEM((EXTRA, BS), jnp.float32)],
        ),
        out_shape=[
            jax.ShapeDtypeStruct((cells, samples), perturb.dtype),
            jax.ShapeDtypeStruct((B_DEV * (BS + EXTRA), BS), jnp.float32),
        ]
        + [jax.ShapeDtypeStruct((count, BS), jnp.int16) for count in counts],
        compiler_params=pltpu.CompilerParams(vmem_limit_bytes=BIG),
        cost_estimate=pl.CostEstimate(flops=2 * cells * cells * samples, bytes_accessed=12 * MIB, transcendentals=0),
    )(dest, perturb, perturb)


def total_kernel(kept_ref, up_ref, first_ref, second_ref, down_ref, out_ref):
    rows = BS // 4
    block = BS + EXTRA
    coded = BS + CODE_EXTRA
    for r in range(B_DEV):
        middle = (first_ref, r) if r < B_DEV // 2 else (second_ref, r - B_DEV // 2)
        sources = [(up_ref, r), middle, (down_ref, r)]
        extras = [
            ref[at * coded + BS : (at + 1) * coded, :].astype(jnp.int32).astype(jnp.float32) for ref, at in sources
        ]
        for j in range(4):
            here = slice(r * block + j * rows, r * block + (j + 1) * rows)
            tile = kept_ref[here, :]
            for (ref, at), extra in zip(sources, extras):
                piece = ref[at * coded + j * rows : at * coded + (j + 1) * rows, :].astype(jnp.int32)
                tile = tile + piece.astype(jnp.float32) * decoded_scale(extra[j : j + 1, :])
            out_ref[here, :] = tile
        norm = kept_ref[r * block + BS : r * block + BS + 1, :]
        for extra in extras:
            code, high, low = (extra[4 + i : 5 + i, :] for i in range(3))
            norm = norm + (high + low * (1.0 / TOP)) * decoded_scale(code)
        out_ref[r * block + BS : (r + 1) * block, :] = jnp.broadcast_to(norm, (EXTRA, BS))


def own_total(kept, coded):
    return pl.pallas_call(
        total_kernel,
        out_shape=jax.ShapeDtypeStruct(kept.shape, kept.dtype),
        compiler_params=pltpu.CompilerParams(vmem_limit_bytes=16 * MIB),
        cost_estimate=pl.CostEstimate(flops=4 * MIB, bytes_accessed=4 * MIB, transcendentals=0),
    )(kept, *coded)


def remote_kernel(stage, slot_ref, dest_ref, mate_ref, at_ref, *refs):
    blocks, parts, (cols_ref, tile_ref, norm_ref, sems) = refs[:4], refs[4:-4], refs[-4:]
    samp = len(parts)
    samples = cols_ref.shape[1]
    rows = BS // samp
    r = pl.program_id(0)

    @pl.when(r == 0)
    def _():
        copies = []
        for q in range(4):
            for side in range(2):
                start = pl.multiple_of(mate_ref[side] * BS + stage * HALF, HALF) if q == 1 else side * HALF
                copies.append(
                    pltpu.make_async_copy(
                        blocks[q].at[:, pl.ds(start, HALF)],
                        cols_ref.at[2 * q + side],
                        sems.at[2 * q + side],
                    )
                )
        for copy in copies:
            copy.start()
        step, lanes = 256, 32
        for slot, copy in enumerate(copies):
            copy.wait()

            def add(i, total):
                x = cols_ref[slot, pl.ds(pl.multiple_of(i * step, step), step), :].astype(jnp.float32)
                return total + jnp.sum(jnp.square(x).reshape(step // lanes, lanes, HALF), axis=0)

            total = lax.fori_loop(0, samples // step, add, jnp.zeros((lanes, HALF), jnp.float32))
            norm_ref[slot // 2, slot % 2 : slot % 2 + 1, :] = jnp.sum(total, axis=0, keepdims=True)

    at = at_ref[...]
    codes = [[] for _ in range(samp - 1)]
    for pair in range(2):
        u = r * 4 + 2 * pair
        cols = jnp.concatenate([cols_ref[slot_ref[u]], cols_ref[slot_ref[u + 1]]], axis=1)
        tile = jnp.dot(at, cols, preferred_element_type=jnp.float32)
        tile_ref[...] = tile
        for side in range(2):
            j = 2 * pair + side
            for d in range(samp):
                first = pl.multiple_of(dest_ref[d] * rows, rows)
                piece = tile_ref[pl.ds(first, rows), side * HALF : (side + 1) * HALF]
                if d > 0:
                    piece, code = encode(piece)
                    piece = piece.astype(jnp.int32).astype(jnp.int16)
                    codes[d - 1].append(code)
                parts[d][j * rows : (j + 1) * rows, :] = piece

    norms = norm_ref[r]
    norm_codes = []
    for side in range(2):
        norm = norms[side : side + 1, :]
        norm_codes += encode_norm(norm)
        parts[0][BS + side * 4 : BS + side * 4 + 4, :] = jnp.broadcast_to(norm, (4, HALF))
    for d in range(1, samp):
        parts[d][BS : BS + CODE_EXTRA, :] = with_rows(CODE_EXTRA, HALF, codes[d - 1] + norm_codes)


def remote_tiles(stage, slots, dest, mate_blocks, at, blocks, samp):
    cells, samples = at.shape
    blocks_out = [(BS + EXTRA, jnp.float32)] + [(BS + CODE_EXTRA, jnp.int16)] * (samp - 1)
    out_specs = [pl.BlockSpec((block, HALF), lambda r, *s: (r, 0)) for block, _ in blocks_out]
    out_shape = [jax.ShapeDtypeStruct((B_DEV * block, HALF), dtype) for block, dtype in blocks_out]
    return pl.pallas_call(
        functools.partial(remote_kernel, stage),
        grid_spec=pltpu.PrefetchScalarGridSpec(
            num_scalar_prefetch=3,
            grid=(B_DEV,),
            in_specs=[pl.BlockSpec((BS, samples), lambda r, *s: (r, 0))] + [pl.BlockSpec(memory_space=pl.ANY)] * 4,
            out_specs=out_specs,
            scratch_shapes=[
                pltpu.VMEM((8, samples, HALF), at.dtype),
                pltpu.VMEM((BS, BS), jnp.float32),
                pltpu.VMEM((B_DEV, 8, HALF), jnp.float32),
                pltpu.SemaphoreType.DMA((8,)),
            ],
        ),
        out_shape=out_shape,
        compiler_params=pltpu.CompilerParams(vmem_limit_bytes=BIG),
        cost_estimate=pl.CostEstimate(flops=2 * cells * cells * samples, bytes_accessed=10 * MIB, transcendentals=0),
    )(slots, dest, mate_blocks, at, *blocks)


def final_kernel(half, place_ref, slot_ref, dest_ref, taper_ref, own_ref, kept_ref, *refs):
    coded_refs, out_ref, norm_ref = refs[:3], refs[-2], refs[-1]
    rows = out_ref.shape[0] // PAIR_DEV
    first = dest_ref[0] * rows
    cols = slice(half * HALF, (half + 1) * HALF)
    lane = lax.broadcasted_iota(jnp.int32, (rows, BS), 1)
    row = lax.broadcasted_iota(jnp.int32, (rows, BS), 0)
    mine = lane == row + first
    block = BS + EXTRA
    coded = BS + CODE_EXTRA
    extras = []
    for r in range(B_DEV):
        extras.append(
            [ref[r * coded + BS : (r + 1) * coded, :].astype(jnp.int32).astype(jnp.float32) for ref in coded_refs]
        )
        for side in range(2):
            norm = kept_ref[r * block + BS + side * 4 : r * block + BS + side * 4 + 1, :]
            for extra in extras[r]:
                code, high, low = (extra[4 + 3 * side + i : 5 + 3 * side + i, :] for i in range(3))
                norm = norm + (high + low * (1.0 / TOP)) * decoded_scale(code)
            norm_ref[2 * r + side : 2 * r + side + 1, :] = norm
    for r in range(B_DEV):
        base = r * block
        row_norm = own_ref[base + BS : base + BS + 1, :]
        row_norm = jnp.sum(jnp.where(mine, row_norm, 0.0), axis=1, keepdims=True)
        row_scale = jnp.broadcast_to(lax.rsqrt(row_norm + EPSILON), (rows, HALF))
        for j in range(4):
            u = r * 4 + j
            norm = own_ref[j * block + BS : j * block + BS + 1, cols]
            col_scale = taper_ref[u] * lax.rsqrt(norm + EPSILON)
            tile = own_ref[base + j * rows : base + (j + 1) * rows, cols]
            out_ref[pl.ds(place_ref[u], rows, stride=PAIR_DEV), :] = tile * row_scale * col_scale
        for j in range(4):
            u = r * 4 + j
            norm = norm_ref[pl.ds(slot_ref[u], 1), :]
            col_scale = taper_ref[16 + u] * lax.rsqrt(norm + EPSILON)
            tile = kept_ref[base + j * rows : base + (j + 1) * rows, :]
            for ref, extra in zip(coded_refs, extras[r]):
                piece = ref[r * coded + j * rows : r * coded + (j + 1) * rows, :].astype(jnp.int32).astype(jnp.float32)
                tile = tile + piece * decoded_scale(extra[j : j + 1, :])
            out_ref[pl.ds(place_ref[16 + u], rows, stride=PAIR_DEV), :] = tile * row_scale * col_scale


def final(half, place, slots, dest, tapers, own, rems, out, rows):
    before = [] if out is None else [out]
    vmem = pl.BlockSpec(memory_space=pltpu.VMEM)
    whole = lambda shape: vmem if before else pl.BlockSpec(shape, lambda i, *s: (0,) * len(shape))
    return pl.pallas_call(
        functools.partial(final_kernel, half),
        grid_spec=pltpu.PrefetchScalarGridSpec(
            num_scalar_prefetch=4,
            grid=(1,),
            in_specs=[whole(own.shape)]
            + [whole(rem.shape) for rem in rems]
            + [pl.BlockSpec(memory_space=pl.ANY)] * len(before),
            out_specs=pl.BlockSpec((rows * PAIR_DEV, HALF), lambda i, *s: (0, half)),
            scratch_shapes=[pltpu.VMEM((8, HALF), jnp.float32)],
        ),
        out_shape=jax.ShapeDtypeStruct((rows * PAIR_DEV, BS), jnp.float32),
        compiler_params=pltpu.CompilerParams(vmem_limit_bytes=16 * MIB if before else BIG),
        input_output_aliases={5 + len(rems): 0} if before else {},
        cost_estimate=pl.CostEstimate(flops=MIB, bytes_accessed=4 * MIB, transcendentals=0),
    )(place, slots, dest, tapers, own, *rems, *before)


def body(perturb, partner, bins):
    blk_count = lax.axis_size("blk")
    samp = lax.axis_size("samp")
    here = lax.axis_index("blk")
    owner = partner // B_DEV
    inside = partner % B_DEV
    offset = (owner - here + blk_count + REACH) % blk_count - REACH
    mate = 1 - 2 * (here % 2)
    kind = jnp.where(offset == -2, 0, jnp.where(offset == 2, 3, jnp.where(offset == mate, 1, 2)))
    own = offset == 0
    kind = jnp.where(own, -1, kind)
    four = jnp.arange(4, dtype=jnp.int32)
    hit = (kind.reshape(1, 1, -1) == four[:, None, None]) & (inside.reshape(1, 1, -1) == four[None, :, None])
    need = jnp.any(hit, axis=2)
    low = jnp.min(jnp.where(need, four[None], B_DEV - 1), axis=1)
    high = jnp.max(jnp.where(need, four[None], 0), axis=1)
    want = jnp.stack([low, high], axis=1)
    mates = exchanged(perturb, 1)
    asked = jnp.concatenate([exchanged(want[q], q, back=True) for q in (0, 2, 3)])

    k_ids = jnp.arange(K_PART, dtype=jnp.int32)[None, :, None]
    is_high = jnp.sum(jnp.where(kind[:, :, None] == four, high[None, None], 0), axis=2) == inside
    slot = 2 * kind + is_high.astype(jnp.int32)
    remote = (~own).astype(jnp.int32)
    earlier = (jnp.arange(K_PART)[:, None] < jnp.arange(K_PART)[None, :]).astype(jnp.int32)
    rank = jnp.sum(remote[:, :, None] * earlier[None], axis=1)
    is_own = own[:, :, None] & (inside[:, :, None] == four)
    is_rem = (~own)[:, :, None] & (rank[:, :, None] == four)
    pick = lambda mask, value: jnp.sum(jnp.where(mask, value, 0), axis=1)
    bin_match = bins[:, :, None] == jnp.arange(NBIN, dtype=jnp.int32)[None, None, :]
    taper = jnp.sum(jnp.where(bin_match, taper_table()[None, None, :], 0.0), axis=2)[:, :, None]
    both = jnp.stack([is_own, is_rem])
    first_place = jnp.arange(B_DEV, dtype=jnp.int32)[None, :, None] * K_PART
    place = (jnp.sum(jnp.where(both, k_ids[None], 0), axis=2) + first_place).reshape(-1)
    tapers = jnp.sum(jnp.where(both, taper[None], 0.0), axis=2).reshape(-1)
    slots = pick(is_rem, slot[:, :, None]).reshape(-1)

    rows = BS // samp
    me = lax.axis_index("samp")
    dest = (me + jnp.arange(samp, dtype=jnp.int32)) % samp
    chosen = [select(stage, asked, perturb) for stage in range(STAGES)]
    got = []
    for stage in range(STAGES):
        got.append([exchanged(chosen[stage][i], q) for i, q in enumerate((0, 2, 3))])
    held, _, mates = lax.optimization_barrier((perturb, chosen[1][0], mates))
    at, kept, *own_parts = own_tiles(dest, held)
    *own_parts, below, across, above = lax.optimization_barrier((*own_parts, *got[0]))
    got = [[below, mates, across, above], [got[1][0], mates, got[1][1], got[1][2]]]
    own_parts = spread(own_parts)
    sums = []
    for stage in range(STAGES):
        parts = list(remote_tiles(stage, slots, dest, want[1], at, got[stage], samp))
        if stage == 0:
            parts, own_parts = lax.optimization_barrier((parts, own_parts))
        last = [parts[0]] + [passed_along(parts[d], "samp", d) for d in range(1, samp)]
        if stage == 0:
            dest, last[1] = lax.optimization_barrier((dest, last[1]))
        sums.append(last)

    own_sum = own_total(kept, own_parts)
    out = final(0, place, slots, dest, tapers, own_sum, sums[0], None, rows)
    out = final(1, place, slots, dest, tapers, own_sum, sums[1], out, rows)
    return out.reshape(rows, PAIR_DEV, BS)


def solution(mesh):
    return jax.shard_map(
        body,
        mesh=mesh,
        in_specs=(P("samp", "blk"), P("blk", None), P("blk", None)),
        out_specs=P("samp", "blk", None),
        check_vma=False,
    )
```

```python
import functools

import jax
import jax.numpy as jnp
from jax import lax
from jax.experimental import pallas as pl
from jax.experimental.pallas import tpu as pltpu
from jax.sharding import PartitionSpec as P

BS = 256
B_DEV = 4
K_PART = 8
REACH = 2
NBIN = 32
PAIR_DEV = 32
HALF = 128
STAGES = 2
EXTRA = 8
CODE_EXTRA = 16
TOP = 32766.0
PIECES = 4
STEPS = 256.0

EPSILON = 1e-06
MIB = 1 << 20
BIG = 58 * MIB


def passed_along(value, axis, steps):
    count = lax.axis_size(axis)
    pairs = [(source, (source + steps) % count) for source in range(count)]
    return lax.ppermute(value, axis, pairs)


def exchanged(value, kind, back=False):
    count = lax.axis_size("blk")
    source_of = (
        lambda i: i - 2,
        lambda i: i ^ 1,
        lambda i: i - 1 if i % 2 == 0 else i + 1,
        lambda i: i + 2,
    )[kind]
    pairs = [(source_of(i) % count, i) for i in range(count)]
    if back:
        pairs = [(b, a) for a, b in pairs]
    return lax.ppermute(value, "blk", sorted(pairs))


def spread(parts):
    up, first, down = parts
    down = passed_along(down, "samp", -1)
    up = passed_along(up, "samp", 1)
    first = passed_along(first, "samp", 2)
    second = passed_along(down[up.shape[0] :], "samp", -1)
    return [up, first, second, down]


def taper_table():
    scaled = 2.0 * (jnp.arange(NBIN, dtype=jnp.float32) + 0.5) / NBIN
    inner = (((-0.25 * scaled + 0.5) * scaled + 0.625) * scaled - 5.0 / 3.0) * scaled * scaled + 1.0
    outer = (
        ((((scaled / 12.0 - 0.5) * scaled + 0.625) * scaled + 5.0 / 3.0) * scaled - 5.0) * scaled
        + 4.0
        - 2.0 / (3.0 * scaled)
    )
    return jnp.where(scaled <= 1.0, inner, outer)


def scale_code(largest):
    return jnp.ceil(jnp.log2(jnp.maximum(largest, 1e-30)) * STEPS)


def encode(tile):
    code = scale_code(jnp.max(jnp.abs(tile), axis=0, keepdims=True))
    scaled = jnp.round(tile * (jnp.exp2(code * (-1.0 / STEPS)) * TOP))
    return jnp.clip(scaled, -TOP, TOP), code


def encode_norm(norm):
    code = scale_code(norm)
    scaled = norm * (jnp.exp2(code * (-1.0 / STEPS)) * TOP)
    high = jnp.round(scaled)
    return [code, high, jnp.round((scaled - high) * TOP)]


def decoded_scale(code):
    return jnp.exp2(code * (1.0 / STEPS)) * (1.0 / TOP)


def select_kernel(plan, want_ref, source_ref, *refs):
    outs, held_ref, in_sems, out_sems = refs[:-3], refs[-3], refs[-2], refs[-1]
    reads, writes = [], []
    samples = held_ref.shape[1]
    size = samples // PIECES
    for i, (q, side, half, out, column) in enumerate(plan):
        start = pl.multiple_of(want_ref[q * 2 + side] * BS + half * HALF, HALF)
        for piece in range(PIECES):
            at = slice(piece * size, (piece + 1) * size)
            held = held_ref.at[i, at]
            n = i * PIECES + piece
            reads.append(pltpu.make_async_copy(source_ref.at[at, pl.ds(start, HALF)], held, in_sems.at[n]))
            target = outs[out].at[at, pl.ds(column * HALF, HALF)]
            writes.append(pltpu.make_async_copy(held, target, out_sems.at[n]))
    for read in reads:
        read.start()
    for read, write in zip(reads, writes):
        read.wait()
        write.start()
    for write in writes:
        write.wait()


def select(stage, want, perturb):
    samples = perturb.shape[0]
    widths = [2 * HALF] * 3
    plan = [(out, side, stage, out, side) for out in range(3) for side in range(2)]
    return pl.pallas_call(
        functools.partial(select_kernel, plan),
        grid_spec=pltpu.PrefetchScalarGridSpec(
            num_scalar_prefetch=1,
            grid=(),
            in_specs=[pl.BlockSpec(memory_space=pl.ANY)],
            out_specs=[pl.BlockSpec(memory_space=pltpu.HBM)] * len(widths),
            scratch_shapes=[
                pltpu.VMEM((len(plan), samples, HALF), perturb.dtype),
                pltpu.SemaphoreType.DMA((len(plan) * PIECES,)),
                pltpu.SemaphoreType.DMA((len(plan) * PIECES,)),
            ],
        ),
        out_shape=[jax.ShapeDtypeStruct((samples, width), perturb.dtype) for width in widths],
        compiler_params=pltpu.CompilerParams(vmem_limit_bytes=BIG),
        cost_estimate=pl.CostEstimate(flops=0, bytes_accessed=MIB * len(plan), transcendentals=0),
    )(want, perturb)


def with_rows(count, width, rows):
    row_id = lax.broadcasted_iota(jnp.int32, (count, width), 0)
    block = jnp.zeros((count, width), jnp.float32)
    for i, row in enumerate(rows):
        block = jnp.where(row_id == i, row, block)
    return block.astype(jnp.int32).astype(jnp.int16)


def own_kernel(dest_ref, x_ref, row_ref, at_ref, kept_ref, up_ref, first_ref, down_ref, tile_ref, norm_ref):
    rows = BS // 4
    coded = BS + CODE_EXTRA
    r = pl.program_id(0)
    half = B_DEV // 2
    at_ref[...] = jnp.transpose(row_ref[...])
    at = at_ref[...]

    def store(d, start, value):
        size = value.shape[0]
        base = pl.multiple_of(r * coded, 16) + start
        if d == 1:
            up_ref[pl.ds(base, size), :] = value
        elif d == 3:
            down_ref[pl.ds(base, size), :] = value
        else:

            @pl.when(r < half)
            def _():
                first_ref[pl.ds(base, size), :] = value

            @pl.when(r >= half)
            def _():
                down_ref[pl.ds(base + half * coded, size), :] = value

    codes = [[] for _ in range(3)]
    for c in range(B_DEV):
        tile_ref[...] = jnp.dot(at, x_ref[:, c * BS : (c + 1) * BS], preferred_element_type=jnp.float32)
        for d in range(4):
            piece = tile_ref[pl.ds(pl.multiple_of(dest_ref[d] * rows, rows), rows), :]
            if d == 0:
                kept_ref[c * rows : (c + 1) * rows, :] = piece
                continue
            piece, code = encode(piece)
            codes[d - 1].append(code)
            store(d, c * rows, piece.astype(jnp.int32).astype(jnp.int16))

        @pl.when(r == c)
        def _():
            here = lax.broadcasted_iota(jnp.int32, (BS, BS), 0) == lax.broadcasted_iota(jnp.int32, (BS, BS), 1)
            norm = jnp.sum(jnp.where(here, tile_ref[...], 0.0), axis=0, keepdims=True)
            norm_ref[...] = jnp.broadcast_to(norm, norm_ref.shape)

    kept_ref[BS : BS + EXTRA, :] = norm_ref[...]
    norm_codes = encode_norm(norm_ref[0:1, :])
    for d in range(1, 4):
        store(d, BS, with_rows(CODE_EXTRA, BS, codes[d - 1] + norm_codes))


def own_tiles(dest, perturb):
    samples, cells = perturb.shape
    coded = BS + CODE_EXTRA
    counts = [B_DEV * coded, B_DEV // 2 * coded, (B_DEV + B_DEV // 2) * coded]
    return pl.pallas_call(
        own_kernel,
        grid_spec=pltpu.PrefetchScalarGridSpec(
            num_scalar_prefetch=1,
            grid=(B_DEV,),
            in_specs=[
                pl.BlockSpec((samples, cells), lambda r, *s: (0, 0)),
                pl.BlockSpec((samples, BS), lambda r, *s: (0, r)),
            ],
            out_specs=[
                pl.BlockSpec((BS, samples), lambda r, *s: (r, 0)),
                pl.BlockSpec((BS + EXTRA, BS), lambda r, *s: (r, 0)),
            ]
            + [pl.BlockSpec((count, BS), lambda r, *s: (0, 0)) for count in counts],
            scratch_shapes=[pltpu.VMEM((BS, BS), jnp.float32), pltpu.VMEM((EXTRA, BS), jnp.float32)],
        ),
        out_shape=[
            jax.ShapeDtypeStruct((cells, samples), perturb.dtype),
            jax.ShapeDtypeStruct((B_DEV * (BS + EXTRA), BS), jnp.float32),
        ]
        + [jax.ShapeDtypeStruct((count, BS), jnp.int16) for count in counts],
        compiler_params=pltpu.CompilerParams(vmem_limit_bytes=BIG),
        cost_estimate=pl.CostEstimate(flops=2 * cells * cells * samples, bytes_accessed=12 * MIB, transcendentals=0),
    )(dest, perturb, perturb)


def total_kernel(kept_ref, up_ref, first_ref, second_ref, down_ref, out_ref):
    rows = BS // 4
    block = BS + EXTRA
    coded = BS + CODE_EXTRA
    for r in range(B_DEV):
        middle = (first_ref, r) if r < B_DEV // 2 else (second_ref, r - B_DEV // 2)
        sources = [(up_ref, r), middle, (down_ref, r)]
        extras = [
            ref[at * coded + BS : (at + 1) * coded, :].astype(jnp.int32).astype(jnp.float32) for ref, at in sources
        ]
        for j in range(4):
            here = slice(r * block + j * rows, r * block + (j + 1) * rows)
            tile = kept_ref[here, :]
            for (ref, at), extra in zip(sources, extras):
                piece = ref[at * coded + j * rows : at * coded + (j + 1) * rows, :].astype(jnp.int32)
                tile = tile + piece.astype(jnp.float32) * decoded_scale(extra[j : j + 1, :])
            out_ref[here, :] = tile
        norm = kept_ref[r * block + BS : r * block + BS + 1, :]
        for extra in extras:
            code, high, low = (extra[4 + i : 5 + i, :] for i in range(3))
            norm = norm + (high + low * (1.0 / TOP)) * decoded_scale(code)
        out_ref[r * block + BS : (r + 1) * block, :] = jnp.broadcast_to(norm, (EXTRA, BS))


def own_total(kept, coded):
    return pl.pallas_call(
        total_kernel,
        out_shape=jax.ShapeDtypeStruct(kept.shape, kept.dtype),
        compiler_params=pltpu.CompilerParams(vmem_limit_bytes=16 * MIB),
        cost_estimate=pl.CostEstimate(flops=4 * MIB, bytes_accessed=4 * MIB, transcendentals=0),
    )(kept, *coded)


def remote_kernel(stage, slot_ref, dest_ref, mate_ref, at_ref, *refs):
    blocks, parts, (cols_ref, tile_ref, norm_ref, sems) = refs[:4], refs[4:-4], refs[-4:]
    samp = len(parts)
    samples = cols_ref.shape[1]
    rows = BS // samp
    r = pl.program_id(0)

    @pl.when(r == 0)
    def _():
        copies = []
        for q in range(4):
            for side in range(2):
                start = pl.multiple_of(mate_ref[side] * BS + stage * HALF, HALF) if q == 1 else side * HALF
                copies.append(
                    pltpu.make_async_copy(
                        blocks[q].at[:, pl.ds(start, HALF)],
                        cols_ref.at[2 * q + side],
                        sems.at[2 * q + side],
                    )
                )
        for copy in copies:
            copy.start()
        step, lanes = 256, 32
        for slot, copy in enumerate(copies):
            copy.wait()

            def add(i, total):
                x = cols_ref[slot, pl.ds(pl.multiple_of(i * step, step), step), :].astype(jnp.float32)
                return total + jnp.sum(jnp.square(x).reshape(step // lanes, lanes, HALF), axis=0)

            total = lax.fori_loop(0, samples // step, add, jnp.zeros((lanes, HALF), jnp.float32))
            norm_ref[slot // 2, slot % 2 : slot % 2 + 1, :] = jnp.sum(total, axis=0, keepdims=True)

    at = at_ref[...]
    codes = [[] for _ in range(samp - 1)]
    for pair in range(2):
        u = r * 4 + 2 * pair
        cols = jnp.concatenate([cols_ref[slot_ref[u]], cols_ref[slot_ref[u + 1]]], axis=1)
        tile = jnp.dot(at, cols, preferred_element_type=jnp.float32)
        tile_ref[...] = tile
        for side in range(2):
            j = 2 * pair + side
            for d in range(samp):
                first = pl.multiple_of(dest_ref[d] * rows, rows)
                piece = tile_ref[pl.ds(first, rows), side * HALF : (side + 1) * HALF]
                if d > 0:
                    piece, code = encode(piece)
                    piece = piece.astype(jnp.int32).astype(jnp.int16)
                    codes[d - 1].append(code)
                parts[d][j * rows : (j + 1) * rows, :] = piece

    norms = norm_ref[r]
    norm_codes = []
    for side in range(2):
        norm = norms[side : side + 1, :]
        norm_codes += encode_norm(norm)
        parts[0][BS + side * 4 : BS + side * 4 + 4, :] = jnp.broadcast_to(norm, (4, HALF))
    for d in range(1, samp):
        parts[d][BS : BS + CODE_EXTRA, :] = with_rows(CODE_EXTRA, HALF, codes[d - 1] + norm_codes)


def remote_tiles(stage, slots, dest, mate_blocks, at, blocks, samp):
    cells, samples = at.shape
    blocks_out = [(BS + EXTRA, jnp.float32)] + [(BS + CODE_EXTRA, jnp.int16)] * (samp - 1)
    out_specs = [pl.BlockSpec((block, HALF), lambda r, *s: (r, 0)) for block, _ in blocks_out]
    out_shape = [jax.ShapeDtypeStruct((B_DEV * block, HALF), dtype) for block, dtype in blocks_out]
    return pl.pallas_call(
        functools.partial(remote_kernel, stage),
        grid_spec=pltpu.PrefetchScalarGridSpec(
            num_scalar_prefetch=3,
            grid=(B_DEV,),
            in_specs=[pl.BlockSpec((BS, samples), lambda r, *s: (r, 0))] + [pl.BlockSpec(memory_space=pl.ANY)] * 4,
            out_specs=out_specs,
            scratch_shapes=[
                pltpu.VMEM((8, samples, HALF), at.dtype),
                pltpu.VMEM((BS, BS), jnp.float32),
                pltpu.VMEM((B_DEV, 8, HALF), jnp.float32),
                pltpu.SemaphoreType.DMA((8,)),
            ],
        ),
        out_shape=out_shape,
        compiler_params=pltpu.CompilerParams(vmem_limit_bytes=BIG),
        cost_estimate=pl.CostEstimate(flops=2 * cells * cells * samples, bytes_accessed=10 * MIB, transcendentals=0),
    )(slots, dest, mate_blocks, at, *blocks)


def final_kernel(half, place_ref, slot_ref, dest_ref, taper_ref, own_ref, kept_ref, *refs):
    coded_refs, out_ref, norm_ref = refs[:3], refs[-2], refs[-1]
    rows = out_ref.shape[0] // PAIR_DEV
    first = dest_ref[0] * rows
    cols = slice(half * HALF, (half + 1) * HALF)
    lane = lax.broadcasted_iota(jnp.int32, (rows, BS), 1)
    row = lax.broadcasted_iota(jnp.int32, (rows, BS), 0)
    mine = lane == row + first
    block = BS + EXTRA
    coded = BS + CODE_EXTRA
    extras = []
    for r in range(B_DEV):
        extras.append(
            [ref[r * coded + BS : (r + 1) * coded, :].astype(jnp.int32).astype(jnp.float32) for ref in coded_refs]
        )
        for side in range(2):
            norm = kept_ref[r * block + BS + side * 4 : r * block + BS + side * 4 + 1, :]
            for extra in extras[r]:
                code, high, low = (extra[4 + 3 * side + i : 5 + 3 * side + i, :] for i in range(3))
                norm = norm + (high + low * (1.0 / TOP)) * decoded_scale(code)
            norm_ref[2 * r + side : 2 * r + side + 1, :] = norm
    for r in range(B_DEV):
        base = r * block
        row_norm = own_ref[base + BS : base + BS + 1, :]
        row_norm = jnp.sum(jnp.where(mine, row_norm, 0.0), axis=1, keepdims=True)
        row_scale = jnp.broadcast_to(lax.rsqrt(row_norm + EPSILON), (rows, HALF))
        for j in range(4):
            u = r * 4 + j
            norm = own_ref[j * block + BS : j * block + BS + 1, cols]
            col_scale = taper_ref[u] * lax.rsqrt(norm + EPSILON)
            tile = own_ref[base + j * rows : base + (j + 1) * rows, cols]
            out_ref[pl.ds(place_ref[u], rows, stride=PAIR_DEV), :] = tile * row_scale * col_scale
        for j in range(4):
            u = r * 4 + j
            norm = norm_ref[pl.ds(slot_ref[u], 1), :]
            col_scale = taper_ref[16 + u] * lax.rsqrt(norm + EPSILON)
            tile = kept_ref[base + j * rows : base + (j + 1) * rows, :]
            for ref, extra in zip(coded_refs, extras[r]):
                piece = ref[r * coded + j * rows : r * coded + (j + 1) * rows, :].astype(jnp.int32).astype(jnp.float32)
                tile = tile + piece * decoded_scale(extra[j : j + 1, :])
            out_ref[pl.ds(place_ref[16 + u], rows, stride=PAIR_DEV), :] = tile * row_scale * col_scale


def final(half, place, slots, dest, tapers, own, rems, out, rows):
    before = [] if out is None else [out]
    vmem = pl.BlockSpec(memory_space=pltpu.VMEM)
    whole = lambda shape: vmem if before else pl.BlockSpec(shape, lambda i, *s: (0,) * len(shape))
    return pl.pallas_call(
        functools.partial(final_kernel, half),
        grid_spec=pltpu.PrefetchScalarGridSpec(
            num_scalar_prefetch=4,
            grid=(1,),
            in_specs=[whole(own.shape)]
            + [whole(rem.shape) for rem in rems]
            + [pl.BlockSpec(memory_space=pl.ANY)] * len(before),
            out_specs=pl.BlockSpec((rows * PAIR_DEV, HALF), lambda i, *s: (0, half)),
            scratch_shapes=[pltpu.VMEM((8, HALF), jnp.float32)],
        ),
        out_shape=jax.ShapeDtypeStruct((rows * PAIR_DEV, BS), jnp.float32),
        compiler_params=pltpu.CompilerParams(vmem_limit_bytes=16 * MIB if before else BIG),
        input_output_aliases={5 + len(rems): 0} if before else {},
        cost_estimate=pl.CostEstimate(flops=MIB, bytes_accessed=4 * MIB, transcendentals=0),
    )(place, slots, dest, tapers, own, *rems, *before)


def body(perturb, partner, bins):
    blk_count = lax.axis_size("blk")
    samp = lax.axis_size("samp")
    here = lax.axis_index("blk")
    owner = partner // B_DEV
    inside = partner % B_DEV
    offset = (owner - here + blk_count + REACH) % blk_count - REACH
    mate = 1 - 2 * (here % 2)
    kind = jnp.where(offset == -2, 0, jnp.where(offset == 2, 3, jnp.where(offset == mate, 1, 2)))
    own = offset == 0
    kind = jnp.where(own, -1, kind)
    four = jnp.arange(4, dtype=jnp.int32)
    hit = (kind.reshape(1, 1, -1) == four[:, None, None]) & (inside.reshape(1, 1, -1) == four[None, :, None])
    need = jnp.any(hit, axis=2)
    low = jnp.min(jnp.where(need, four[None], B_DEV - 1), axis=1)
    high = jnp.max(jnp.where(need, four[None], 0), axis=1)
    want = jnp.stack([low, high], axis=1)
    mates = exchanged(perturb, 1)
    asked = jnp.concatenate([exchanged(want[q], q, back=True) for q in (0, 2, 3)])

    k_ids = jnp.arange(K_PART, dtype=jnp.int32)[None, :, None]
    is_high = jnp.sum(jnp.where(kind[:, :, None] == four, high[None, None], 0), axis=2) == inside
    slot = 2 * kind + is_high.astype(jnp.int32)
    remote = (~own).astype(jnp.int32)
    earlier = (jnp.arange(K_PART)[:, None] < jnp.arange(K_PART)[None, :]).astype(jnp.int32)
    rank = jnp.sum(remote[:, :, None] * earlier[None], axis=1)
    is_own = own[:, :, None] & (inside[:, :, None] == four)
    is_rem = (~own)[:, :, None] & (rank[:, :, None] == four)
    pick = lambda mask, value: jnp.sum(jnp.where(mask, value, 0), axis=1)
    bin_match = bins[:, :, None] == jnp.arange(NBIN, dtype=jnp.int32)[None, None, :]
    taper = jnp.sum(jnp.where(bin_match, taper_table()[None, None, :], 0.0), axis=2)[:, :, None]
    both = jnp.stack([is_own, is_rem])
    first_place = jnp.arange(B_DEV, dtype=jnp.int32)[None, :, None] * K_PART
    place = (jnp.sum(jnp.where(both, k_ids[None], 0), axis=2) + first_place).reshape(-1)
    tapers = jnp.sum(jnp.where(both, taper[None], 0.0), axis=2).reshape(-1)
    slots = pick(is_rem, slot[:, :, None]).reshape(-1)

    rows = BS // samp
    me = lax.axis_index("samp")
    dest = (me + jnp.arange(samp, dtype=jnp.int32)) % samp
    chosen = [select(stage, asked, perturb) for stage in range(STAGES)]
    got = []
    for stage in range(STAGES):
        got.append([exchanged(chosen[stage][i], q) for i, q in enumerate((0, 2, 3))])
    held, _, mates = lax.optimization_barrier((perturb, chosen[1][0], mates))
    at, kept, *own_parts = own_tiles(dest, held)
    *own_parts, below, across, above = lax.optimization_barrier((*own_parts, *got[0]))
    got = [[below, mates, across, above], [got[1][0], mates, got[1][1], got[1][2]]]
    own_parts = spread(own_parts)
    sums = []
    for stage in range(STAGES):
        parts = list(remote_tiles(stage, slots, dest, want[1], at, got[stage], samp))
        if stage == 0:
            parts, own_parts = lax.optimization_barrier((parts, own_parts))
        last = [parts[0]] + [passed_along(parts[d], "samp", d) for d in range(1, samp)]
        if stage == 0:
            dest, last[1] = lax.optimization_barrier((dest, last[1]))
        sums.append(last)

    own_sum = own_total(kept, own_parts)
    out = final(0, place, slots, dest, tapers, own_sum, sums[0], None, rows)
    out = final(1, place, slots, dest, tapers, own_sum, sums[1], out, rows)
    return out.reshape(rows, PAIR_DEV, BS)


def solution(mesh):
    return jax.shard_map(
        body,
        mesh=mesh,
        in_specs=(P("samp", "blk"), P("blk", None), P("blk", None)),
        out_specs=P("samp", "blk", None),
        check_vma=False,
    )
```
